32 devices in a mesh: gx: 8 (over z, y), gy: 4 (over x, core).
Axes of the slice: x: 2, y: 2, z: 4, core: 2. Of those that a mesh axis runs over, the one named last changes fastest.
Arguments:
- populations: float32 [19, 16, 32, 1024], P(None, None, 'gx', 'gy'), may hold values from -6 to 6
- fraction: float32 [16, 3, 4096], P('gx', None, 'gy'), may hold values from 0 to 1
- spans: int32 [16, 32, 1], P('gx'), may hold values from 0 to 3; in each aligned block of 64 rows (0 to 63, 64 to 127, ..., all dimensions but the last counted through in order) at most 32 rows name the same one
- stiffness: int32 [16], P('gx'), may hold values from 1 to 8
Outputs:
- populations_out: float32 [19, 16, 32, 1024], P(None, None, 'gx', 'gy')
- marker_vel: float32 [16, 3, 4096], P('gx', None, 'gy')
The draws below stay inside these ranges and needn't reach their ends.
Inputs may be any that keep to these rules, and one draw needn't show every extreme that they name: `spans`: among the 64 blocks of the filaments of one gx index, no tile is named by more than 32 blocks, and one is named by exactly 32.
All inputs are finite; a program needn't handle non-finite values.
Results may differ from the reference program's by a relative error of at most 0.0003.
Values sent between devices are 32-bit elements; how exact they have to be, the bound alone decides.
No kernel may reach another device: no remote copies, remote signals or barrier semaphores. Data moves between devices by JAX's collectives and lax.ppermute only.
A program may use at most 64 MiB of HBM per device.

```python
import math
import jax
import jax.numpy as jnp
import numpy as np

CX = 4
CY = 256
NZ = 16
STEPS = 2
FIL_ROW = 2
M = 4096
FIL = 16
NB = 32
BMAX = 32
NX = 32
NY = 1024
N_GY = 4


def plant(values, stream_key, low, high):
    spot = [jax.random.randint(jax.random.fold_in(stream_key, axis), (), 0, length) for axis, length in enumerate(values.shape)]
    widest = values.shape.index(max(values.shape))
    beside = spot[:widest] + [(spot[widest] + 1) % values.shape[widest]] + spot[widest + 1:]
    return values.at[tuple(spot)].set(low).at[tuple(beside)].set(high)


def levels(own_key, dims, pieces, least, top_value):
    factor_of = 1.0
    for axis_at, shards_of in pieces:
        draws = jax.random.uniform(jax.random.fold_in(jax.random.fold_in(own_key, 6), axis_at), (shards_of,), jnp.float32, least / len(pieces), top_value / len(pieces))
        factor_of = factor_of * jnp.repeat(jnp.exp(draws), dims[axis_at] // shards_of).reshape((-1,) + (1,) * (len(dims) - 1 - axis_at))
    return factor_of


def deal_out(key, own, number, rows, number_of, top, limit, slope):
    order = jax.random.permutation(key, number_of)
    heavy_load, usual = portions_of(number_of, rows * top, limit, slope, True), portions_of(number_of, rows * top, limit, slope, False)
    places = jnp.arange(number_of)

    def named(lengths, rotation):
        used = int((lengths > 0).sum())
        fixed = max(1, used // 4)
        shifted = fixed + (places - fixed + rotation * (used - fixed)) % max(1, number_of - fixed)
        return jnp.zeros((number_of,), jnp.int32).at[order[jnp.where(places < fixed, places, shifted)]].set(jnp.asarray(lengths, jnp.int32))

    lengths = jnp.where(number % 4 == 0, named(heavy_load, number // 4), named(usual, number - number // 4 - 1))
    mixed = jax.random.permutation(jax.random.fold_in(own, 3), number_of)
    source_of, receiver = mixed[0:number_of // 2 * 2:2], mixed[1:number_of // 2 * 2:2]
    slack = jnp.minimum(lengths[source_of] - 1, limit - lengths[receiver]) // 2
    slack = jnp.where((source_of == order[0]) | (receiver == order[0]) | (lengths[receiver] == 0), 0, jnp.maximum(slack, 0))
    shifted = jax.random.randint(jax.random.fold_in(own, 4), (number_of // 2,), 0, 1 << 20) % (slack + 1)
    lengths = lengths.at[source_of].add(-shifted).at[receiver].add(shifted)
    labels = jnp.searchsorted(jnp.cumsum(lengths), jnp.arange(rows * top), side="right").astype(jnp.int32)
    table = labels.reshape(top, rows).T
    table = table[jax.random.permutation(jax.random.fold_in(own, 1), rows)]
    rotation = jax.random.randint(jax.random.fold_in(own, 2), (rows, 1), 0, top)
    return jnp.take_along_axis(table, (jnp.arange(top)[None, :] + rotation) % top, axis=1)


def portions_of(amount, total, most, skew, full):
    weights = [(1 << 20) // math.isqrt(standing ** skew) + 1 for standing in range(1, amount + 1)]
    largest = most if full else min(most, max(-(-total // amount), total * weights[0] // sum(weights)))
    least = 1 if total - largest >= amount - 1 else 0
    holding, surplus = [largest] + [least] * (amount - 1), total - largest - least * (amount - 1)
    while surplus > 0:
        free = [i for i in range(1, amount) if holding[i] < largest] or [i for i in range(1, amount) if holding[i] < most]
        whole, remaining = sum([weights[i] for i in free]), surplus
        for i in free:
            extra = min(most - holding[i], max(1, remaining * weights[i] // whole), surplus)
            holding[i] = holding[i] + extra
            surplus = surplus - extra
    return np.array(holding)


def gaussian(own_key, extent, width, reach, split=(), kind=jnp.bfloat16):
    entries = width * jax.random.normal(own_key, extent, jnp.float32)
    if split:
        entries = entries * levels(own_key, extent, split, -0.22, 0.18)
    return jnp.clip(entries, -reach, reach).astype(kind)


def setup_inputs(seed: int = 0) -> dict:
    keys = jax.random.split(jax.random.key(seed), 5)
    populations = gaussian(keys[0], (19, NZ, NX, NY), 1.0, 6.0, ((2, 8), (3, 4)), jnp.float32)
    fraction = jnp.clip(1.0 * jax.random.uniform(keys[1], (FIL, 3, M), jnp.float32) ** levels(keys[1], (FIL, 3, M), ((0, 8), (2, 4)), -0.2, 0.2), 0.0, 1.0)
    spans_keys = jax.random.split(jax.random.fold_in(keys[2], 1), FIL * NB // (FIL_ROW * NB))
    spans_turns = jax.random.permutation(jax.random.fold_in(keys[2], 3), FIL * NB // (FIL_ROW * NB))
    spans = jax.vmap(lambda own, number: deal_out(jax.random.fold_in(keys[2], 2), own, number, FIL_ROW * NB, N_GY, 1, BMAX, 2))(spans_keys, spans_turns).reshape((FIL, NB, 1))
    stiffness = plant(jax.random.randint(keys[3], (FIL,), 1, 9), jax.random.fold_in(keys[3], 1), 1, 8).astype(jnp.int32)
    return dict(populations=populations, fraction=fraction, spans=spans, stiffness=stiffness)


velocity_set = ((0, 0, 0), (1, 0, 0), (-1, 0, 0), (0, 1, 0), (0, -1, 0), (0, 0, 1), (0, 0, -1),
                (1, 1, 0), (-1, -1, 0), (1, -1, 0), (-1, 1, 0), (1, 0, 1), (-1, 0, -1),
                (1, 0, -1), (-1, 0, 1), (0, 1, 1), (0, -1, -1), (0, 1, -1), (0, -1, 1))
lattice_weight = (1.0 / 3.0,) + (1.0 / 18.0,) * 6 + (1.0 / 36.0,) * 12
relax_time = 0.8
deviation_unit = 0.002
feedback_gain = 2.0
stiff_unit = 0.002


def opposite(entry):
    return entry + 1 if entry % 2 == 1 else entry - 1


def kernel_weight(distance):
    return jnp.where(jnp.abs(distance) < 2.0, 0.25 * (1.0 + jnp.cos((0.5 * math.pi) * distance)), 0.0)


def periodic_gap(gap, period):
    half = 0.5 * period
    return jnp.where(gap > half, gap - period, jnp.where(gap < -half, gap + period, gap))


def marker_places(fraction, spans, row_anchor, tile_x, tile_y, depth):
    block_size = fraction.shape[2] // spans.shape[1]
    span_cells = jnp.repeat(spans[:, :, 0] * tile_y, block_size, axis=1).astype(jnp.float32)
    xpos = row_anchor[:, None] + 1.0 + fraction[:, 0] * (tile_x - 3.01)
    ypos = span_cells + fraction[:, 1] * tile_y
    zpos = 1.0 + fraction[:, 2] * (depth - 3.01)
    return jnp.stack([xpos, ypos, zpos], axis=1)


def elastic(places, period):
    ahead = places[:, :, 1:] - places[:, :, :-1]
    ahead = jnp.stack([ahead[:, 0], periodic_gap(ahead[:, 1], period), ahead[:, 2]], axis=1)
    edge = jnp.zeros(ahead.shape[:2] + (1,), jnp.float32)
    return jnp.concatenate([ahead, edge], 2) - jnp.concatenate([edge, ahead], 2)


def project(vector, parts, like):
    total = jnp.zeros_like(like)
    for axis_dim in range(3):
        if vector[axis_dim] != 0:
            total = total + float(vector[axis_dim]) * parts[axis_dim]
    return total


def moments(deviation):
    fpop = [lattice_weight[entry] + deviation_unit * deviation[entry] for entry in range(19)]
    dens = fpop[0]
    for entry in range(1, 19):
        dens = dens + fpop[entry]
    momentum = []
    for axis_dim in range(3):
        total = jnp.zeros_like(dens)
        for entry in range(19):
            if velocity_set[entry][axis_dim] != 0:
                total = total + float(velocity_set[entry][axis_dim]) * fpop[entry]
        momentum.append(total)
    return fpop, dens, momentum


def relax(fpop, dens, momentum, force):
    velocity = [(momentum[axis_dim] + 0.5 * force[axis_dim]) / dens for axis_dim in range(3)]
    speed_sq = velocity[0] * velocity[0] + velocity[1] * velocity[1] + velocity[2] * velocity[2]
    factor = 1.0 - 0.5 / relax_time
    drift_base = -(velocity[0] * force[0] + velocity[1] * force[1] + velocity[2] * force[2])
    post = []
    for entry in range(19):
        vector = velocity_set[entry]
        along = project(vector, velocity, dens)
        push = project(vector, force, dens)
        drift = push + drift_base
        equil = lattice_weight[entry] * dens * (1.0 + 3.0 * along + 4.5 * along * along - 1.5 * speed_sq)
        source = factor * lattice_weight[entry] * (3.0 * drift + 9.0 * along * push)
        post.append(fpop[entry] - (fpop[entry] - equil) / relax_time + source)
    return post


def bounce(moved, post):
    result = []
    for entry in range(19):
        lift = velocity_set[entry][2]
        plane = moved[entry]
        if lift == 1:
            plane = jnp.concatenate([post[opposite(entry)][:1], plane[:-1]], 0)
        elif lift == -1:
            plane = jnp.concatenate([plane[1:], post[opposite(entry)][-1:]], 0)
        result.append((plane - lattice_weight[entry]) / deviation_unit)
    return jnp.stack(result)


def stencil_parts(places):
    base = jnp.floor(places).astype(jnp.int32)
    cells = base[..., None] + jnp.arange(-1, 3, dtype=jnp.int32)
    weights = kernel_weight(places[..., None] - cells.astype(jnp.float32))
    zcell = cells[:, 2][:, :, :, None, None]
    xcell = cells[:, 0][:, :, None, :, None]
    ycell = jnp.mod(cells[:, 1], NY)[:, :, None, None, :]
    joint = weights[:, 2][:, :, :, None, None] * weights[:, 0][:, :, None, :, None]
    joint = joint * weights[:, 1][:, :, None, None, :]
    shape = joint.shape
    return (jnp.broadcast_to(zcell, shape), jnp.broadcast_to(xcell, shape), jnp.broadcast_to(ycell, shape), joint)


def interpolate(flow, parts):
    zcell, xcell, ycell, joint = parts
    values = [jnp.sum(flow[axis_dim][zcell, xcell, ycell] * joint, axis=(2, 3, 4)) for axis_dim in range(3)]
    return jnp.stack(values, axis=1)


def spread(force, parts):
    zcell, xcell, ycell, joint = parts
    fields = []
    for axis_dim in range(3):
        grid = jnp.zeros((NZ, NX, NY), jnp.float32)
        fields.append(grid.at[zcell, xcell, ycell].add(force[:, axis_dim][:, :, None, None, None] * joint))
    return fields


def reference(populations, fraction, spans, stiffness):
    row_anchor = ((jnp.arange(FIL, dtype=jnp.int32) // FIL_ROW) * CX).astype(jnp.float32)
    places = marker_places(fraction, spans, row_anchor, CX, CY, NZ)
    parts = stencil_parts(places)
    bend = elastic(places, NY) * (stiffness.astype(jnp.float32) * (stiff_unit / CY))[:, None, None]
    deviation = populations
    marker_speed = jnp.zeros((FIL, 3, M), jnp.float32)
    for step in range(STEPS):
        fpop, dens, momentum = moments(deviation)
        flow = jnp.stack([part / dens for part in momentum])
        marker_speed = interpolate(flow, parts)
        force = bend - feedback_gain * marker_speed
        field_force = spread(force, parts)
        post = relax(fpop, dens, momentum, field_force)
        moved = []
        for entry in range(19):
            shift_x, shift_y = velocity_set[entry][0], velocity_set[entry][1]
            moved.append(jnp.roll(post[entry], (shift_x, shift_y), axis=(1, 2)))
        deviation = bounce(moved, post)
    return deviation, marker_speed / deviation_unit
```

```python
import functools
import math

import jax
import jax.numpy as jnp
from jax import lax
from jax.experimental import pallas as pl
from jax.experimental.pallas import tpu as pltpu
from jax.sharding import PartitionSpec as P

STEPS = 2

velocity_set = (
    (0, 0, 0),
    (1, 0, 0),
    (-1, 0, 0),
    (0, 1, 0),
    (0, -1, 0),
    (0, 0, 1),
    (0, 0, -1),
    (1, 1, 0),
    (-1, -1, 0),
    (1, -1, 0),
    (-1, 1, 0),
    (1, 0, 1),
    (-1, 0, -1),
    (1, 0, -1),
    (-1, 0, 1),
    (0, 1, 1),
    (0, -1, -1),
    (0, 1, -1),
    (0, -1, 1),
)
lattice_weight = (1.0 / 3.0,) + (1.0 / 18.0,) * 6 + (1.0 / 36.0,) * 12
unit = 0.002
feedback_gain = 2.0
EAST = tuple(i for i in range(19) if velocity_set[i][0] == 1)
WEST = tuple(i for i in range(19) if velocity_set[i][0] == -1)

DEPTH = 16
ROWS = DEPTH * 8
BLOCK = 128
GROUP = 4
FIELDS = 9
VMEM_LIMIT = 40 * 1024 * 1024


def opposite(entry):
    return entry + 1 if entry % 2 == 1 else entry - 1


def iotas(shape=(8, 128)):
    return lax.broadcasted_iota(jnp.int32, shape, 0), lax.broadcasted_iota(jnp.int32, shape, 1)


def turn(value, shift, axis):
    shift = shift % value.shape[axis]
    return pltpu.roll(value, shift, axis) if shift else value


def pack_edges(slices):
    _, lane = iotas()
    total = jnp.zeros((8, 128), jnp.float32)
    for z in range(DEPTH):
        total = jnp.where((lane >= 5 * z) & (lane < 5 * z + 5), turn(slices(z), 5 * z + 2, 1), total)
    return total


def signed_sum(terms):
    total = None
    for sign, value in terms:
        if total is None:
            total = value if sign > 0 else -value
        else:
            total = total + value if sign > 0 else total - value
    return total


def dot_c(vector, parts):
    return signed_sum([(vector[a], parts[a]) for a in range(3) if vector[a] != 0])


def moments(dev):
    total = dev[0]
    for entry in range(1, 19):
        total = total + dev[entry]
    momentum = [
        signed_sum([(velocity_set[e][a], dev[e]) for e in range(19) if velocity_set[e][a] != 0]) for a in range(3)
    ]
    return total, momentum, 1.0 + unit * total


def collide(dev, force):
    total, momentum, dens = moments(dev)
    inverse = 1.0 / dens
    vel = [(momentum[a] + 0.5 * force[a]) * inverse for a in range(3)]
    odd_base = [3.75 * momentum[a] + 3.0 * force[a] for a in range(3)]
    even_base = [5.625 * momentum[a] + 6.1875 * force[a] for a in range(3)]
    along = vel[0] * even_base[0] + vel[1] * even_base[1] + vel[2] * even_base[2]
    base = 1.25 * total - (unit / 3.0) * along
    post = [lattice_weight[0] * base - 0.25 * dev[0]]
    scaled = [unit * vel[a] for a in range(3)]
    for entry in range(1, 19, 2):
        vector, weight = velocity_set[entry], lattice_weight[entry]
        odd = weight * dot_c(vector, odd_base)
        even = weight * (base + dot_c(vector, scaled) * dot_c(vector, even_base))
        post.append((even + odd) - 0.25 * dev[entry])
        post.append((even - odd) - 0.25 * dev[entry + 1])
    return post


def edge_kernel(pop_ref, edge_ref):
    for entry in range(19):
        edge_ref[entry] = pack_edges(lambda z: pop_ref[entry, 8 * z : 8 * z + 8, :])


def shifted(tiles, shift):
    lane = lax.broadcasted_iota(jnp.int32, tiles[0].shape, 1)
    if shift == 0:
        return tiles[1:-1]
    rolled = [turn(tile, -shift, 1) for tile in tiles]
    if shift > 0:
        return [jnp.where(lane >= 128 - shift, rolled[i + 1], rolled[i]) for i in range(1, len(tiles) - 1)]
    return [jnp.where(lane < -shift, rolled[i - 1], rolled[i]) for i in range(1, len(tiles) - 1)]


def basis_fields(four):
    return (
        0.25 * ((four[0] + four[2]) + (four[1] + four[3])),
        0.25 * (four[2] - four[0]),
        0.25 * (four[1] - four[3]),
    )


def basis_cells(three):
    one, sine, cosine = three
    return one - sine, one + cosine, one + sine, one - cosine


def prepare_matrix(flow_ref, halo_ref, matrix_ref):
    for c in range(3):
        per_x = []
        for x in range(4):
            per_x.append(
                [
                    halo_ref[c, pl.ds(4 + x, DEPTH, stride=8), :],
                    flow_ref[c, pl.ds(x, DEPTH, stride=8), :],
                    flow_ref[c, pl.ds(4 + x, DEPTH, stride=8), :],
                    halo_ref[c, pl.ds(x, DEPTH, stride=8), :],
                ]
            )
        by_basis = [basis_fields([per_x[x][t] for x in range(4)]) for t in range(4)]
        for xf in range(3):
            tiles = [by_basis[t][xf] for t in range(4)]
            four = [shifted(tiles, s) for s in (-1, 0, 1, 2)]
            for half in range(2):
                fields = basis_fields([four[s][half] for s in range(4)])
                for yf in range(3):
                    row = ((c * 3 + yf) * 3 + xf) * DEPTH
                    high = fields[yf].astype(jnp.bfloat16)
                    low = (fields[yf] - high.astype(jnp.float32)).astype(jnp.bfloat16)
                    matrix_ref[row : row + DEPTH, half * 128 : half * 128 + 128] = high
                    matrix_ref[row : row + DEPTH, 256 + half * 128 : 256 + half * 128 + 128] = low


def couple(slots, table_ref, matrix_ref, total_ref, speed_ref):
    rows = 3 * FIELDS * DEPTH
    width = GROUP * BLOCK
    total_ref[...] = jnp.zeros_like(total_ref)
    column = lax.broadcasted_iota(jnp.int32, (256, BLOCK), 0).astype(jnp.float32)
    z_cell = lax.broadcasted_iota(jnp.int32, (DEPTH, BLOCK), 0).astype(jnp.float32)

    def body(step, carry):
        first = step * GROUP
        hot, weight_z, coef = [], [], []
        for g in range(GROUP):
            slot = first + g
            q = lambda k: table_ref[slot, k : k + 1, :]
            hot.append(jnp.where(column == q(0), 1.0, 0.0).astype(jnp.bfloat16))
            gap = z_cell - q(5)
            sine, cosine = q(6), q(7)
            weight_z.append(
                jnp.where(
                    gap == -1.0,
                    0.25 - 0.25 * sine,
                    jnp.where(
                        gap == 0.0,
                        0.25 + 0.25 * cosine,
                        jnp.where(gap == 1.0, 0.25 + 0.25 * sine, jnp.where(gap == 2.0, 0.25 - 0.25 * cosine, 0.0)),
                    ),
                )
            )
            by, bx = (None, q(1), q(2)), (None, q(3), q(4))
            coef.append(
                [
                    [by[i] if bx[k] is None else bx[k] if by[i] is None else by[i] * bx[k] for k in range(3)]
                    for i in range(3)
                ]
            )
        hot = jnp.concatenate(hot, axis=1)
        across = jnp.dot(
            matrix_ref[...], jnp.concatenate([hot, hot], axis=0), preferred_element_type=jnp.float32
        )
        spread_high, spread_low = [], []
        for g in range(GROUP):
            slot = first + g
            columns = slice(g * BLOCK, (g + 1) * BLOCK)
            pieces = []
            for c in range(3):
                sums = None
                for yf in range(3):
                    for xf in range(3):
                        row = ((c * 3 + yf) * 3 + xf) * DEPTH
                        term = across[row : row + DEPTH, columns]
                        factor = coef[g][yf][xf]
                        term = term if factor is None else term * factor
                        sums = term if sums is None else sums + term
                speed = jnp.sum(sums * weight_z[g], axis=0, keepdims=True)
                speed_ref[slot, c : c + 1, :] = speed
                push = (table_ref[slot, 8 + c : 9 + c, :] - feedback_gain * speed) * table_ref[slot, 11:12, :]
                for yf in range(3):
                    for xf in range(3):
                        factor = coef[g][yf][xf]
                        pieces.append(weight_z[g] * (push if factor is None else push * factor))
            piece = jnp.concatenate(pieces, axis=0)
            high = piece.astype(jnp.bfloat16)
            spread_high.append(high)
            spread_low.append((piece - high.astype(jnp.float32)).astype(jnp.bfloat16))
        left = jnp.concatenate(spread_high + spread_low, axis=1)
        total_ref[...] += lax.dot_general(
            left,
            jnp.concatenate([hot, hot], axis=1),
            (((1,), (1,)), ((), ())),
            preferred_element_type=jnp.float32,
        )
        return carry

    lax.fori_loop(0, slots // GROUP, body, 0)


def finish_force(total_ref, halo_ref, force_ref, force_edge_ref):
    lane = lax.broadcasted_iota(jnp.int32, (DEPTH, 128), 1)
    zero = jnp.zeros((DEPTH, 128), jnp.float32)
    for c in range(3):
        by_basis = []
        for xf in range(3):
            field = []
            for yf in range(3):
                row = ((c * 3 + yf) * 3 + xf) * DEPTH
                field.append([total_ref[row : row + DEPTH, 0:128], total_ref[row : row + DEPTH, 128:256]])
            cells = [basis_cells([field[yf][half] for yf in range(3)]) for half in range(2)]
            sums = None
            for k, shift in enumerate((1, 0, -1, -2)):
                tiles = shifted([zero, zero, cells[0][k], cells[1][k], zero, zero], shift)
                sums = tiles if sums is None else [a + b for a, b in zip(sums, tiles)]
            by_basis.append(sums)
        by_x = [basis_cells([by_basis[xf][t] * 0.0625 for xf in range(3)]) for t in range(4)]
        for x in range(4):
            left, low, high, right = (by_x[t][x] for t in range(4))
            force_ref[c, pl.ds(x, DEPTH, stride=8), :] = low
            force_ref[c, pl.ds(4 + x, DEPTH, stride=8), :] = high
            halo_ref[c, pl.ds(4 + x, DEPTH, stride=8), :] = jnp.where(lane >= 64, left, low)
            halo_ref[c, pl.ds(x, DEPTH, stride=8), :] = jnp.where(lane >= 64, high, right)
        force_edge_ref[c] = pack_edges(lambda z: halo_ref[c, 8 * z : 8 * z + 8, :])


def flow_slices(load, flow_ref):
    for z in range(DEPTH):
        total, momentum, dens = moments(load(z))
        inverse = 1.0 / dens
        for c in range(3):
            flow_ref[c, 8 * z : 8 * z + 8, :] = momentum[c] * inverse


def flow_edges(edges, halo_ref):
    total, momentum, dens = moments(edges)
    inverse = 1.0 / dens
    for c in range(3):
        flow = momentum[c] * inverse
        for z in range(DEPTH):
            halo_ref[c, 8 * z : 8 * z + 8, :] = turn(flow, -(5 * z + 2), 1)


def gather_markers(span_y, slots, spans_ref, where_ref, stiff_ref, fraction_ref, span_ref, places_ref, picked_ref, table_ref):
    filaments = fraction_ref.shape[0] // 3
    blocks = fraction_ref.shape[1]
    block, lane = iotas((blocks, BLOCK))
    anchor = (where_ref[0] * 4).astype(jnp.float32)
    mine = where_ref[1]
    tile_start = (mine * 256).astype(jnp.float32)
    for f in range(filaments):
        places = [
            anchor + 1.0 + fraction_ref[3 * f] * (4 - 3.01),
            span_ref[f] + fraction_ref[3 * f + 1] * 256.0,
            1.0 + fraction_ref[3 * f + 2] * (DEPTH - 3.01),
        ]
        factor = stiff_ref[f].astype(jnp.float32) * (1.0 / 256.0)
        for c in range(3):
            ahead = turn(places[c], -1, 1)
            ahead = jnp.where(lane == BLOCK - 1, turn(ahead, -1, 0), ahead) - places[c]
            if c == 1:
                half = 0.5 * span_y
                ahead = jnp.where(ahead > half, ahead - span_y, jnp.where(ahead < -half, ahead + span_y, ahead))
            ahead = jnp.where((lane == BLOCK - 1) & (block == blocks - 1), 0.0, ahead)
            behind = turn(ahead, 1, 1)
            behind = jnp.where(lane == 0, turn(behind, 1, 0), behind)
            start = f * blocks * 8
            places_ref[pl.ds(start + 3 + c, blocks, stride=8), :] = (ahead - behind) * factor
        places_ref[pl.ds(start, blocks, stride=8), :] = places[0] - anchor
        places_ref[pl.ds(start + 1, blocks, stride=8), :] = places[1] - tile_start
        places_ref[pl.ds(start + 2, blocks, stride=8), :] = places[2]
    picked_ref[...] = jnp.zeros_like(picked_ref)

    def pick(index, count):
        source = pl.multiple_of(index * 8, 8)
        target = pl.multiple_of(count * 8, 8)
        picked_ref[pl.ds(target, 8), :] = places_ref[pl.ds(source, 8), :]
        return count + (spans_ref[index] == mine).astype(jnp.int32)

    count = lax.fori_loop(0, filaments * blocks, pick, jnp.int32(0))
    got = lambda k: picked_ref[pl.ds(k, slots, stride=8), :]
    slot, _ = iotas((slots, BLOCK))

    def put(k, value):
        table_ref[:, k, :] = value

    def basis(t):
        return jnp.cos((0.5 * math.pi) * (1.0 - t)), jnp.cos((0.5 * math.pi) * t)

    y = got(1)
    base = jnp.minimum(jnp.floor(y), 255.0)
    put(0, base)
    sine, cosine = basis(y - base)
    put(1, sine)
    put(2, cosine)
    sine, cosine = basis(got(0) - 1.0)
    put(3, sine)
    put(4, cosine)
    z = got(2)
    base = jnp.floor(z)
    put(5, base)
    sine, cosine = basis(z - base)
    put(6, sine)
    put(7, cosine)
    for c in range(3):
        put(8 + c, got(3 + c))
    put(11, jnp.where(slot < count, 1.0, 0.0))


def first_kernel(
    span_y, slots, spans_ref, where_ref, stiff_ref,
    pop_ref, edge_ref, left_ref, right_ref, fraction_ref, span_ref,
    force_ref, force_edge_ref, edges_ref, table_ref,
    flow_ref, halo_ref, matrix_ref, total_ref, speed_ref, places_ref, picked_ref,
):
    gather_markers(span_y, slots, spans_ref, where_ref, stiff_ref, fraction_ref, span_ref, places_ref, picked_ref, table_ref)
    row, lane = iotas()
    j = lane % 5
    from_left = (row >= 4) & (j < 2)
    from_right = (row < 4) & (j >= 2)
    edges = []
    for entry in range(19):
        own = turn(edge_ref[entry], 4, 0)
        value = jnp.where(from_left, left_ref[entry], jnp.where(from_right, right_ref[entry], own))
        edges_ref[entry] = value
        edges.append(value)
    flow_slices(lambda z: [pop_ref[e, 8 * z : 8 * z + 8, :] for e in range(19)], flow_ref)
    flow_edges(edges, halo_ref)
    prepare_matrix(flow_ref, halo_ref, matrix_ref)
    couple(slots, table_ref, matrix_ref, total_ref, speed_ref)
    finish_force(total_ref, halo_ref, force_ref, force_edge_ref)


def collide_kernel(pop_ref, edges_ref, force_ref, force_edge_ref, left_ref, right_ref, post_ref, post_edge_ref, east_ref, west_ref):
    row, lane = iotas()
    force_edge = [
        force_edge_ref[c] + jnp.where(row >= 4, turn(left_ref[c], 4, 0), turn(right_ref[c], 4, 0)) for c in range(3)
    ]
    swapped = [turn(value, 4, 0) for value in force_edge]
    patch = ((row < 4) & (lane < 3)) | ((row >= 4) & (lane >= 126))
    for z in range(DEPTH):
        part = slice(8 * z, 8 * z + 8)
        force = [jnp.where(patch, turn(swapped[c], -(5 * z + 2), 1), force_ref[c, part, :]) for c in range(3)]
        post = collide([pop_ref[e, part, :] for e in range(19)], force)
        for e in range(19):
            post_ref[e, part, :] = post[e]
    post = collide([edges_ref[e] for e in range(19)], force_edge)
    for e in range(19):
        post_edge_ref[e] = post[e]
    for k in range(5):
        east_ref[k, 0:32, :] = post_ref[EAST[k], pl.ds(3, 32, stride=4), :]
        east_ref[k, 32:40, :] = post[EAST[k]]
        west_ref[k, 0:32, :] = post_ref[WEST[k], pl.ds(0, 32, stride=4), :]
        west_ref[k, 32:40, :] = post[WEST[k]]


def stream(post_ref, post_edge_ref, east_ref, west_ref, moved_ref, store, store_edge):
    row, lane = iotas()
    patches = {1: (row < 4) & (lane == 0), -1: (row >= 4) & (lane == 127)}
    low_wall, high_wall = lane < 5, lane >= 75
    for e in range(19):
        cx, cy, cz = velocity_set[e]
        edge = post_edge_ref[e]
        if cx == 1:
            k = EAST.index(e)
            edge = jnp.where(row % 4 == 0, turn(east_ref[k, 32:40, :], 5, 0), turn(edge, 1, 0))
        elif cx == -1:
            k = WEST.index(e)
            edge = jnp.where(row % 4 == 3, turn(west_ref[k, 32:40, :], 3, 0), turn(edge, -1, 0))
        edge = turn(edge, cy + 5 * cz, 1)
        if cz == 1:
            edge = jnp.where(low_wall, post_edge_ref[opposite(e)], edge)
        elif cz == -1:
            edge = jnp.where(high_wall, post_edge_ref[opposite(e)], edge)
        store_edge(e, edge)
        if cx != 0:
            for z in range(DEPTH):
                moved_ref[k, 8 * z : 8 * z + 8, :] = turn(post_ref[e, 8 * z : 8 * z + 8, :], cx, 0)
            if cx == 1:
                moved_ref[k, pl.ds(0, 32, stride=4), :] = east_ref[k, 0:32, :]
            else:
                moved_ref[k, pl.ds(3, 32, stride=4), :] = west_ref[k, 0:32, :]
        swapped = turn(edge, 4, 0)
        for z in range(DEPTH):
            source = z - cz
            if 0 <= source < DEPTH:
                part = slice(8 * source, 8 * source + 8)
                value = post_ref[e, part, :] if cx == 0 else moved_ref[k, part, :]
                if cy != 0:
                    value = turn(value, cy, 1)
                    value = jnp.where(lane == (0 if cy == 1 else 127), turn(value, 4, 0), value)
                    value = jnp.where(patches[cy], turn(swapped, -(5 * z + 2), 1), value)
            else:
                value = post_ref[opposite(e), 8 * z : 8 * z + 8, :]
            store(e, z, value)


def second_kernel(
    slots, blocks, shares, spans_ref, where_ref,
    post_ref, post_edge_ref, east_ref, west_ref, table_ref,
    dev_ref, edges_ref, force_ref, force_edge_ref, speeds_ref,
    moved_ref, flow_ref, halo_ref, matrix_ref, total_ref, speed_ref, spot_ref,
):
    def store(e, z, value):
        dev_ref[e, 8 * z : 8 * z + 8, :] = value

    def store_edge(e, value):
        edges_ref[e] = value

    stream(post_ref, post_edge_ref, east_ref, west_ref, moved_ref, store, store_edge)
    flow_slices(lambda z: [dev_ref[e, 8 * z : 8 * z + 8, :] for e in range(19)], flow_ref)
    flow_edges([edges_ref[e] for e in range(19)], halo_ref)
    prepare_matrix(flow_ref, halo_ref, matrix_ref)
    speed_ref[...] = jnp.zeros_like(speed_ref)
    couple(slots, table_ref, matrix_ref, total_ref, speed_ref)
    finish_force(total_ref, halo_ref, force_ref, force_edge_ref)
    mine = where_ref[1]

    def place(index, count):
        here = spans_ref[index] == mine
        value = speed_ref[jnp.minimum(count, slots - 1)]
        spot_ref[pl.ds(pl.multiple_of(index * 8, 8), 8), :] = jnp.where(here, value, 0.0)
        return count + here.astype(jnp.int32)

    lax.fori_loop(0, spans_ref.shape[0], place, jnp.int32(0))
    filaments = spans_ref.shape[0] // blocks
    share = blocks // shares
    for s in range(shares):
        for f in range(filaments):
            for c in range(3):
                speeds_ref[s, 3 * f + c] = spot_ref[pl.ds((f * blocks + s * share) * 8 + c, share, stride=8), :]


def last_kernel(post_ref, post_edge_ref, east_ref, west_ref, dev_ref, moved_ref):
    def store(e, z, value):
        dev_ref[e, 8 * z : 8 * z + 8, :] = value

    stream(post_ref, post_edge_ref, east_ref, west_ref, moved_ref, store, lambda e, value: None)


def call(body, outs, scratch, n_smem, args):
    spec = [pl.BlockSpec(memory_space=pltpu.SMEM)] * n_smem
    spec += [pl.BlockSpec(memory_space=pltpu.VMEM)] * (len(args) - n_smem)
    return pl.pallas_call(
        body,
        out_shape=[jax.ShapeDtypeStruct(shape, jnp.float32) for shape in outs],
        in_specs=spec,
        out_specs=[pl.BlockSpec(memory_space=pltpu.VMEM)] * len(outs),
        scratch_shapes=scratch,
        compiler_params=pltpu.CompilerParams(vmem_limit_bytes=VMEM_LIMIT),
    )(*args)


def ring(value, axis, step):
    count = lax.axis_size(axis)
    return lax.ppermute(value, axis, [(i, (i + step) % count) for i in range(count)])


def per_device(populations, fraction, spans, stiffness):
    depth, tile_x, tile_y = populations.shape[1:]
    columns = lax.axis_size("gy")
    span_y = float(tile_y * columns)
    my_row, my_column = lax.axis_index("gx"), lax.axis_index("gy")
    filaments, _, share = fraction.shape
    blocks = spans.shape[1]
    share_blocks = share // BLOCK
    slots = max(GROUP, 2 * filaments * blocks // columns)
    f32 = jnp.float32

    field = (19, ROWS, 128)
    edge = (19, 8, 128)
    halves = tile_y // 128
    pop = populations.reshape(19, depth, tile_x, halves, 128).transpose(0, 1, 3, 2, 4).reshape(field)
    rows = lax.all_gather(fraction.reshape(filaments * 3, share_blocks, BLOCK), "gy", axis=0)
    rows = rows.transpose(1, 0, 2, 3).reshape(filaments * 3, blocks, BLOCK)
    flat_spans = spans[:, :, 0].reshape(-1)
    span_rows = jnp.broadcast_to((spans * tile_y).astype(f32), (filaments, blocks, BLOCK))
    where = jnp.stack([my_row, my_column]).astype(jnp.int32)

    (own_edge,) = call(edge_kernel, [edge], [], 0, (pop,))
    left, right = ring(own_edge, "gy", 1), ring(own_edge, "gy", -1)

    force_shape, force_edge_shape = (3, ROWS, 128), (3, 8, 128)
    table_shape = (slots, 16, BLOCK)
    coupling = [
        pltpu.VMEM(force_shape, f32),
        pltpu.VMEM(force_shape, f32),
        pltpu.VMEM((3 * FIELDS * DEPTH, 512), jnp.bfloat16),
        pltpu.VMEM((3 * FIELDS * DEPTH, 256), f32),
        pltpu.VMEM((slots, 8, BLOCK), f32),
    ]
    force, force_edge, edges, table = call(
        functools.partial(first_kernel, span_y, slots),
        [force_shape, force_edge_shape, edge, table_shape],
        coupling + [pltpu.VMEM((filaments * blocks * 8, BLOCK), f32), pltpu.VMEM(((slots + 1) * 8, BLOCK), f32)],
        3,
        (flat_spans, where, stiffness, pop, own_edge, left, right, rows, span_rows),
    )

    plane = (5, 40, 128)
    moved = pltpu.VMEM((5, ROWS, 128), f32)

    def collision(dev, edges, force, force_edge):
        left, right = ring(force_edge, "gy", 1), ring(force_edge, "gy", -1)
        post, post_edge, east, west = call(
            collide_kernel, [field, edge, plane, plane], [], 0, (dev, edges, force, force_edge, left, right)
        )
        return post, post_edge, ring(east, "gx", 1), ring(west, "gx", -1)

    post = collision(pop, edges, force, force_edge)
    speeds_shape = (columns, filaments * 3, share_blocks, BLOCK)
    dev, edges, force, force_edge, speeds = call(
        functools.partial(second_kernel, slots, blocks, columns),
        [field, edge, force_shape, force_edge_shape, speeds_shape],
        [moved] + coupling + [pltpu.VMEM((filaments * blocks * 8, BLOCK), f32)],
        2,
        (flat_spans, where) + tuple(post) + (table,),
    )
    post = collision(dev, edges, force, force_edge)
    speed = jnp.sum(lax.all_to_all(speeds, "gy", 0, 0, tiled=True), axis=0)
    (dev,) = call(last_kernel, [field], [moved], 0, tuple(post))
    dev = dev.reshape(19, depth, halves, tile_x, 128).transpose(0, 1, 3, 2, 4).reshape(populations.shape)
    return dev, speed.reshape(fraction.shape)


def solution(mesh):
    placed = (P(None, None, "gx", "gy"), P("gx", None, "gy"), P("gx", None, None), P("gx"))
    return jax.shard_map(
        per_device,
        mesh=mesh,
        in_specs=placed,
        out_specs=(P(None, None, "gx", "gy"), P("gx", None, "gy")),
        check_vma=False,
    )
```

```python
import functools
import math

import jax
import jax.numpy as jnp
from jax import lax
from jax.experimental import pallas as pl
from jax.experimental.pallas import tpu as pltpu
from jax.sharding import PartitionSpec as P

STEPS = 2

velocity_set = (
    (0, 0, 0),
    (1, 0, 0),
    (-1, 0, 0),
    (0, 1, 0),
    (0, -1, 0),
    (0, 0, 1),
    (0, 0, -1),
    (1, 1, 0),
    (-1, -1, 0),
    (1, -1, 0),
    (-1, 1, 0),
    (1, 0, 1),
    (-1, 0, -1),
    (1, 0, -1),
    (-1, 0, 1),
    (0, 1, 1),
    (0, -1, -1),
    (0, 1, -1),
    (0, -1, 1),
)
lattice_weight = (1.0 / 3.0,) + (1.0 / 18.0,) * 6 + (1.0 / 36.0,) * 12
unit = 0.002
feedback_gain = 2.0
EAST = tuple(i for i in range(19) if velocity_set[i][0] == 1)
WEST = tuple(i for i in range(19) if velocity_set[i][0] == -1)
STILL = tuple(i for i in range(19) if velocity_set[i][0] == 0)
MOVING = EAST + WEST

DEPTH = 16
ROWS = DEPTH * 8
BLOCK = 128
GROUP = 4
FIELDS = 9
VMEM_LIMIT = 40 * 1024 * 1024


def opposite(entry):
    return entry + 1 if entry % 2 == 1 else entry - 1


def iotas(shape=(8, 128)):
    return lax.broadcasted_iota(jnp.int32, shape, 0), lax.broadcasted_iota(jnp.int32, shape, 1)


def turn(value, shift, axis):
    shift = shift % value.shape[axis]
    return pltpu.roll(value, shift, axis) if shift else value


def pack_edges(slices):
    _, lane = iotas()
    total = jnp.zeros((8, 128), jnp.float32)
    for z in range(DEPTH):
        total = jnp.where((lane >= 5 * z) & (lane < 5 * z + 5), turn(slices(z), 5 * z + 2, 1), total)
    return total


def signed_sum(terms):
    total = None
    for sign, value in terms:
        if total is None:
            total = value if sign > 0 else -value
        else:
            total = total + value if sign > 0 else total - value
    return total


def dot_c(vector, parts):
    return signed_sum([(vector[a], parts[a]) for a in range(3) if vector[a] != 0])


def moments(dev):
    total = dev[0]
    for entry in range(1, 19):
        total = total + dev[entry]
    momentum = [
        signed_sum([(velocity_set[e][a], dev[e]) for e in range(19) if velocity_set[e][a] != 0]) for a in range(3)
    ]
    return total, momentum, 1.0 + unit * total


def collide(dev, force):
    total, momentum, dens = moments(dev)
    inverse = 1.0 / dens
    vel = [(momentum[a] + 0.5 * force[a]) * inverse for a in range(3)]
    odd_base = [3.75 * momentum[a] + 3.0 * force[a] for a in range(3)]
    even_base = [5.625 * momentum[a] + 6.1875 * force[a] for a in range(3)]
    along = vel[0] * even_base[0] + vel[1] * even_base[1] + vel[2] * even_base[2]
    base = 1.25 * total - (unit / 3.0) * along
    post = [lattice_weight[0] * base - 0.25 * dev[0]]
    scaled = [unit * vel[a] for a in range(3)]
    for entry in range(1, 19, 2):
        vector, weight = velocity_set[entry], lattice_weight[entry]
        odd = weight * dot_c(vector, odd_base)
        even = weight * (base + dot_c(vector, scaled) * dot_c(vector, even_base))
        post.append((even + odd) - 0.25 * dev[entry])
        post.append((even - odd) - 0.25 * dev[entry + 1])
    return post


def edge_kernel(pop_ref, edge_ref):
    for entry in range(19):
        edge_ref[entry] = pack_edges(lambda z: pop_ref[entry, 8 * z : 8 * z + 8, :])


def flow_kernel(pop_ref, flow_ref):
    flow_slices(lambda z: [pop_ref[e, 8 * z : 8 * z + 8, :] for e in range(19)], flow_ref)


def shifted(tiles, shift):
    lane = lax.broadcasted_iota(jnp.int32, tiles[0].shape, 1)
    if shift == 0:
        return tiles[1:-1]
    rolled = [turn(tile, -shift, 1) for tile in tiles]
    if shift > 0:
        return [jnp.where(lane >= 128 - shift, rolled[i + 1], rolled[i]) for i in range(1, len(tiles) - 1)]
    return [jnp.where(lane < -shift, rolled[i - 1], rolled[i]) for i in range(1, len(tiles) - 1)]


def basis_fields(four):
    return (
        0.25 * ((four[0] + four[2]) + (four[1] + four[3])),
        0.25 * (four[2] - four[0]),
        0.25 * (four[1] - four[3]),
    )


def basis_cells(three):
    one, sine, cosine = three
    return one - sine, one + cosine, one + sine, one - cosine


def prepare_matrix(flow_ref, halo_ref, matrix_ref):
    for c in range(3):
        per_x = []
        for x in range(4):
            per_x.append(
                [
                    halo_ref[c, pl.ds(4 + x, DEPTH, stride=8), :],
                    flow_ref[c, pl.ds(x, DEPTH, stride=8), :],
                    flow_ref[c, pl.ds(4 + x, DEPTH, stride=8), :],
                    halo_ref[c, pl.ds(x, DEPTH, stride=8), :],
                ]
            )
        by_basis = [basis_fields([per_x[x][t] for x in range(4)]) for t in range(4)]
        for xf in range(3):
            tiles = [by_basis[t][xf] for t in range(4)]
            four = [shifted(tiles, s) for s in (-1, 0, 1, 2)]
            for half in range(2):
                fields = basis_fields([four[s][half] for s in range(4)])
                for yf in range(3):
                    row = ((c * 3 + yf) * 3 + xf) * DEPTH
                    high = fields[yf].astype(jnp.bfloat16)
                    low = (fields[yf] - high.astype(jnp.float32)).astype(jnp.bfloat16)
                    matrix_ref[row : row + DEPTH, half * 128 : half * 128 + 128] = high
                    matrix_ref[row : row + DEPTH, 256 + half * 128 : 256 + half * 128 + 128] = low


def couple(slots, table_ref, matrix_ref, total_ref, speed_ref):
    rows = 3 * FIELDS * DEPTH
    width = GROUP * BLOCK
    total_ref[...] = jnp.zeros_like(total_ref)
    column = lax.broadcasted_iota(jnp.int32, (256, BLOCK), 0).astype(jnp.float32)
    z_cell = lax.broadcasted_iota(jnp.int32, (DEPTH, BLOCK), 0).astype(jnp.float32)

    def body(step):
        first = step * GROUP
        hot, weight_z, coef = [], [], []
        for g in range(GROUP):
            slot = first + g
            q = lambda k: table_ref[slot, k : k + 1, :]
            hot.append(jnp.where(column == q(0), 1.0, 0.0).astype(jnp.bfloat16))
            gap = z_cell - q(5)
            sine, cosine = q(6), q(7)
            weight_z.append(
                jnp.where(
                    gap == -1.0,
                    0.25 - 0.25 * sine,
                    jnp.where(
                        gap == 0.0,
                        0.25 + 0.25 * cosine,
                        jnp.where(gap == 1.0, 0.25 + 0.25 * sine, jnp.where(gap == 2.0, 0.25 - 0.25 * cosine, 0.0)),
                    ),
                )
            )
            by, bx = (None, q(1), q(2)), (None, q(3), q(4))
            coef.append(
                [
                    [by[i] if bx[k] is None else bx[k] if by[i] is None else by[i] * bx[k] for k in range(3)]
                    for i in range(3)
                ]
            )
        hot = jnp.concatenate(hot, axis=1)
        across = jnp.dot(
            matrix_ref[...], jnp.concatenate([hot, hot], axis=0), preferred_element_type=jnp.float32
        )
        spread_high, spread_low = [], []
        for g in range(GROUP):
            slot = first + g
            columns = slice(g * BLOCK, (g + 1) * BLOCK)
            pieces = []
            for c in range(3):
                sums = None
                for yf in range(3):
                    for xf in range(3):
                        row = ((c * 3 + yf) * 3 + xf) * DEPTH
                        term = across[row : row + DEPTH, columns]
                        factor = coef[g][yf][xf]
                        term = term if factor is None else term * factor
                        sums = term if sums is None else sums + term
                speed = jnp.sum(sums * weight_z[g], axis=0, keepdims=True)
                speed_ref[slot, c : c + 1, :] = speed
                push = (table_ref[slot, 8 + c : 9 + c, :] - feedback_gain * speed) * table_ref[slot, 11:12, :]
                for yf in range(3):
                    for xf in range(3):
                        factor = coef[g][yf][xf]
                        pieces.append(weight_z[g] * (push if factor is None else push * factor))
            piece = jnp.concatenate(pieces, axis=0)
            high = piece.astype(jnp.bfloat16)
            spread_high.append(high)
            spread_low.append((piece - high.astype(jnp.float32)).astype(jnp.bfloat16))
        left = jnp.concatenate(spread_high + spread_low, axis=1)
        total_ref[...] += lax.dot_general(
            left,
            jnp.concatenate([hot, hot], axis=1),
            (((1,), (1,)), ((), ())),
            preferred_element_type=jnp.float32,
        )

    for step in range(slots // GROUP):
        body(step)


def finish_force(total_ref, halo_ref, force_ref, force_edge_ref):
    lane = lax.broadcasted_iota(jnp.int32, (DEPTH, 128), 1)
    zero = jnp.zeros((DEPTH, 128), jnp.float32)
    for c in range(3):
        by_basis = []
        for xf in range(3):
            field = []
            for yf in range(3):
                row = ((c * 3 + yf) * 3 + xf) * DEPTH
                field.append([total_ref[row : row + DEPTH, 0:128], total_ref[row : row + DEPTH, 128:256]])
            cells = [basis_cells([field[yf][half] for yf in range(3)]) for half in range(2)]
            sums = None
            for k, shift in enumerate((1, 0, -1, -2)):
                tiles = shifted([zero, zero, cells[0][k], cells[1][k], zero, zero], shift)
                sums = tiles if sums is None else [a + b for a, b in zip(sums, tiles)]
            by_basis.append(sums)
        by_x = [basis_cells([by_basis[xf][t] * 0.0625 for xf in range(3)]) for t in range(4)]
        for x in range(4):
            left, low, high, right = (by_x[t][x] for t in range(4))
            force_ref[c, pl.ds(x, DEPTH, stride=8), :] = low
            force_ref[c, pl.ds(4 + x, DEPTH, stride=8), :] = high
            halo_ref[c, pl.ds(4 + x, DEPTH, stride=8), :] = jnp.where(lane >= 64, left, low)
            halo_ref[c, pl.ds(x, DEPTH, stride=8), :] = jnp.where(lane >= 64, high, right)
        force_edge_ref[8 * c : 8 * c + 8, :] = pack_edges(lambda z: halo_ref[c, 8 * z : 8 * z + 8, :])


def flow_slices(load, flow_ref):
    for z in range(DEPTH):
        total, momentum, dens = moments(load(z))
        inverse = 1.0 / dens
        for c in range(3):
            flow_ref[c, 8 * z : 8 * z + 8, :] = momentum[c] * inverse


def flow_edges(edges, halo_ref):
    total, momentum, dens = moments(edges)
    inverse = 1.0 / dens
    for c in range(3):
        flow = momentum[c] * inverse
        for z in range(DEPTH):
            halo_ref[c, 8 * z : 8 * z + 8, :] = turn(flow, -(5 * z + 2), 1)


def gather_markers(span_y, slots, filaments, spans_ref, where_ref, stiff_ref, part_refs, places_ref, picked_ref, table_ref):
    columns = len(part_refs)
    share = part_refs[0].shape[0] // (3 * filaments)
    blocks = share * columns
    block, lane = iotas((blocks, BLOCK))
    anchor = (where_ref[0] * 4).astype(jnp.float32)
    mine = where_ref[1]
    tile_start = (mine * 256).astype(jnp.float32)
    for s in range(columns):
        source = lax.rem(mine + (columns - s), columns)
        for f in range(filaments):
            for k in range(share):
                index = f * blocks + source * share + k
                span = (spans_ref[index] * 256).astype(jnp.float32)
                row = lambda c: part_refs[s][(c * share + k) * filaments + f][None, :]
                start = pl.multiple_of(index * 8, 8)
                three = [anchor + 1.0 + row(0) * (4 - 3.01), span + row(1) * 256.0, 1.0 + row(2) * (DEPTH - 3.01)]
                places_ref[pl.ds(start, 8), :] = jnp.concatenate(three + [jnp.zeros((5, BLOCK), jnp.float32)], axis=0)
    for f in range(filaments):
        factor = stiff_ref[f].astype(jnp.float32) * (1.0 / 256.0)
        start = f * blocks * 8
        places = [places_ref[pl.ds(start + c, blocks, stride=8), :] for c in range(3)]
        for c in range(3):
            ahead = turn(places[c], -1, 1)
            ahead = jnp.where(lane == BLOCK - 1, turn(ahead, -1, 0), ahead) - places[c]
            if c == 1:
                half = 0.5 * span_y
                ahead = jnp.where(ahead > half, ahead - span_y, jnp.where(ahead < -half, ahead + span_y, ahead))
            ahead = jnp.where((lane == BLOCK - 1) & (block == blocks - 1), 0.0, ahead)
            behind = turn(ahead, 1, 1)
            behind = jnp.where(lane == 0, turn(behind, 1, 0), behind)
            places_ref[pl.ds(start + 3 + c, blocks, stride=8), :] = (ahead - behind) * factor
        places_ref[pl.ds(start, blocks, stride=8), :] = places[0] - anchor
        places_ref[pl.ds(start + 1, blocks, stride=8), :] = places[1] - tile_start
    picked_ref[...] = jnp.zeros_like(picked_ref)

    def pick(index, count):
        source = pl.multiple_of(index * 8, 8)
        target = pl.multiple_of(count * 8, 8)
        picked_ref[pl.ds(target, 8), :] = places_ref[pl.ds(source, 8), :]
        return count + (spans_ref[index] == mine).astype(jnp.int32)

    count = lax.fori_loop(0, filaments * blocks, pick, jnp.int32(0), unroll=8)
    got = lambda k: picked_ref[pl.ds(k, slots, stride=8), :]
    slot, _ = iotas((slots, BLOCK))

    def put(k, value):
        table_ref[:, k, :] = value

    def basis(t):
        return jnp.cos((0.5 * math.pi) * (1.0 - t)), jnp.cos((0.5 * math.pi) * t)

    y = got(1)
    base = jnp.minimum(jnp.floor(y), 255.0)
    put(0, base)
    sine, cosine = basis(y - base)
    put(1, sine)
    put(2, cosine)
    sine, cosine = basis(got(0) - 1.0)
    put(3, sine)
    put(4, cosine)
    z = got(2)
    base = jnp.floor(z)
    put(5, base)
    sine, cosine = basis(z - base)
    put(6, sine)
    put(7, cosine)
    for c in range(3):
        put(8 + c, got(3 + c))
    put(11, jnp.where(slot < count, 1.0, 0.0))


def first_kernel(span_y, slots, filaments, columns, spans_ref, where_ref, stiff_ref, flow_ref, edge_ref, left_ref, right_ref, *refs):
    part_refs, refs = refs[:columns], refs[columns:]
    force_ref, force_edge_ref, edges_ref, table_ref = refs[:4]
    halo_ref, matrix_ref, total_ref, speed_ref, places_ref, picked_ref = refs[4:]
    gather_markers(
        span_y, slots, filaments, spans_ref, where_ref, stiff_ref, part_refs, places_ref, picked_ref, table_ref
    )
    row, lane = iotas()
    j = lane % 5
    from_left = (row >= 4) & (j < 2)
    from_right = (row < 4) & (j >= 2)
    edges = []
    for entry in range(19):
        own = turn(edge_ref[entry], 4, 0)
        value = jnp.where(from_left, left_ref[entry], jnp.where(from_right, right_ref[entry], own))
        edges_ref[entry] = value
        edges.append(value)
    flow_edges(edges, halo_ref)
    prepare_matrix(flow_ref, halo_ref, matrix_ref)
    couple(slots, table_ref, matrix_ref, total_ref, speed_ref)
    finish_force(total_ref, halo_ref, force_ref, force_edge_ref)


def collide_kernel(split, *refs):
    dev_refs, refs = refs[: split + 1], refs[split + 1 :]
    edges_ref, force_ref, force_edge_ref, left_ref, right_ref, post_ref, post_edge_ref, east_ref, west_ref = refs

    def dev(e, part):
        if not split:
            return dev_refs[0][e, part, :]
        return dev_refs[0][STILL.index(e), part, :] if e in STILL else dev_refs[1][MOVING.index(e), part, :]

    row, lane = iotas()
    force_edge = [
        force_edge_ref[8 * c : 8 * c + 8, :]
        + jnp.where(row >= 4, turn(left_ref[8 * c : 8 * c + 8, :], 4, 0), turn(right_ref[8 * c : 8 * c + 8, :], 4, 0))
        for c in range(3)
    ]
    swapped = [turn(value, 4, 0) for value in force_edge]
    patch = ((row < 4) & (lane < 3)) | ((row >= 4) & (lane >= 126))
    for z in range(DEPTH):
        part = slice(8 * z, 8 * z + 8)
        force = [jnp.where(patch, turn(swapped[c], -(5 * z + 2), 1), force_ref[c, part, :]) for c in range(3)]
        post = collide([dev(e, part) for e in range(19)], force)
        for e in range(19):
            post_ref[e, part, :] = post[e]
    post = collide([edges_ref[e] for e in range(19)], force_edge)
    for e in range(19):
        post_edge_ref[e] = post[e]
    for k in range(5):
        east_ref[k, 0:32, :] = post_ref[EAST[k], pl.ds(3, 32, stride=4), :]
        east_ref[k, 32:40, :] = post[EAST[k]]
        west_ref[k, 0:32, :] = post_ref[WEST[k], pl.ds(0, 32, stride=4), :]
        west_ref[k, 32:40, :] = post[WEST[k]]


def stream(entries, post_ref, post_edge_ref, east_ref, west_ref, moved_ref, store, store_edge):
    row, lane = iotas()
    patches = {1: (row < 4) & (lane == 0), -1: (row >= 4) & (lane == 127)}
    low_wall, high_wall = lane < 5, lane >= 75
    for e in entries:
        cx, cy, cz = velocity_set[e]
        edge = post_edge_ref[e]
        if cx == 1:
            k = EAST.index(e)
            edge = jnp.where(row % 4 == 0, turn(east_ref[k, 32:40, :], 5, 0), turn(edge, 1, 0))
        elif cx == -1:
            k = WEST.index(e)
            edge = jnp.where(row % 4 == 3, turn(west_ref[k, 32:40, :], 3, 0), turn(edge, -1, 0))
        edge = turn(edge, cy + 5 * cz, 1)
        if cz == 1:
            edge = jnp.where(low_wall, post_edge_ref[opposite(e)], edge)
        elif cz == -1:
            edge = jnp.where(high_wall, post_edge_ref[opposite(e)], edge)
        store_edge(e, edge)
        if cx != 0:
            for z in range(DEPTH):
                moved_ref[k, 8 * z : 8 * z + 8, :] = turn(post_ref[e, 8 * z : 8 * z + 8, :], cx, 0)
            if cx == 1:
                moved_ref[k, pl.ds(0, 32, stride=4), :] = east_ref[k, 0:32, :]
            else:
                moved_ref[k, pl.ds(3, 32, stride=4), :] = west_ref[k, 0:32, :]
        swapped = turn(edge, 4, 0)
        for z in range(DEPTH):
            source = z - cz
            if 0 <= source < DEPTH:
                part = slice(8 * source, 8 * source + 8)
                value = post_ref[e, part, :] if cx == 0 else moved_ref[k, part, :]
                if cy != 0:
                    value = turn(value, cy, 1)
                    value = jnp.where(lane == (0 if cy == 1 else 127), turn(value, 4, 0), value)
                    value = jnp.where(patches[cy], turn(swapped, -(5 * z + 2), 1), value)
            else:
                value = post_ref[opposite(e), 8 * z : 8 * z + 8, :]
            store(e, z, value)


def still_kernel(post_ref, post_edge_ref, dev_ref, edges_ref):
    def store(e, z, value):
        dev_ref[STILL.index(e), 8 * z : 8 * z + 8, :] = value

    def store_edge(e, value):
        edges_ref[STILL.index(e)] = value

    stream(STILL, post_ref, post_edge_ref, None, None, None, store, store_edge)


def second_kernel(
    slots, blocks, columns, spans_ref, where_ref,
    post_ref, post_edge_ref, still_ref, still_edge_ref, east_ref, west_ref, table_ref, *refs
):
    dev_ref, edges_ref, force_ref, to_right_ref, to_left_ref = refs[:5]
    share_refs, refs = refs[5 : 3 + columns], refs[3 + columns :]
    moved_ref, flow_ref, halo_ref, matrix_ref, total_ref, speed_ref, spot_ref = refs

    def store(e, z, value):
        dev_ref[MOVING.index(e), 8 * z : 8 * z + 8, :] = value

    def store_edge(e, value):
        edges_ref[e] = value

    def dev(e, z):
        part = slice(8 * z, 8 * z + 8)
        return still_ref[STILL.index(e), part, :] if e in STILL else dev_ref[MOVING.index(e), part, :]

    stream(MOVING, post_ref, post_edge_ref, east_ref, west_ref, moved_ref, store, store_edge)
    for k, e in enumerate(STILL):
        edges_ref[e] = still_edge_ref[k]
    flow_slices(lambda z: [dev(e, z) for e in range(19)], flow_ref)
    flow_edges([edges_ref[e] for e in range(19)], halo_ref)
    prepare_matrix(flow_ref, halo_ref, matrix_ref)
    speed_ref[...] = jnp.zeros_like(speed_ref)
    couple(slots, table_ref, matrix_ref, total_ref, speed_ref)
    finish_force(total_ref, halo_ref, force_ref, to_right_ref)
    to_left_ref[0:24, :] = to_right_ref[0:24, :]
    mine = where_ref[1]

    def place(index, count):
        here = spans_ref[index] == mine
        spot_ref[index] = jnp.where(here, speed_ref[jnp.minimum(count, slots - 1)], 0.0)
        return count + here.astype(jnp.int32)

    total = spans_ref.shape[0]
    lax.fori_loop(0, total, place, jnp.int32(0), unroll=8)
    filaments = total // blocks
    share = blocks // columns
    others = iter(share_refs)
    for s in range(columns):
        target, start = (to_right_ref, 24) if s == 1 else (to_left_ref, 24) if s == columns - 1 else (next(others), 0)
        owner = lax.rem(mine + s, columns)
        for f in range(filaments):
            for k in range(share):
                for c in range(3):
                    row = start + (c * share + k) * filaments + f
                    target[row : row + 1, :] = spot_ref[f * blocks + owner * share + k, c : c + 1, :]


def last_still_kernel(post_ref, post_edge_ref, dev_ref, kept_ref, sems):
    def store(e, z, value):
        kept_ref[STILL.index(e), 8 * z : 8 * z + 8, :] = value

    copies = []
    for k, e in enumerate(STILL):
        stream((e,), post_ref, post_edge_ref, None, None, None, store, lambda e, value: None)
        copies.append(pltpu.make_async_copy(kept_ref.at[k], dev_ref.at[e], sems.at[k]))
        copies[-1].start()
    for copy in copies:
        copy.wait()


def last_kernel(post_ref, post_edge_ref, east_ref, west_ref, old_ref, dev_ref, moved_ref, kept_ref, sems):
    def store(e, z, value):
        kept_ref[MOVING.index(e), 8 * z : 8 * z + 8, :] = value

    copies = []
    for k, e in enumerate(MOVING):
        stream((e,), post_ref, post_edge_ref, east_ref, west_ref, moved_ref, store, lambda e, value: None)
        copies.append(pltpu.make_async_copy(kept_ref.at[k], dev_ref.at[e], sems.at[k]))
        copies[-1].start()
    for copy in copies:
        copy.wait()


def call(body, outs, scratch, n_smem, args, flops=0, **extra):
    spec = [pl.BlockSpec(memory_space=pltpu.SMEM)] * n_smem
    spec += [pl.BlockSpec(memory_space=pltpu.VMEM)] * (len(args) - n_smem)
    moved = 4 * sum(math.prod(shape) for shape in outs)
    options = dict(
        in_specs=spec,
        out_specs=[pl.BlockSpec(memory_space=pltpu.VMEM)] * len(outs),
        cost_estimate=pl.CostEstimate(flops=flops, bytes_accessed=2 * moved, transcendentals=0),
    )
    options.update(extra)
    return pl.pallas_call(
        body,
        out_shape=[jax.ShapeDtypeStruct(shape, jnp.float32) for shape in outs],
        scratch_shapes=scratch,
        compiler_params=pltpu.CompilerParams(vmem_limit_bytes=VMEM_LIMIT),
        **options,
    )(*args)


def ring(value, axis, step):
    count = lax.axis_size(axis)
    return lax.ppermute(value, axis, [(i, (i + step) % count) for i in range(count)])


def per_device(populations, fraction, spans, stiffness):
    depth, tile_x, tile_y = populations.shape[1:]
    columns = lax.axis_size("gy")
    span_y = float(tile_y * columns)
    filaments, _, share = fraction.shape
    blocks = spans.shape[1]
    share_blocks = share // BLOCK
    slots = max(GROUP, 2 * filaments * blocks // columns)
    f32 = jnp.float32

    own_part = fraction.reshape(filaments, 3, share_blocks, BLOCK).transpose(1, 2, 0, 3)
    own_part = own_part.reshape(3 * share_blocks * filaments, BLOCK)
    parts = [own_part] + [ring(own_part, "gy", s) for s in range(1, columns)]

    field = (19, ROWS, 128)
    edge = (19, 8, 128)
    halves = tile_y // 128
    pop = populations.reshape(19, depth, tile_x, halves, 128).transpose(0, 1, 3, 2, 4).reshape(field)
    flat_spans = spans.reshape(-1)
    where = jnp.stack([lax.axis_index("gx"), lax.axis_index("gy")]).astype(jnp.int32)

    (own_edge,) = call(edge_kernel, [edge], [], 0, (pop,))
    left, right = ring(own_edge, "gy", 1), ring(own_edge, "gy", -1)
    force_shape = (3, ROWS, 128)
    (flow,) = call(flow_kernel, [force_shape], [], 0, (pop,))

    table_shape = (slots, 16, BLOCK)
    coupling = [
        pltpu.VMEM(force_shape, f32),
        pltpu.VMEM((3 * FIELDS * DEPTH, 512), jnp.bfloat16),
        pltpu.VMEM((3 * FIELDS * DEPTH, 256), f32),
        pltpu.VMEM((slots, 8, BLOCK), f32),
    ]
    force, force_edge, edges, table = call(
        functools.partial(first_kernel, span_y, slots, filaments, columns),
        [force_shape, (24, 128), edge, table_shape],
        coupling + [pltpu.VMEM((filaments * blocks * 8, BLOCK), f32), pltpu.VMEM(((slots + 1) * 8, BLOCK), f32)],
        3,
        (flat_spans, where, stiffness, flow, own_edge, left, right, *parts),
    )

    plane = (5, 40, 128)
    moved = pltpu.VMEM((5, ROWS, 128), f32)

    def collision(dev, edges, force, force_edge, left, right):
        post, post_edge, east, west = call(
            functools.partial(collide_kernel, len(dev) - 1),
            [field, edge, plane, plane], [], 0, (*dev, edges, force, force_edge, left, right),
        )
        return post, post_edge, ring(east, "gx", 1), ring(west, "gx", -1)

    left, right = ring(force_edge, "gy", 1), ring(force_edge, "gy", -1)
    post, post_edge, east, west = collision((pop,), edges, force, force_edge, left, right)
    still, still_edge = call(still_kernel, [(9, ROWS, 128), (9, 8, 128)], [], 0, (post, post_edge))
    share_rows = 3 * share_blocks * filaments
    dev, edges, force, to_right, to_left, *chunks = call(
        functools.partial(second_kernel, slots, blocks, columns),
        [(10, ROWS, 128), edge, force_shape] + [(24 + share_rows, BLOCK)] * 2 + [(share_rows, BLOCK)] * (columns - 2),
        [moved, pltpu.VMEM(force_shape, f32)] + coupling + [pltpu.VMEM((filaments * blocks, 8, BLOCK), f32)],
        2,
        (flat_spans, where, post, post_edge, still, still_edge, east, west, table),
    )
    left, right = ring(to_right, "gy", 1), ring(to_left, "gy", -1)
    post, post_edge, east, west = collision((still, dev), edges, force, to_right, left, right)
    speed = chunks[0] + left[24:] + right[24:]
    for s in range(2, columns - 1):
        speed = speed + ring(chunks[s - 1], "gy", s)
    speed = speed.reshape(3, share_blocks, filaments, BLOCK).transpose(2, 0, 1, 3).reshape(fraction.shape)

    anywhere = pl.BlockSpec(memory_space=pl.ANY)
    inside = pl.BlockSpec(memory_space=pltpu.VMEM)
    (dev,) = call(
        last_still_kernel, [field],
        [pltpu.VMEM((9, ROWS, 128), f32), pltpu.SemaphoreType.DMA((9,))],
        0, (post, post_edge), out_specs=[anywhere],
    )
    (dev,) = call(
        last_kernel, [field],
        [moved, pltpu.VMEM((10, ROWS, 128), f32), pltpu.SemaphoreType.DMA((10,))],
        0, (post, post_edge, east, west, dev),
        in_specs=[inside] * 4 + [anywhere], out_specs=[anywhere], input_output_aliases={4: 0},
    )
    dev = dev.reshape(19, depth, halves, tile_x, 128).transpose(0, 1, 3, 2, 4).reshape(populations.shape)
    return dev, speed


def solution(mesh):
    placed = (P(None, None, "gx", "gy"), P("gx", None, "gy"), P("gx", None, None), P("gx"))
    return jax.shard_map(
        per_device,
        mesh=mesh,
        in_specs=placed,
        out_specs=(P(None, None, "gx", "gy"), P("gx", None, "gy")),
        check_vma=False,
    )
```

```python
import functools
import math

import jax
import jax.numpy as jnp
from jax import lax
from jax.experimental import pallas as pl
from jax.experimental.pallas import tpu as pltpu
from jax.sharding import PartitionSpec as P

STEPS = 2

velocity_set = (
    (0, 0, 0),
    (1, 0, 0),
    (-1, 0, 0),
    (0, 1, 0),
    (0, -1, 0),
    (0, 0, 1),
    (0, 0, -1),
    (1, 1, 0),
    (-1, -1, 0),
    (1, -1, 0),
    (-1, 1, 0),
    (1, 0, 1),
    (-1, 0, -1),
    (1, 0, -1),
    (-1, 0, 1),
    (0, 1, 1),
    (0, -1, -1),
    (0, 1, -1),
    (0, -1, 1),
)
lattice_weight = (1.0 / 3.0,) + (1.0 / 18.0,) * 6 + (1.0 / 36.0,) * 12
unit = 0.002
feedback_gain = 2.0
EAST = tuple(i for i in range(19) if velocity_set[i][0] == 1)
WEST = tuple(i for i in range(19) if velocity_set[i][0] == -1)
STILL = tuple(i for i in range(19) if velocity_set[i][0] == 0)
MOVING = EAST + WEST

DEPTH = 16
ROWS = DEPTH * 8
BLOCK = 128
GROUP = 4
FIELDS = 9
EDGE_ROWS = 80
VMEM_LIMIT = 40 * 1024 * 1024


def opposite(entry):
    return entry + 1 if entry % 2 == 1 else entry - 1


def iotas(shape=(8, 128)):
    return lax.broadcasted_iota(jnp.int32, shape, 0), lax.broadcasted_iota(jnp.int32, shape, 1)


def turn(value, shift, axis):
    shift = shift % value.shape[axis]
    return pltpu.roll(value, shift, axis) if shift else value


def pack_edges(slices):
    _, lane = iotas()
    total = jnp.zeros((8, 128), jnp.float32)
    for z in range(DEPTH):
        total = jnp.where((lane >= 5 * z) & (lane < 5 * z + 5), turn(slices(z), 5 * z + 2, 1), total)
    return total


def signed_sum(terms):
    total = None
    for sign, value in terms:
        if total is None:
            total = value if sign > 0 else -value
        else:
            total = total + value if sign > 0 else total - value
    return total


def dot_c(vector, parts):
    return signed_sum([(vector[a], parts[a]) for a in range(3) if vector[a] != 0])


def moments(dev):
    total = dev[0]
    for entry in range(1, 19):
        total = total + dev[entry]
    momentum = [
        signed_sum([(velocity_set[e][a], dev[e]) for e in range(19) if velocity_set[e][a] != 0]) for a in range(3)
    ]
    return total, momentum, 1.0 + unit * total


def collide(dev, force):
    total, momentum, dens = moments(dev)
    inverse = 1.0 / dens
    vel = [(momentum[a] + 0.5 * force[a]) * inverse for a in range(3)]
    odd_base = [3.75 * momentum[a] + 3.0 * force[a] for a in range(3)]
    even_base = [5.625 * momentum[a] + 6.1875 * force[a] for a in range(3)]
    along = vel[0] * even_base[0] + vel[1] * even_base[1] + vel[2] * even_base[2]
    base = 1.25 * total - (unit / 3.0) * along
    post = [lattice_weight[0] * base - 0.25 * dev[0]]
    scaled = [unit * vel[a] for a in range(3)]
    for entry in range(1, 19, 2):
        vector, weight = velocity_set[entry], lattice_weight[entry]
        odd = weight * dot_c(vector, odd_base)
        even = weight * (base + dot_c(vector, scaled) * dot_c(vector, even_base))
        post.append((even + odd) - 0.25 * dev[entry])
        post.append((even - odd) - 0.25 * dev[entry + 1])
    return post


def merge_edges(own, left, right):
    row, lane = iotas()
    j = lane % 5
    from_left = (row >= 4) & (j < 2)
    from_right = (row < 4) & (j >= 2)
    return jnp.where(from_left, left, jnp.where(from_right, right, turn(own, 4, 0)))


def flow_kernel(pop_ref, part_ref, flow_ref, payload_ref, sem):
    rows = part_ref.shape[0]
    copy = pltpu.make_async_copy(part_ref, payload_ref.at[pl.ds(0, rows)], sem)
    copy.start()
    flow_slices(lambda z: [pop_ref[e, 8 * z : 8 * z + 8, :] for e in range(19)], flow_ref)
    for c in range(3):
        payload_ref[rows + 8 * c : rows + 8 * c + 8, :] = pack_edges(lambda z: flow_ref[c, 8 * z : 8 * z + 8, :])
    copy.wait()


def edge_kernel(pop_ref, edge_ref, to_right_ref, to_left_ref):
    row, _ = iotas()
    edges = []
    for e in range(19):
        edges.append(pack_edges(lambda z: pop_ref[e, 8 * z : 8 * z + 8, :]))
        edge_ref[e] = edges[e]
    for k in range(10):
        other = turn(edges[2 * k + 1], 4, 0) if k < 9 else edges[2 * k]
        to_right_ref[8 * k : 8 * k + 8, :] = jnp.where(row >= 4, edges[2 * k], other)
        to_left_ref[8 * k : 8 * k + 8, :] = jnp.where(row < 4, edges[2 * k], other)


def shifted(tiles, shift):
    lane = lax.broadcasted_iota(jnp.int32, tiles[0].shape, 1)
    if shift == 0:
        return tiles[1:-1]
    rolled = [turn(tile, -shift, 1) for tile in tiles]
    if shift > 0:
        return [jnp.where(lane >= 128 - shift, rolled[i + 1], rolled[i]) for i in range(1, len(tiles) - 1)]
    return [jnp.where(lane < -shift, rolled[i - 1], rolled[i]) for i in range(1, len(tiles) - 1)]


def basis_fields(four):
    return (
        0.25 * ((four[0] + four[2]) + (four[1] + four[3])),
        0.25 * (four[2] - four[0]),
        0.25 * (four[1] - four[3]),
    )


def basis_cells(three):
    one, sine, cosine = three
    return one - sine, one + cosine, one + sine, one - cosine


def prepare_matrix(flow_ref, halo_ref, matrix_ref):
    for c in range(3):
        per_x = []
        for x in range(4):
            per_x.append(
                [
                    halo_ref[c, pl.ds(4 + x, DEPTH, stride=8), :],
                    flow_ref[c, pl.ds(x, DEPTH, stride=8), :],
                    flow_ref[c, pl.ds(4 + x, DEPTH, stride=8), :],
                    halo_ref[c, pl.ds(x, DEPTH, stride=8), :],
                ]
            )
        by_basis = [basis_fields([per_x[x][t] for x in range(4)]) for t in range(4)]
        for xf in range(3):
            tiles = [by_basis[t][xf] for t in range(4)]
            four = [shifted(tiles, s) for s in (-1, 0, 1, 2)]
            for half in range(2):
                fields = basis_fields([four[s][half] for s in range(4)])
                for yf in range(3):
                    row = ((c * 3 + yf) * 3 + xf) * DEPTH
                    high = fields[yf].astype(jnp.bfloat16)
                    low = (fields[yf] - high.astype(jnp.float32)).astype(jnp.bfloat16)
                    matrix_ref[row : row + DEPTH, half * 128 : half * 128 + 128] = high
                    matrix_ref[row : row + DEPTH, 256 + half * 128 : 256 + half * 128 + 128] = low


def couple(slots, table_ref, matrix_ref, total_ref, speed_ref):
    rows = 3 * FIELDS * DEPTH
    width = GROUP * BLOCK
    total_ref[...] = jnp.zeros_like(total_ref)
    column = lax.broadcasted_iota(jnp.int32, (256, BLOCK), 0).astype(jnp.float32)
    z_cell = lax.broadcasted_iota(jnp.int32, (DEPTH, BLOCK), 0).astype(jnp.float32)

    def body(step):
        first = step * GROUP
        hot, weight_z, coef = [], [], []
        for g in range(GROUP):
            slot = first + g
            q = lambda k: table_ref[slot, k : k + 1, :]
            hot.append(jnp.where(column == q(0), 1.0, 0.0).astype(jnp.bfloat16))
            gap = z_cell - q(5)
            sine, cosine = q(6), q(7)
            weight_z.append(
                jnp.where(
                    gap == -1.0,
                    0.25 - 0.25 * sine,
                    jnp.where(
                        gap == 0.0,
                        0.25 + 0.25 * cosine,
                        jnp.where(gap == 1.0, 0.25 + 0.25 * sine, jnp.where(gap == 2.0, 0.25 - 0.25 * cosine, 0.0)),
                    ),
                )
            )
            by, bx = (None, q(1), q(2)), (None, q(3), q(4))
            coef.append(
                [
                    [by[i] if bx[k] is None else bx[k] if by[i] is None else by[i] * bx[k] for k in range(3)]
                    for i in range(3)
                ]
            )
        hot = jnp.concatenate(hot, axis=1)
        across = jnp.dot(
            matrix_ref[...], jnp.concatenate([hot, hot], axis=0), preferred_element_type=jnp.float32
        )
        spread_high, spread_low = [], []
        for g in range(GROUP):
            slot = first + g
            columns = slice(g * BLOCK, (g + 1) * BLOCK)
            pieces = []
            for c in range(3):
                sums = None
                for yf in range(3):
                    for xf in range(3):
                        row = ((c * 3 + yf) * 3 + xf) * DEPTH
                        term = across[row : row + DEPTH, columns]
                        factor = coef[g][yf][xf]
                        term = term if factor is None else term * factor
                        sums = term if sums is None else sums + term
                speed = jnp.sum(sums * weight_z[g], axis=0, keepdims=True)
                speed_ref[slot, c : c + 1, :] = speed
                push = (table_ref[slot, 8 + c : 9 + c, :] - feedback_gain * speed) * table_ref[slot, 11:12, :]
                for yf in range(3):
                    for xf in range(3):
                        factor = coef[g][yf][xf]
                        pieces.append(weight_z[g] * (push if factor is None else push * factor))
            piece = jnp.concatenate(pieces, axis=0)
            high = piece.astype(jnp.bfloat16)
            spread_high.append(high)
            spread_low.append((piece - high.astype(jnp.float32)).astype(jnp.bfloat16))
        left = jnp.concatenate(spread_high + spread_low, axis=1)
        total_ref[...] += lax.dot_general(
            left,
            jnp.concatenate([hot, hot], axis=1),
            (((1,), (1,)), ((), ())),
            preferred_element_type=jnp.float32,
        )

    for step in range(slots // GROUP):
        body(step)


def finish_force(total_ref, halo_ref, force_ref, force_edge_ref, start=0):
    lane = lax.broadcasted_iota(jnp.int32, (DEPTH, 128), 1)
    zero = jnp.zeros((DEPTH, 128), jnp.float32)
    for c in range(3):
        by_basis = []
        for xf in range(3):
            field = []
            for yf in range(3):
                row = ((c * 3 + yf) * 3 + xf) * DEPTH
                field.append([total_ref[row : row + DEPTH, 0:128], total_ref[row : row + DEPTH, 128:256]])
            cells = [basis_cells([field[yf][half] for yf in range(3)]) for half in range(2)]
            sums = None
            for k, shift in enumerate((1, 0, -1, -2)):
                tiles = shifted([zero, zero, cells[0][k], cells[1][k], zero, zero], shift)
                sums = tiles if sums is None else [a + b for a, b in zip(sums, tiles)]
            by_basis.append(sums)
        by_x = [basis_cells([by_basis[xf][t] * 0.0625 for xf in range(3)]) for t in range(4)]
        for x in range(4):
            left, low, high, right = (by_x[t][x] for t in range(4))
            force_ref[c, pl.ds(x, DEPTH, stride=8), :] = low
            force_ref[c, pl.ds(4 + x, DEPTH, stride=8), :] = high
            halo_ref[c, pl.ds(4 + x, DEPTH, stride=8), :] = jnp.where(lane >= 64, left, low)
            halo_ref[c, pl.ds(x, DEPTH, stride=8), :] = jnp.where(lane >= 64, high, right)
        row = start + 8 * c
        force_edge_ref[row : row + 8, :] = pack_edges(lambda z: halo_ref[c, 8 * z : 8 * z + 8, :])


def flow_slices(load, flow_ref):
    for z in range(DEPTH):
        total, momentum, dens = moments(load(z))
        inverse = 1.0 / dens
        for c in range(3):
            flow_ref[c, 8 * z : 8 * z + 8, :] = momentum[c] * inverse


def edge_flow(edges):
    total, momentum, dens = moments(edges)
    inverse = 1.0 / dens
    return [momentum[c] * inverse for c in range(3)]


def flow_edges(flows, halo_ref):
    for c in range(3):
        flow = flows[c]
        for z in range(DEPTH):
            halo_ref[c, 8 * z : 8 * z + 8, :] = turn(flow, -(5 * z + 2), 1)


def gather_markers(span_y, slots, filaments, share, spans_ref, where_ref, stiff_ref, part_refs, places_ref, picked_ref, table_ref):
    columns = len(part_refs)
    blocks = share * columns
    block, lane = iotas((blocks, BLOCK))
    anchor = (where_ref[0] * 4).astype(jnp.float32)
    mine = where_ref[1]
    tile_start = (mine * 256).astype(jnp.float32)
    for s in range(columns):
        source = lax.rem(mine + (columns - s), columns)
        for f in range(filaments):
            for k in range(share):
                index = f * blocks + source * share + k
                span = (spans_ref[index] * 256).astype(jnp.float32)
                row = lambda c: part_refs[s][(c * share + k) * filaments + f][None, :]
                start = pl.multiple_of(index * 8, 8)
                three = [anchor + 1.0 + row(0) * (4 - 3.01), span + row(1) * 256.0, 1.0 + row(2) * (DEPTH - 3.01)]
                places_ref[pl.ds(start, 8), :] = jnp.concatenate(three + [jnp.zeros((5, BLOCK), jnp.float32)], axis=0)
    for f in range(filaments):
        factor = stiff_ref[f].astype(jnp.float32) * (1.0 / 256.0)
        start = f * blocks * 8
        places = [places_ref[pl.ds(start + c, blocks, stride=8), :] for c in range(3)]
        for c in range(3):
            ahead = turn(places[c], -1, 1)
            ahead = jnp.where(lane == BLOCK - 1, turn(ahead, -1, 0), ahead) - places[c]
            if c == 1:
                half = 0.5 * span_y
                ahead = jnp.where(ahead > half, ahead - span_y, jnp.where(ahead < -half, ahead + span_y, ahead))
            ahead = jnp.where((lane == BLOCK - 1) & (block == blocks - 1), 0.0, ahead)
            behind = turn(ahead, 1, 1)
            behind = jnp.where(lane == 0, turn(behind, 1, 0), behind)
            places_ref[pl.ds(start + 3 + c, blocks, stride=8), :] = (ahead - behind) * factor
        places_ref[pl.ds(start, blocks, stride=8), :] = places[0] - anchor
        places_ref[pl.ds(start + 1, blocks, stride=8), :] = places[1] - tile_start
    picked_ref[...] = jnp.zeros_like(picked_ref)

    def pick(index, count):
        source = pl.multiple_of(index * 8, 8)
        target = pl.multiple_of(count * 8, 8)
        picked_ref[pl.ds(target, 8), :] = places_ref[pl.ds(source, 8), :]
        return count + (spans_ref[index] == mine).astype(jnp.int32)

    count = lax.fori_loop(0, filaments * blocks, pick, jnp.int32(0), unroll=8)
    got = lambda k: picked_ref[pl.ds(k, slots, stride=8), :]
    slot, _ = iotas((slots, BLOCK))

    def put(k, value):
        table_ref[:, k, :] = value

    def basis(t):
        return jnp.cos((0.5 * math.pi) * (1.0 - t)), jnp.cos((0.5 * math.pi) * t)

    y = got(1)
    base = jnp.minimum(jnp.floor(y), 255.0)
    put(0, base)
    sine, cosine = basis(y - base)
    put(1, sine)
    put(2, cosine)
    sine, cosine = basis(got(0) - 1.0)
    put(3, sine)
    put(4, cosine)
    z = got(2)
    base = jnp.floor(z)
    put(5, base)
    sine, cosine = basis(z - base)
    put(6, sine)
    put(7, cosine)
    for c in range(3):
        put(8 + c, got(3 + c))
    put(11, jnp.where(slot < count, 1.0, 0.0))


def first_kernel(span_y, slots, filaments, columns, spans_ref, where_ref, stiff_ref, flow_ref, right_edge_ref, left_edge_ref, *refs):
    part_refs, refs = refs[:columns], refs[columns:]
    force_ref, to_right_ref, to_left_ref, table_ref = refs[:4]
    halo_ref, matrix_ref, total_ref, speed_ref, places_ref, picked_ref = refs[4:]
    share = spans_ref.shape[0] // (filaments * columns)
    to_right_ref[0:EDGE_ROWS, :] = right_edge_ref[...]
    to_left_ref[0:EDGE_ROWS, :] = left_edge_ref[...]
    gather_markers(
        span_y, slots, filaments, share, spans_ref, where_ref, stiff_ref, part_refs, places_ref, picked_ref, table_ref
    )
    flows = []
    for c in range(3):
        start = 3 * share * filaments + 8 * c
        flows.append(merge_edges(*(part_refs[s][start : start + 8, :] for s in (0, 1, -1))))
    flow_edges(flows, halo_ref)
    prepare_matrix(flow_ref, halo_ref, matrix_ref)
    couple(slots, table_ref, matrix_ref, total_ref, speed_ref)
    finish_force(total_ref, halo_ref, force_ref, to_right_ref, EDGE_ROWS)
    to_left_ref[EDGE_ROWS:, :] = to_right_ref[EDGE_ROWS:, :]


def collide_kernel(first, *refs):
    if first:
        pop_ref, edge_ref = refs[:2]
        force_ref, own_ref, left_ref, right_ref, post_ref, post_edge_ref, east_ref, west_ref = refs[2:]
        start = EDGE_ROWS
        edges = []
        for e in range(19):
            part, shift = slice(8 * (e // 2), 8 * (e // 2) + 8), 4 * (e % 2)
            edges.append(merge_edges(edge_ref[e], turn(left_ref[part, :], shift, 0), turn(right_ref[part, :], shift, 0)))
    else:
        still_ref, moving_ref, edges_ref = refs[:3]
        force_ref, own_ref, left_ref, right_ref, post_ref, post_edge_ref, east_ref, west_ref = refs[3:]
        start = 0
        edges = [edges_ref[e] for e in range(19)]

    def dev(e, part):
        if first:
            return pop_ref[e, part, :]
        return still_ref[STILL.index(e), part, :] if e in STILL else moving_ref[MOVING.index(e), part, :]

    def force_part(ref, c):
        return ref[start + 8 * c : start + 8 * c + 8, :]

    row, lane = iotas()
    force_edge = [
        force_part(own_ref, c)
        + jnp.where(row >= 4, turn(force_part(left_ref, c), 4, 0), turn(force_part(right_ref, c), 4, 0))
        for c in range(3)
    ]
    swapped = [turn(value, 4, 0) for value in force_edge]
    patch = ((row < 4) & (lane < 3)) | ((row >= 4) & (lane >= 126))
    for z in range(DEPTH):
        part = slice(8 * z, 8 * z + 8)
        force = [jnp.where(patch, turn(swapped[c], -(5 * z + 2), 1), force_ref[c, part, :]) for c in range(3)]
        post = collide([dev(e, part) for e in range(19)], force)
        for e in range(19):
            post_ref[e, part, :] = post[e]
    post = collide(edges, force_edge)
    for e in range(19):
        post_edge_ref[e] = post[e]
    for k in range(5):
        east_ref[k, 0:32, :] = post_ref[EAST[k], pl.ds(3, 32, stride=4), :]
        east_ref[k, 32:40, :] = post[EAST[k]]
        west_ref[k, 0:32, :] = post_ref[WEST[k], pl.ds(0, 32, stride=4), :]
        west_ref[k, 32:40, :] = post[WEST[k]]


def stream(entries, post_ref, post_edge_ref, east_ref, west_ref, moved_ref, store, store_edge):
    row, lane = iotas()
    patches = {1: (row < 4) & (lane == 0), -1: (row >= 4) & (lane == 127)}
    low_wall, high_wall = lane < 5, lane >= 75
    for e in entries:
        cx, cy, cz = velocity_set[e]
        edge = post_edge_ref[e]
        if cx == 1:
            k = EAST.index(e)
            edge = jnp.where(row % 4 == 0, turn(east_ref[k, 32:40, :], 5, 0), turn(edge, 1, 0))
        elif cx == -1:
            k = WEST.index(e)
            edge = jnp.where(row % 4 == 3, turn(west_ref[k, 32:40, :], 3, 0), turn(edge, -1, 0))
        edge = turn(edge, cy + 5 * cz, 1)
        if cz == 1:
            edge = jnp.where(low_wall, post_edge_ref[opposite(e)], edge)
        elif cz == -1:
            edge = jnp.where(high_wall, post_edge_ref[opposite(e)], edge)
        store_edge(e, edge)
        if cx != 0:
            for z in range(DEPTH):
                moved_ref[k, 8 * z : 8 * z + 8, :] = turn(post_ref[e, 8 * z : 8 * z + 8, :], cx, 0)
            if cx == 1:
                moved_ref[k, pl.ds(0, 32, stride=4), :] = east_ref[k, 0:32, :]
            else:
                moved_ref[k, pl.ds(3, 32, stride=4), :] = west_ref[k, 0:32, :]
        swapped = turn(edge, 4, 0)
        for z in range(DEPTH):
            source = z - cz
            if 0 <= source < DEPTH:
                part = slice(8 * source, 8 * source + 8)
                value = post_ref[e, part, :] if cx == 0 else moved_ref[k, part, :]
                if cy != 0:
                    value = turn(value, cy, 1)
                    value = jnp.where(lane == (0 if cy == 1 else 127), turn(value, 4, 0), value)
                    value = jnp.where(patches[cy], turn(swapped, -(5 * z + 2), 1), value)
            else:
                value = post_ref[opposite(e), 8 * z : 8 * z + 8, :]
            store(e, z, value)


def still_kernel(post_ref, post_edge_ref, dev_ref, edges_ref):
    def store(e, z, value):
        dev_ref[STILL.index(e), 8 * z : 8 * z + 8, :] = value

    def store_edge(e, value):
        edges_ref[STILL.index(e)] = value

    stream(STILL, post_ref, post_edge_ref, None, None, None, store, store_edge)


def second_kernel(
    slots, blocks, columns, spans_ref, where_ref,
    post_ref, post_edge_ref, still_ref, still_edge_ref, east_ref, west_ref, table_ref, *refs
):
    dev_ref, edges_ref, force_ref, to_right_ref, to_left_ref = refs[:5]
    share_refs, refs = refs[5 : 3 + columns], refs[3 + columns :]
    moved_ref, flow_ref, halo_ref, matrix_ref, total_ref, speed_ref, spot_ref = refs

    def store(e, z, value):
        dev_ref[MOVING.index(e), 8 * z : 8 * z + 8, :] = value

    def store_edge(e, value):
        edges_ref[e] = value

    def dev(e, z):
        part = slice(8 * z, 8 * z + 8)
        return still_ref[STILL.index(e), part, :] if e in STILL else dev_ref[MOVING.index(e), part, :]

    stream(MOVING, post_ref, post_edge_ref, east_ref, west_ref, moved_ref, store, store_edge)
    for k, e in enumerate(STILL):
        edges_ref[e] = still_edge_ref[k]
    flow_slices(lambda z: [dev(e, z) for e in range(19)], flow_ref)
    flow_edges(edge_flow([edges_ref[e] for e in range(19)]), halo_ref)
    prepare_matrix(flow_ref, halo_ref, matrix_ref)
    speed_ref[...] = jnp.zeros_like(speed_ref)
    couple(slots, table_ref, matrix_ref, total_ref, speed_ref)
    finish_force(total_ref, halo_ref, force_ref, to_right_ref)
    to_left_ref[0:24, :] = to_right_ref[0:24, :]
    mine = where_ref[1]

    def place(index, count):
        here = spans_ref[index] == mine
        spot_ref[index] = jnp.where(here, speed_ref[jnp.minimum(count, slots - 1)], 0.0)
        return count + here.astype(jnp.int32)

    total = spans_ref.shape[0]
    lax.fori_loop(0, total, place, jnp.int32(0), unroll=8)
    filaments = total // blocks
    share = blocks // columns
    others = iter(share_refs)
    for s in range(columns):
        target, start = (to_right_ref, 24) if s == 1 else (to_left_ref, 24) if s == columns - 1 else (next(others), 0)
        owner = lax.rem(mine + s, columns)
        for f in range(filaments):
            for k in range(share):
                for c in range(3):
                    row = start + (c * share + k) * filaments + f
                    target[row : row + 1, :] = spot_ref[f * blocks + owner * share + k, c : c + 1, :]


def last_still_kernel(post_ref, post_edge_ref, dev_ref, kept_ref, sems):
    def store(e, z, value):
        kept_ref[STILL.index(e), 8 * z : 8 * z + 8, :] = value

    copies = []
    for k, e in enumerate(STILL):
        stream((e,), post_ref, post_edge_ref, None, None, None, store, lambda e, value: None)
        copies.append(pltpu.make_async_copy(kept_ref.at[k], dev_ref.at[e], sems.at[k]))
        copies[-1].start()
    for copy in copies:
        copy.wait()


def last_kernel(post_ref, post_edge_ref, east_ref, west_ref, old_ref, dev_ref, moved_ref, kept_ref, sems):
    def store(e, z, value):
        kept_ref[MOVING.index(e), 8 * z : 8 * z + 8, :] = value

    copies = []
    for k, e in enumerate(MOVING):
        stream((e,), post_ref, post_edge_ref, east_ref, west_ref, moved_ref, store, lambda e, value: None)
        copies.append(pltpu.make_async_copy(kept_ref.at[k], dev_ref.at[e], sems.at[k]))
        copies[-1].start()
    for copy in copies:
        copy.wait()


def call(body, outs, scratch, n_smem, args, flops=0, **extra):
    spec = [pl.BlockSpec(memory_space=pltpu.SMEM)] * n_smem
    spec += [pl.BlockSpec(memory_space=pltpu.VMEM)] * (len(args) - n_smem)
    moved = 4 * sum(math.prod(shape) for shape in outs)
    options = dict(
        in_specs=spec,
        out_specs=[pl.BlockSpec(memory_space=pltpu.VMEM)] * len(outs),
        cost_estimate=pl.CostEstimate(flops=flops, bytes_accessed=2 * moved, transcendentals=0),
    )
    options.update(extra)
    return pl.pallas_call(
        body,
        out_shape=[jax.ShapeDtypeStruct(shape, jnp.float32) for shape in outs],
        scratch_shapes=scratch,
        compiler_params=pltpu.CompilerParams(vmem_limit_bytes=VMEM_LIMIT),
        **options,
    )(*args)


def ring(value, axis, step):
    count = lax.axis_size(axis)
    return lax.ppermute(value, axis, [(i, (i + step) % count) for i in range(count)])


def per_device(populations, fraction, spans, stiffness):
    depth, tile_x, tile_y = populations.shape[1:]
    columns = lax.axis_size("gy")
    span_y = float(tile_y * columns)
    filaments, _, share = fraction.shape
    blocks = spans.shape[1]
    share_blocks = share // BLOCK
    slots = max(GROUP, 2 * filaments * blocks // columns)
    f32 = jnp.float32

    own_part = fraction.reshape(filaments, 3, share_blocks, BLOCK).transpose(1, 2, 0, 3)
    own_part = own_part.reshape(3 * share_blocks * filaments, BLOCK)

    field = (19, ROWS, 128)
    edge = (19, 8, 128)
    halves = tile_y // 128
    pop = populations.reshape(19, depth, tile_x, halves, 128).transpose(0, 1, 3, 2, 4).reshape(field)
    flat_spans = spans.reshape(-1)
    where = jnp.stack([lax.axis_index("gx"), lax.axis_index("gy")]).astype(jnp.int32)

    force_shape = (3, ROWS, 128)
    share_rows = 3 * share_blocks * filaments
    inside, anywhere = pl.BlockSpec(memory_space=pltpu.VMEM), pl.BlockSpec(memory_space=pl.ANY)
    flow, payload = call(
        flow_kernel, [force_shape, (share_rows + 24, BLOCK)], [pltpu.SemaphoreType.DMA], 0, (pop, own_part),
        in_specs=[inside, anywhere],
    )
    parts = [payload] + [ring(payload, "gy", s) for s in range(1, columns)]
    own_edge, right_edge, left_edge = call(edge_kernel, [edge, (EDGE_ROWS, 128), (EDGE_ROWS, 128)], [], 0, (pop,))

    table_shape = (slots, 16, BLOCK)
    coupling = [
        pltpu.VMEM(force_shape, f32),
        pltpu.VMEM((3 * FIELDS * DEPTH, 512), jnp.bfloat16),
        pltpu.VMEM((3 * FIELDS * DEPTH, 256), f32),
        pltpu.VMEM((slots, 8, BLOCK), f32),
    ]
    force, to_right, to_left, table = call(
        functools.partial(first_kernel, span_y, slots, filaments, columns),
        [force_shape, (EDGE_ROWS + 24, 128), (EDGE_ROWS + 24, 128), table_shape],
        coupling + [pltpu.VMEM((filaments * blocks * 8, BLOCK), f32), pltpu.VMEM(((slots + 1) * 8, BLOCK), f32)],
        3,
        (flat_spans, where, stiffness, flow, right_edge, left_edge, *parts),
    )

    plane = (5, 40, 128)
    moved = pltpu.VMEM((5, ROWS, 128), f32)

    def collision(first, dev, force, force_edge, left, right):
        post, post_edge, east, west = call(
            functools.partial(collide_kernel, first),
            [field, edge, plane, plane], [], 0, (*dev, force, force_edge, left, right),
        )
        return post, post_edge, ring(east, "gx", 1), ring(west, "gx", -1)

    left, right = ring(to_right, "gy", 1), ring(to_left, "gy", -1)
    post, post_edge, east, west = collision(True, (pop, own_edge), force, to_right, left, right)
    still, still_edge = call(still_kernel, [(9, ROWS, 128), (9, 8, 128)], [], 0, (post, post_edge))
    dev, edges, force, to_right, to_left, *chunks = call(
        functools.partial(second_kernel, slots, blocks, columns),
        [(10, ROWS, 128), edge, force_shape] + [(24 + share_rows, BLOCK)] * 2 + [(share_rows, BLOCK)] * (columns - 2),
        [moved, pltpu.VMEM(force_shape, f32)] + coupling + [pltpu.VMEM((filaments * blocks, 8, BLOCK), f32)],
        2,
        (flat_spans, where, post, post_edge, still, still_edge, east, west, table),
    )
    left, right = ring(to_right, "gy", 1), ring(to_left, "gy", -1)
    post, post_edge, east, west = collision(False, (still, dev, edges), force, to_right, left, right)
    speed = chunks[0] + left[24:] + right[24:]
    for s in range(2, columns - 1):
        speed = speed + ring(chunks[s - 1], "gy", s)
    speed = speed.reshape(3, share_blocks, filaments, BLOCK).transpose(2, 0, 1, 3).reshape(fraction.shape)

    (dev,) = call(
        last_still_kernel, [field],
        [pltpu.VMEM((9, ROWS, 128), f32), pltpu.SemaphoreType.DMA((9,))],
        0, (post, post_edge), out_specs=[anywhere],
    )
    (dev,) = call(
        last_kernel, [field],
        [moved, pltpu.VMEM((10, ROWS, 128), f32), pltpu.SemaphoreType.DMA((10,))],
        0, (post, post_edge, east, west, dev),
        in_specs=[inside] * 4 + [anywhere], out_specs=[anywhere], input_output_aliases={4: 0},
    )
    dev = dev.reshape(19, depth, halves, tile_x, 128).transpose(0, 1, 3, 2, 4).reshape(populations.shape)
    return dev, speed


def solution(mesh):
    placed = (P(None, None, "gx", "gy"), P("gx", None, "gy"), P("gx", None, None), P("gx"))
    return jax.shard_map(
        per_device,
        mesh=mesh,
        in_specs=placed,
        out_specs=(P(None, None, "gx", "gy"), P("gx", None, "gy")),
        check_vma=False,
    )
```

```python
import functools
import math

import jax
import jax.numpy as jnp
from jax import lax
from jax.experimental import pallas as pl
from jax.experimental.pallas import tpu as pltpu
from jax.sharding import PartitionSpec as P

STEPS = 2

velocity_set = (
    (0, 0, 0),
    (1, 0, 0),
    (-1, 0, 0),
    (0, 1, 0),
    (0, -1, 0),
    (0, 0, 1),
    (0, 0, -1),
    (1, 1, 0),
    (-1, -1, 0),
    (1, -1, 0),
    (-1, 1, 0),
    (1, 0, 1),
    (-1, 0, -1),
    (1, 0, -1),
    (-1, 0, 1),
    (0, 1, 1),
    (0, -1, -1),
    (0, 1, -1),
    (0, -1, 1),
)
lattice_weight = (1.0 / 3.0,) + (1.0 / 18.0,) * 6 + (1.0 / 36.0,) * 12
unit = 0.002
feedback_gain = 2.0
EAST = tuple(i for i in range(19) if velocity_set[i][0] == 1)
WEST = tuple(i for i in range(19) if velocity_set[i][0] == -1)
STILL = tuple(i for i in range(19) if velocity_set[i][0] == 0)
MOVING = EAST + WEST

DEPTH = 16
ROWS = DEPTH * 8
BLOCK = 128
GROUP = 32
PLANE = 160
PLANE_ROWS = 176
FIELDS = 9
EDGE_ROWS = 80
TINY = 1e-30
FINE = jnp.float8_e4m3fn
VMEM_LIMIT = 40 * 1024 * 1024


def opposite(entry):
    return entry + 1 if entry % 2 == 1 else entry - 1


def iotas(shape=(8, 128)):
    return lax.broadcasted_iota(jnp.int32, shape, 0), lax.broadcasted_iota(jnp.int32, shape, 1)


def turn(value, shift, axis):
    shift = shift % value.shape[axis]
    return pltpu.roll(value, shift, axis) if shift else value


def pack_edges(slices):
    _, lane = iotas()
    total = jnp.zeros((8, 128), jnp.float32)
    for z in range(DEPTH):
        total = jnp.where((lane >= 5 * z) & (lane < 5 * z + 5), turn(slices(z), 5 * z + 2, 1), total)
    return total


def signed_sum(terms):
    total = None
    for sign, value in terms:
        if total is None:
            total = value if sign > 0 else -value
        else:
            total = total + value if sign > 0 else total - value
    return total


def dot_c(vector, parts):
    return signed_sum([(vector[a], parts[a]) for a in range(3) if vector[a] != 0])


def moments(dev):
    total = dev[0]
    for entry in range(1, 19):
        total = total + dev[entry]
    momentum = [
        signed_sum([(velocity_set[e][a], dev[e]) for e in range(19) if velocity_set[e][a] != 0]) for a in range(3)
    ]
    return total, momentum, 1.0 + unit * total


def collide(dev, force):
    total, momentum, dens = moments(dev)
    inverse = 1.0 / dens
    vel = [(momentum[a] + 0.5 * force[a]) * inverse for a in range(3)]
    odd_base = [3.75 * momentum[a] + 3.0 * force[a] for a in range(3)]
    even_base = [5.625 * momentum[a] + 6.1875 * force[a] for a in range(3)]
    along = vel[0] * even_base[0] + vel[1] * even_base[1] + vel[2] * even_base[2]
    base = 1.25 * total - (unit / 3.0) * along
    post = [lattice_weight[0] * base - 0.25 * dev[0]]
    scaled = [unit * vel[a] for a in range(3)]
    for entry in range(1, 19, 2):
        vector, weight = velocity_set[entry], lattice_weight[entry]
        odd = weight * dot_c(vector, odd_base)
        even = weight * (base + dot_c(vector, scaled) * dot_c(vector, even_base))
        post.append((even + odd) - 0.25 * dev[entry])
        post.append((even - odd) - 0.25 * dev[entry + 1])
    return post


def merge_edges(own, left, right):
    row, lane = iotas()
    j = lane % 5
    from_left = (row >= 4) & (j < 2)
    from_right = (row < 4) & (j >= 2)
    return jnp.where(from_left, left, jnp.where(from_right, right, turn(own, 4, 0)))


def flow_kernel(pop_ref, part_ref, flow_ref, payload_ref, sem):
    rows = part_ref.shape[0]
    copy = pltpu.make_async_copy(part_ref, payload_ref.at[pl.ds(0, rows)], sem)
    copy.start()
    flow_slices(lambda z: [pop_ref[e, 8 * z : 8 * z + 8, :] for e in range(19)], flow_ref)
    for c in range(3):
        payload_ref[rows + 8 * c : rows + 8 * c + 8, :] = pack_edges(lambda z: flow_ref[c, 8 * z : 8 * z + 8, :])
    copy.wait()


def edge_kernel(pop_ref, edge_ref, to_right_ref, to_left_ref):
    row, _ = iotas()
    edges = []
    for e in range(19):
        edges.append(pack_edges(lambda z: pop_ref[e, 8 * z : 8 * z + 8, :]))
        edge_ref[e] = edges[e]
    for k in range(10):
        other = turn(edges[2 * k + 1], 4, 0) if k < 9 else edges[2 * k]
        to_right_ref[8 * k : 8 * k + 8, :] = jnp.where(row >= 4, edges[2 * k], other)
        to_left_ref[8 * k : 8 * k + 8, :] = jnp.where(row < 4, edges[2 * k], other)


def shifted(tiles, shift):
    lane = lax.broadcasted_iota(jnp.int32, tiles[0].shape, 1)
    if shift == 0:
        return tiles[1:-1]
    rolled = [turn(tile, -shift, 1) for tile in tiles]
    if shift > 0:
        return [jnp.where(lane >= 128 - shift, rolled[i + 1], rolled[i]) for i in range(1, len(tiles) - 1)]
    return [jnp.where(lane < -shift, rolled[i - 1], rolled[i]) for i in range(1, len(tiles) - 1)]


def basis_fields(four):
    return (
        0.25 * ((four[0] + four[2]) + (four[1] + four[3])),
        0.25 * (four[2] - four[0]),
        0.25 * (four[1] - four[3]),
    )


def basis_cells(three):
    one, sine, cosine = three
    return one - sine, one + cosine, one + sine, one - cosine


def largest(value):
    return jnp.max(jnp.max(jnp.abs(value), axis=1, keepdims=True), axis=0, keepdims=True)


def prepare_matrix(flow_ref, halo_ref, matrix_ref, rest_ref):
    top = None
    for c in range(3):
        for z in range(DEPTH):
            part = slice(8 * z, 8 * z + 8)
            both = jnp.maximum(jnp.abs(flow_ref[c, part, :]), jnp.abs(halo_ref[c, part, :]))
            top = both if top is None else jnp.maximum(top, both)
    top = jnp.maximum(largest(top), TINY)
    scale = 2.0**15 / top
    for c in range(3):
        per_x = []
        for x in range(4):
            tiles = [
                halo_ref[c, pl.ds(4 + x, DEPTH, stride=8), :],
                flow_ref[c, pl.ds(x, DEPTH, stride=8), :],
                flow_ref[c, pl.ds(4 + x, DEPTH, stride=8), :],
                halo_ref[c, pl.ds(x, DEPTH, stride=8), :],
            ]
            per_x.append([tile * scale for tile in tiles])
        by_basis = [basis_fields([per_x[x][t] for x in range(4)]) for t in range(4)]
        for xf in range(3):
            tiles = [by_basis[t][xf] for t in range(4)]
            four = [shifted(tiles, s) for s in (-1, 0, 1, 2)]
            for half in range(2):
                fields = basis_fields([four[s][half] for s in range(4)])
                columns = slice(half * 128, half * 128 + 128)
                for yf in range(3):
                    row = ((c * 3 + yf) * 3 + xf) * DEPTH
                    high = fields[yf].astype(jnp.bfloat16)
                    matrix_ref[row : row + DEPTH, columns] = high
                    rest_ref[row : row + DEPTH, columns] = fields[yf] - high.astype(jnp.float32)
    return top


def couple(slots, table_ref, matrix_ref, rest_ref, total_ref, speed_ref, top):
    group = min(GROUP, slots)
    unscale = top * 2.0**-15
    bound = jnp.maximum(table_ref[0, 12:13, 0:1] + feedback_gain * top, TINY)
    scale = 2.0**17 / bound
    total_ref[...] = jnp.zeros_like(total_ref)
    column = lax.broadcasted_iota(jnp.int32, (256, BLOCK), 0).astype(jnp.float32).astype(jnp.bfloat16)
    one, none = jnp.bfloat16(1), jnp.bfloat16(0)
    z_cell = lax.broadcasted_iota(jnp.int32, (DEPTH, BLOCK), 0).astype(jnp.float32)
    rest = rest_ref[...].astype(FINE)

    def body(step):
        first = step * group
        hot, weight_z, coef = [], [], []
        for g in range(group):
            slot = first + g
            q = lambda k: table_ref[slot, k : k + 1, :]
            hot.append(jnp.where(column == q(0).astype(jnp.bfloat16), one, none))
            gap = z_cell - q(5)
            sine, cosine = q(6), q(7)
            weight_z.append(
                jnp.where(
                    gap == -1.0,
                    0.25 - 0.25 * sine,
                    jnp.where(
                        gap == 0.0,
                        0.25 + 0.25 * cosine,
                        jnp.where(gap == 1.0, 0.25 + 0.25 * sine, jnp.where(gap == 2.0, 0.25 - 0.25 * cosine, 0.0)),
                    ),
                )
            )
            by, bx = (None, q(1), q(2)), (None, q(3), q(4))
            coef.append(
                [
                    [by[i] if bx[k] is None else bx[k] if by[i] is None else by[i] * bx[k] for k in range(3)]
                    for i in range(3)
                ]
            )
        coarse = jnp.concatenate(hot, axis=1)
        fine = coarse.astype(FINE)
        across = jnp.dot(matrix_ref[...], coarse, preferred_element_type=jnp.float32)
        across += jnp.dot(rest, fine, preferred_element_type=jnp.float32)
        spread_high, spread_low = [], []
        for g in range(group):
            slot = first + g
            columns = slice(g * BLOCK, (g + 1) * BLOCK)
            pieces = []
            for c in range(3):
                sums = None
                for yf in range(3):
                    for xf in range(3):
                        row = ((c * 3 + yf) * 3 + xf) * DEPTH
                        term = across[row : row + DEPTH, columns]
                        factor = coef[g][yf][xf]
                        term = term if factor is None else term * factor
                        sums = term if sums is None else sums + term
                speed = jnp.sum(sums * weight_z[g], axis=0, keepdims=True) * unscale
                speed_ref[slot, c : c + 1, :] = speed
                push = (table_ref[slot, 8 + c : 9 + c, :] - feedback_gain * speed) * table_ref[slot, 11:12, :] * scale
                for yf in range(3):
                    for xf in range(3):
                        factor = coef[g][yf][xf]
                        pieces.append(weight_z[g] * (push if factor is None else push * factor))
            piece = jnp.concatenate(pieces, axis=0)
            high = piece.astype(jnp.bfloat16)
            spread_high.append(high)
            spread_low.append((piece - high.astype(jnp.float32)).astype(FINE))
        across_rows = (((1,), (1,)), ((), ()))
        total_ref[...] += lax.dot_general(
            jnp.concatenate(spread_high, axis=1), coarse, across_rows, preferred_element_type=jnp.float32
        ) + lax.dot_general(
            jnp.concatenate(spread_low, axis=1), fine, across_rows, preferred_element_type=jnp.float32
        )

    for step in range(slots // group):
        body(step)
    return bound * 2.0**-21


def finish_force(unscale, total_ref, halo_ref, force_ref, force_edge_ref, start=0):
    lane = lax.broadcasted_iota(jnp.int32, (DEPTH, 128), 1)
    zero = jnp.zeros((DEPTH, 128), jnp.float32)
    for c in range(3):
        by_basis = []
        for xf in range(3):
            field = []
            for yf in range(3):
                row = ((c * 3 + yf) * 3 + xf) * DEPTH
                field.append([total_ref[row : row + DEPTH, 0:128], total_ref[row : row + DEPTH, 128:256]])
            cells = [basis_cells([field[yf][half] for yf in range(3)]) for half in range(2)]
            sums = None
            for k, shift in enumerate((1, 0, -1, -2)):
                tiles = shifted([zero, zero, cells[0][k], cells[1][k], zero, zero], shift)
                sums = tiles if sums is None else [a + b for a, b in zip(sums, tiles)]
            by_basis.append(sums)
        by_x = [basis_cells([by_basis[xf][t] * unscale for xf in range(3)]) for t in range(4)]
        for x in range(4):
            left, low, high, right = (by_x[t][x] for t in range(4))
            force_ref[c, pl.ds(x, DEPTH, stride=8), :] = low
            force_ref[c, pl.ds(4 + x, DEPTH, stride=8), :] = high
            halo_ref[c, pl.ds(4 + x, DEPTH, stride=8), :] = jnp.where(lane >= 64, left, low)
            halo_ref[c, pl.ds(x, DEPTH, stride=8), :] = jnp.where(lane >= 64, high, right)
        row = start + 8 * c
        force_edge_ref[row : row + 8, :] = pack_edges(lambda z: halo_ref[c, 8 * z : 8 * z + 8, :])


def flow_slices(load, flow_ref):
    for z in range(DEPTH):
        total, momentum, dens = moments(load(z))
        inverse = 1.0 / dens
        for c in range(3):
            flow_ref[c, 8 * z : 8 * z + 8, :] = momentum[c] * inverse


def edge_flow(edges):
    total, momentum, dens = moments(edges)
    inverse = 1.0 / dens
    return [momentum[c] * inverse for c in range(3)]


def flow_edges(flows, halo_ref):
    for c in range(3):
        flow = flows[c]
        for z in range(DEPTH):
            halo_ref[c, 8 * z : 8 * z + 8, :] = turn(flow, -(5 * z + 2), 1)


def gather_markers(span_y, slots, filaments, share, spans_ref, where_ref, stiff_ref, part_refs, places_ref, picked_ref, table_ref):
    columns = len(part_refs)
    blocks = share * columns
    block, lane = iotas((blocks, BLOCK))
    anchor = (where_ref[0] * 4).astype(jnp.float32)
    mine = where_ref[1]
    tile_start = (mine * 256).astype(jnp.float32)
    for s in range(columns):
        source = lax.rem(mine + (columns - s), columns)
        for f in range(filaments):
            for k in range(share):
                index = f * blocks + source * share + k
                span = (spans_ref[index] * 256).astype(jnp.float32)
                row = lambda c: part_refs[s][(c * share + k) * filaments + f][None, :]
                start = pl.multiple_of(index * 8, 8)
                three = [anchor + 1.0 + row(0) * (4 - 3.01), span + row(1) * 256.0, 1.0 + row(2) * (DEPTH - 3.01)]
                places_ref[pl.ds(start, 8), :] = jnp.concatenate(three + [jnp.zeros((5, BLOCK), jnp.float32)], axis=0)
    for f in range(filaments):
        factor = stiff_ref[f].astype(jnp.float32) * (1.0 / 256.0)
        start = f * blocks * 8
        places = [places_ref[pl.ds(start + c, blocks, stride=8), :] for c in range(3)]
        for c in range(3):
            ahead = turn(places[c], -1, 1)
            ahead = jnp.where(lane == BLOCK - 1, turn(ahead, -1, 0), ahead) - places[c]
            if c == 1:
                half = 0.5 * span_y
                ahead = jnp.where(ahead > half, ahead - span_y, jnp.where(ahead < -half, ahead + span_y, ahead))
            ahead = jnp.where((lane == BLOCK - 1) & (block == blocks - 1), 0.0, ahead)
            behind = turn(ahead, 1, 1)
            behind = jnp.where(lane == 0, turn(behind, 1, 0), behind)
            places_ref[pl.ds(start + 3 + c, blocks, stride=8), :] = (ahead - behind) * factor
        places_ref[pl.ds(start, blocks, stride=8), :] = places[0] - anchor
        places_ref[pl.ds(start + 1, blocks, stride=8), :] = places[1] - tile_start
    picked_ref[...] = jnp.zeros_like(picked_ref)

    def pick(index, count):
        source = pl.multiple_of(index * 8, 8)
        target = pl.multiple_of(count * 8, 8)
        picked_ref[pl.ds(target, 8), :] = places_ref[pl.ds(source, 8), :]
        return count + (spans_ref[index] == mine).astype(jnp.int32)

    count = lax.fori_loop(0, filaments * blocks, pick, jnp.int32(0), unroll=8)
    got = lambda k: picked_ref[pl.ds(k, slots, stride=8), :]
    slot, _ = iotas((slots, BLOCK))

    def put(k, value):
        table_ref[:, k, :] = value

    def basis(t):
        return jnp.cos((0.5 * math.pi) * (1.0 - t)), jnp.cos((0.5 * math.pi) * t)

    y = got(1)
    base = jnp.minimum(jnp.floor(y), 255.0)
    put(0, base)
    sine, cosine = basis(y - base)
    put(1, sine)
    put(2, cosine)
    sine, cosine = basis(got(0) - 1.0)
    put(3, sine)
    put(4, cosine)
    z = got(2)
    base = jnp.floor(z)
    put(5, base)
    sine, cosine = basis(z - base)
    put(6, sine)
    put(7, cosine)
    bends = [got(3 + c) for c in range(3)]
    for c in range(3):
        put(8 + c, bends[c])
    put(11, jnp.where(slot < count, 1.0, 0.0))
    top = largest(jnp.maximum(jnp.maximum(jnp.abs(bends[0]), jnp.abs(bends[1])), jnp.abs(bends[2])))
    table_ref[0, 12:13, :] = jnp.broadcast_to(top, (1, BLOCK))


def first_kernel(span_y, slots, filaments, columns, spans_ref, where_ref, stiff_ref, flow_ref, right_edge_ref, left_edge_ref, *refs):
    part_refs, refs = refs[:columns], refs[columns:]
    force_ref, to_right_ref, to_left_ref, table_ref = refs[:4]
    halo_ref, matrix_ref, rest_ref, total_ref, speed_ref, places_ref, picked_ref = refs[4:]
    share = spans_ref.shape[0] // (filaments * columns)
    to_right_ref[0:EDGE_ROWS, :] = right_edge_ref[...]
    to_left_ref[0:EDGE_ROWS, :] = left_edge_ref[...]
    gather_markers(
        span_y, slots, filaments, share, spans_ref, where_ref, stiff_ref, part_refs, places_ref, picked_ref, table_ref
    )
    flows = []
    for c in range(3):
        start = 3 * share * filaments + 8 * c
        flows.append(merge_edges(*(part_refs[s][start : start + 8, :] for s in (0, 1, -1))))
    flow_edges(flows, halo_ref)
    top = prepare_matrix(flow_ref, halo_ref, matrix_ref, rest_ref)
    unscale = couple(slots, table_ref, matrix_ref, rest_ref, total_ref, speed_ref, top)
    finish_force(unscale, total_ref, halo_ref, force_ref, to_right_ref, EDGE_ROWS)
    to_left_ref[EDGE_ROWS:, :] = to_right_ref[EDGE_ROWS:, :]


def collide_kernel(first, *refs):
    dev_refs, (force_ref, post_ref, east_ref, west_ref) = refs[:-4], refs[-4:]

    def dev(e, part):
        if first:
            return dev_refs[0][e, part, :]
        for ref, entries in zip(dev_refs, (STILL, EAST, WEST)):
            if e in entries:
                return ref[entries.index(e), part, :]

    for z in range(DEPTH):
        part = slice(8 * z, 8 * z + 8)
        post = collide([dev(e, part) for e in range(19)], [force_ref[c, part, :] for c in range(3)])
        for e in range(19):
            post_ref[e, part, :] = post[e]
    for k in range(5):
        east_ref[32 * k : 32 * k + 32, :] = post_ref[EAST[k], pl.ds(3, 32, stride=4), :]
        west_ref[32 * k : 32 * k + 32, :] = post_ref[WEST[k], pl.ds(0, 32, stride=4), :]


def collide_edge_kernel(first, edge_ref, own_ref, left_ref, right_ref, to_east_ref, to_west_ref, post_edge_ref, east_ref, west_ref):
    row, _ = iotas()
    start = EDGE_ROWS if first else 0
    edges = []
    for e in range(19):
        value = edge_ref[e]
        if first:
            part, shift = slice(8 * (e // 2), 8 * (e // 2) + 8), 4 * (e % 2)
            value = merge_edges(value, turn(left_ref[part, :], shift, 0), turn(right_ref[part, :], shift, 0))
        edges.append(value)
    force = []
    for c in range(3):
        part = slice(start + 8 * c, start + 8 * c + 8)
        force.append(own_ref[part, :] + jnp.where(row >= 4, turn(left_ref[part, :], 4, 0), turn(right_ref[part, :], 4, 0)))
    post = collide(edges, force)
    for e in range(19):
        post_edge_ref[e] = post[e]
    east_ref[0:PLANE, :] = to_east_ref[...]
    west_ref[0:PLANE, :] = to_west_ref[...]
    for k in range(5):
        line = PLANE + 2 * k
        for half in range(2):
            at = 4 * half
            east_ref[line + half : line + half + 1, :] = post[EAST[k]][at + 3 : at + 4, :]
            west_ref[line + half : line + half + 1, :] = post[WEST[k]][at : at + 1, :]
    zero = jnp.zeros((PLANE_ROWS - PLANE - 10, 128), jnp.float32)
    east_ref[PLANE + 10 :, :] = zero
    west_ref[PLANE + 10 :, :] = zero


def stream(entries, post_ref, post_edge_ref, plane_ref, moved_ref, store, store_edge):
    row, lane = iotas()
    low, high = row < 4, row >= 4
    same = (low & (lane < 2)) | (high & (lane == 127))
    patches = {0: same, 1: low & (lane < 3), -1: (low & (lane == 0)) | (high & (lane >= 126))}
    low_wall, high_wall = lane < 5, lane >= 75
    for e in entries:
        cx, cy, cz = velocity_set[e]
        edge = post_edge_ref[e]
        if cx != 0:
            k = (EAST if cx == 1 else WEST).index(e)
            line = PLANE + 2 * k
            beside = jnp.where(low, plane_ref[line : line + 1, :], plane_ref[line + 1 : line + 2, :])
            edge = jnp.where(row % 4 == (0 if cx == 1 else 3), beside, turn(edge, cx, 0))
        edge = turn(edge, cy + 5 * cz, 1)
        if cz == 1:
            edge = jnp.where(low_wall, post_edge_ref[opposite(e)], edge)
        elif cz == -1:
            edge = jnp.where(high_wall, post_edge_ref[opposite(e)], edge)
        store_edge(e, edge)
        if cx != 0:
            for z in range(DEPTH):
                moved_ref[k, 8 * z : 8 * z + 8, :] = turn(post_ref[e, 8 * z : 8 * z + 8, :], cx, 0)
            moved_ref[k, pl.ds(0 if cx == 1 else 3, 32, stride=4), :] = plane_ref[32 * k : 32 * k + 32, :]
        swapped = turn(edge, 4, 0)
        for z in range(DEPTH):
            source, patch = z - cz, patches[cy]
            if 0 <= source < DEPTH:
                part = slice(8 * source, 8 * source + 8)
                value = post_ref[e, part, :] if cx == 0 else moved_ref[k, part, :]
                if cy != 0:
                    value = turn(value, cy, 1)
                    value = jnp.where(lane == (0 if cy == 1 else 127), turn(value, 4, 0), value)
            else:
                value, patch = post_ref[opposite(e), 8 * z : 8 * z + 8, :], same
            store(e, z, jnp.where(patch, turn(swapped, -(5 * z + 2), 1), value))


def stream_kernel(entries, post_ref, post_edge_ref, *refs):
    plane_ref, refs = (None, refs) if entries is STILL else (refs[0], refs[1:])
    dev_ref, edges_ref = refs[:2]
    moved_ref = None if entries is STILL else refs[2]

    def store(e, z, value):
        dev_ref[entries.index(e), 8 * z : 8 * z + 8, :] = value

    def store_edge(e, value):
        edges_ref[entries.index(e)] = value

    stream(entries, post_ref, post_edge_ref, plane_ref, moved_ref, store, store_edge)


def second_kernel(
    slots, blocks, columns, spans_ref, where_ref,
    post_ref, post_edge_ref, still_ref, still_edge_ref, east_dev_ref, east_edge_ref, west_ref, table_ref, *refs
):
    dev_ref, edges_ref, force_ref, to_right_ref, to_left_ref = refs[:5]
    share_refs, refs = refs[5 : 3 + columns], refs[3 + columns :]
    moved_ref, flow_ref, halo_ref, matrix_ref, rest_ref, total_ref, speed_ref, spot_ref = refs

    def store(e, z, value):
        dev_ref[WEST.index(e), 8 * z : 8 * z + 8, :] = value

    def store_edge(e, value):
        edges_ref[e] = value

    def dev(e, z):
        part = slice(8 * z, 8 * z + 8)
        for ref, entries in ((still_ref, STILL), (east_dev_ref, EAST), (dev_ref, WEST)):
            if e in entries:
                return ref[entries.index(e), part, :]

    stream(WEST, post_ref, post_edge_ref, west_ref, moved_ref, store, store_edge)
    for k, e in enumerate(EAST):
        edges_ref[e] = east_edge_ref[k]
    for k, e in enumerate(STILL):
        edges_ref[e] = still_edge_ref[k]
    flow_slices(lambda z: [dev(e, z) for e in range(19)], flow_ref)
    flow_edges(edge_flow([edges_ref[e] for e in range(19)]), halo_ref)
    top = prepare_matrix(flow_ref, halo_ref, matrix_ref, rest_ref)
    speed_ref[...] = jnp.zeros_like(speed_ref)
    unscale = couple(slots, table_ref, matrix_ref, rest_ref, total_ref, speed_ref, top)
    finish_force(unscale, total_ref, halo_ref, force_ref, to_right_ref)
    to_left_ref[0:24, :] = to_right_ref[0:24, :]
    mine = where_ref[1]

    def place(index, count):
        here = spans_ref[index] == mine
        spot_ref[index] = jnp.where(here, speed_ref[jnp.minimum(count, slots - 1)], 0.0)
        return count + here.astype(jnp.int32)

    total = spans_ref.shape[0]
    lax.fori_loop(0, total, place, jnp.int32(0), unroll=8)
    filaments = total // blocks
    share = blocks // columns
    others = iter(share_refs)
    for s in range(columns):
        target, start = (to_right_ref, 24) if s == 1 else (to_left_ref, 24) if s == columns - 1 else (next(others), 0)
        owner = lax.rem(mine + s, columns)
        for f in range(filaments):
            for k in range(share):
                for c in range(3):
                    row = start + (c * share + k) * filaments + f
                    target[row : row + 1, :] = spot_ref[f * blocks + owner * share + k, c : c + 1, :]


def last_kernel(entries, post_ref, post_edge_ref, *refs):
    planes = refs[:2]
    refs = refs if entries is STILL else refs[3:]
    dev_ref, kept_ref, sems = refs[:3]
    moved_ref = None if entries is STILL else refs[3]

    def store(e, z, value):
        kept_ref[entries.index(e), 8 * z : 8 * z + 8, :] = value

    copies = []
    for k, e in enumerate(entries):
        plane_ref = planes[0 if e in EAST else 1]
        stream((e,), post_ref, post_edge_ref, plane_ref, moved_ref, store, lambda e, value: None)
        copies.append(pltpu.make_async_copy(kept_ref.at[k], dev_ref.at[e], sems.at[k]))
        copies[-1].start()
    for copy in copies:
        copy.wait()


def call(body, outs, scratch, n_smem, args, flops=0, **extra):
    spec = [pl.BlockSpec(memory_space=pltpu.SMEM)] * n_smem
    spec += [pl.BlockSpec(memory_space=pltpu.VMEM)] * (len(args) - n_smem)
    moved = 4 * sum(math.prod(shape) for shape in outs)
    options = dict(
        in_specs=spec,
        out_specs=[pl.BlockSpec(memory_space=pltpu.VMEM)] * len(outs),
        cost_estimate=pl.CostEstimate(flops=flops, bytes_accessed=2 * moved, transcendentals=0),
    )
    options.update(extra)
    return pl.pallas_call(
        body,
        out_shape=[jax.ShapeDtypeStruct(shape, jnp.float32) for shape in outs],
        scratch_shapes=scratch,
        compiler_params=pltpu.CompilerParams(vmem_limit_bytes=VMEM_LIMIT),
        **options,
    )(*args)


def ring(value, axis, step):
    count = lax.axis_size(axis)
    return lax.ppermute(value, axis, [(i, (i + step) % count) for i in range(count)])


def per_device(populations, fraction, spans, stiffness):
    depth, tile_x, tile_y = populations.shape[1:]
    columns = lax.axis_size("gy")
    span_y = float(tile_y * columns)
    filaments, _, share = fraction.shape
    blocks = spans.shape[1]
    share_blocks = share // BLOCK
    slots = max(8, 2 * filaments * blocks // columns)
    f32 = jnp.float32

    own_part = fraction.reshape(filaments, 3, share_blocks, BLOCK).transpose(1, 2, 0, 3)
    own_part = own_part.reshape(3 * share_blocks * filaments, BLOCK)

    field = (19, ROWS, 128)
    edge = (19, 8, 128)
    halves = tile_y // 128
    pop = populations.reshape(19, depth, tile_x, halves, 128).transpose(0, 1, 3, 2, 4).reshape(field)
    flat_spans = spans.reshape(-1)
    where = jnp.stack([lax.axis_index("gx"), lax.axis_index("gy")]).astype(jnp.int32)

    force_shape = (3, ROWS, 128)
    share_rows = 3 * share_blocks * filaments
    inside, anywhere = pl.BlockSpec(memory_space=pltpu.VMEM), pl.BlockSpec(memory_space=pl.ANY)
    flow, payload = call(
        flow_kernel, [force_shape, (share_rows + 24, BLOCK)], [pltpu.SemaphoreType.DMA], 0, (pop, own_part),
        in_specs=[inside, anywhere],
    )
    parts = [payload] + [ring(payload, "gy", s) for s in range(1, columns)]
    own_edge, right_edge, left_edge = call(edge_kernel, [edge, (EDGE_ROWS, 128), (EDGE_ROWS, 128)], [], 0, (pop,))

    table_shape = (slots, 16, BLOCK)
    coupling = [
        pltpu.VMEM(force_shape, f32),
        pltpu.VMEM((3 * FIELDS * DEPTH, 256), jnp.bfloat16),
        pltpu.VMEM((3 * FIELDS * DEPTH, 256), f32),
        pltpu.VMEM((3 * FIELDS * DEPTH, 256), f32),
        pltpu.VMEM((slots, 8, BLOCK), f32),
    ]
    force, to_right, to_left, table = call(
        functools.partial(first_kernel, span_y, slots, filaments, columns),
        [force_shape, (EDGE_ROWS + 24, 128), (EDGE_ROWS + 24, 128), table_shape],
        coupling + [pltpu.VMEM((filaments * blocks * 8, BLOCK), f32), pltpu.VMEM(((slots + 1) * 8, BLOCK), f32)],
        3,
        (flat_spans, where, stiffness, flow, right_edge, left_edge, *parts),
    )

    moved = pltpu.VMEM((5, ROWS, 128), f32)
    side = (5, ROWS, 128)

    def collision(first, dev, edges, force, to_right, to_left):
        left, right = ring(to_right, "gy", 1), ring(to_left, "gy", -1)
        post, east, west = call(
            functools.partial(collide_kernel, first), [field, (PLANE, 128), (PLANE, 128)], [], 0, (*dev, force)
        )
        post_edge, east, west = call(
            functools.partial(collide_edge_kernel, first), [edge, (PLANE_ROWS, 128), (PLANE_ROWS, 128)], [], 0,
            (edges, to_right, left, right, east, west),
        )
        return post, post_edge, ring(east, "gx", 1), ring(west, "gx", -1), left, right

    post, post_edge, east, west, _, _ = collision(True, (pop,), own_edge, force, to_right, to_left)
    still, still_edge = call(
        functools.partial(stream_kernel, STILL), [(9, ROWS, 128), (9, 8, 128)], [], 0, (post, post_edge)
    )
    east_dev, east_edge = call(
        functools.partial(stream_kernel, EAST), [side, (5, 8, 128)], [moved], 0, (post, post_edge, east)
    )
    dev, edges, force, to_right, to_left, *chunks = call(
        functools.partial(second_kernel, slots, blocks, columns),
        [side, edge, force_shape] + [(24 + share_rows, BLOCK)] * 2 + [(share_rows, BLOCK)] * (columns - 2),
        [moved, pltpu.VMEM(force_shape, f32)] + coupling + [pltpu.VMEM((filaments * blocks, 8, BLOCK), f32)],
        2,
        (flat_spans, where, post, post_edge, still, still_edge, east_dev, east_edge, west, table),
    )
    post, post_edge, east, west, left, right = collision(
        False, (still, east_dev, dev), edges, force, to_right, to_left
    )
    speed = chunks[0] + left[24:] + right[24:]
    for s in range(2, columns - 1):
        speed = speed + ring(chunks[s - 1], "gy", s)
    speed = speed.reshape(3, share_blocks, filaments, BLOCK).transpose(2, 0, 1, 3).reshape(fraction.shape)

    dev = None
    for entries in (STILL, EAST + WEST):
        count = len(entries)
        scratch = [pltpu.VMEM((count, ROWS, 128), f32), pltpu.SemaphoreType.DMA((count,))]
        extra, args = {}, (post, post_edge)
        if entries is not STILL:
            scratch, args = scratch + [moved], args + (east, west, dev)
            extra = dict(in_specs=[inside] * 4 + [anywhere], input_output_aliases={4: 0})
        (dev,) = call(functools.partial(last_kernel, entries), [field], scratch, 0, args, out_specs=[anywhere], **extra)
    dev = dev.reshape(19, depth, halves, tile_x, 128).transpose(0, 1, 3, 2, 4).reshape(populations.shape)
    return dev, speed


def solution(mesh):
    placed = (P(None, None, "gx", "gy"), P("gx", None, "gy"), P("gx", None, None), P("gx"))
    return jax.shard_map(
        per_device,
        mesh=mesh,
        in_specs=placed,
        out_specs=(P(None, None, "gx", "gy"), P("gx", None, "gy")),
        check_vma=False,
    )
```

```python
import functools
import math

import jax
import jax.numpy as jnp
from jax import lax
from jax.experimental import pallas as pl
from jax.experimental.pallas import tpu as pltpu
from jax.sharding import PartitionSpec as P

STEPS = 2

velocity_set = (
    (0, 0, 0),
    (1, 0, 0),
    (-1, 0, 0),
    (0, 1, 0),
    (0, -1, 0),
    (0, 0, 1),
    (0, 0, -1),
    (1, 1, 0),
    (-1, -1, 0),
    (1, -1, 0),
    (-1, 1, 0),
    (1, 0, 1),
    (-1, 0, -1),
    (1, 0, -1),
    (-1, 0, 1),
    (0, 1, 1),
    (0, -1, -1),
    (0, 1, -1),
    (0, -1, 1),
)
lattice_weight = (1.0 / 3.0,) + (1.0 / 18.0,) * 6 + (1.0 / 36.0,) * 12
unit = 0.002
feedback_gain = 2.0
EAST = tuple(i for i in range(19) if velocity_set[i][0] == 1)
WEST = tuple(i for i in range(19) if velocity_set[i][0] == -1)
STILL = tuple(i for i in range(19) if velocity_set[i][0] == 0)
MOVING = EAST + WEST

DEPTH = 16
ROWS = DEPTH * 8
BLOCK = 128
GROUP = 32
PLANE = 160
PLANE_ROWS = 176
FIELDS = 9
EDGE_ROWS = 80
TINY = 1e-30
FINE = jnp.float8_e4m3fn
VMEM_LIMIT = 40 * 1024 * 1024


def opposite(entry):
    return entry + 1 if entry % 2 == 1 else entry - 1


def iotas(shape=(8, 128)):
    return lax.broadcasted_iota(jnp.int32, shape, 0), lax.broadcasted_iota(jnp.int32, shape, 1)


def turn(value, shift, axis):
    shift = shift % value.shape[axis]
    return pltpu.roll(value, shift, axis) if shift else value


def pack_edges(slices):
    _, lane = iotas()
    total = jnp.zeros((8, 128), jnp.float32)
    for z in range(DEPTH):
        total = jnp.where((lane >= 5 * z) & (lane < 5 * z + 5), turn(slices(z), 5 * z + 2, 1), total)
    return total


def signed_sum(terms):
    total = None
    for sign, value in terms:
        if total is None:
            total = value if sign > 0 else -value
        else:
            total = total + value if sign > 0 else total - value
    return total


def dot_c(vector, parts):
    return signed_sum([(vector[a], parts[a]) for a in range(3) if vector[a] != 0])


def moments(dev):
    total = dev[0]
    for entry in range(1, 19):
        total = total + dev[entry]
    momentum = [
        signed_sum([(velocity_set[e][a], dev[e]) for e in range(19) if velocity_set[e][a] != 0]) for a in range(3)
    ]
    return total, momentum, 1.0 + unit * total


def collide(dev, force):
    total, momentum, dens = moments(dev)
    inverse = 1.0 / dens
    vel = [(momentum[a] + 0.5 * force[a]) * inverse for a in range(3)]
    odd_base = [3.75 * momentum[a] + 3.0 * force[a] for a in range(3)]
    even_base = [5.625 * momentum[a] + 6.1875 * force[a] for a in range(3)]
    along = vel[0] * even_base[0] + vel[1] * even_base[1] + vel[2] * even_base[2]
    base = 1.25 * total - (unit / 3.0) * along
    post = [lattice_weight[0] * base - 0.25 * dev[0]]
    scaled = [unit * vel[a] for a in range(3)]
    for entry in range(1, 19, 2):
        vector, weight = velocity_set[entry], lattice_weight[entry]
        odd = weight * dot_c(vector, odd_base)
        even = weight * (base + dot_c(vector, scaled) * dot_c(vector, even_base))
        post.append((even + odd) - 0.25 * dev[entry])
        post.append((even - odd) - 0.25 * dev[entry + 1])
    return post


def merge_edges(own, left, right):
    row, lane = iotas()
    j = lane % 5
    from_left = (row >= 4) & (j < 2)
    from_right = (row < 4) & (j >= 2)
    return jnp.where(from_left, left, jnp.where(from_right, right, turn(own, 4, 0)))


def flow_kernel(pop_ref, part_ref, flow_ref, payload_ref, sem):
    rows = part_ref.shape[0]
    copy = pltpu.make_async_copy(part_ref, payload_ref.at[pl.ds(0, rows)], sem)
    copy.start()
    flow_slices(lambda z: [pop_ref[e, 8 * z : 8 * z + 8, :] for e in range(19)], flow_ref)
    for c in range(3):
        payload_ref[rows + 8 * c : rows + 8 * c + 8, :] = pack_edges(lambda z: flow_ref[c, 8 * z : 8 * z + 8, :])
    copy.wait()


def edge_kernel(spans_ref, where_ref, pop_ref, edge_ref, to_right_ref, to_left_ref, chosen_ref):
    row, _ = iotas()
    filaments, _, blocks = spans_ref.shape
    slots, mine = chosen_ref.shape[0] - 8, where_ref[1]
    count = jnp.int32(0)
    for f in range(filaments):
        for k in range(blocks):
            chosen_ref[count] = f * blocks + k
            count = count + (spans_ref[f, 0, k] == mine).astype(jnp.int32)
    for n in range(slots):
        chosen_ref[n] = jnp.where(n < count, chosen_ref[n], filaments * blocks)
    chosen_ref[slots] = count
    edges = []
    for e in range(19):
        edges.append(pack_edges(lambda z: pop_ref[e, 8 * z : 8 * z + 8, :]))
        edge_ref[e] = edges[e]
    for k in range(10):
        other = turn(edges[2 * k + 1], 4, 0) if k < 9 else edges[2 * k]
        to_right_ref[8 * k : 8 * k + 8, :] = jnp.where(row >= 4, edges[2 * k], other)
        to_left_ref[8 * k : 8 * k + 8, :] = jnp.where(row < 4, edges[2 * k], other)


def shifted(tiles, shift):
    lane = lax.broadcasted_iota(jnp.int32, tiles[0].shape, 1)
    if shift == 0:
        return tiles[1:-1]
    rolled = [turn(tile, -shift, 1) for tile in tiles]
    if shift > 0:
        return [jnp.where(lane >= 128 - shift, rolled[i + 1], rolled[i]) for i in range(1, len(tiles) - 1)]
    return [jnp.where(lane < -shift, rolled[i - 1], rolled[i]) for i in range(1, len(tiles) - 1)]


def basis_fields(four):
    return (
        0.25 * ((four[0] + four[2]) + (four[1] + four[3])),
        0.25 * (four[2] - four[0]),
        0.25 * (four[1] - four[3]),
    )


def basis_cells(three):
    one, sine, cosine = three
    return one - sine, one + cosine, one + sine, one - cosine


def largest(value):
    return jnp.max(jnp.max(jnp.abs(value), axis=1, keepdims=True), axis=0, keepdims=True)


def prepare_matrix(flow_ref, halo_ref, matrix_ref, rest_ref):
    top = None
    for c in range(3):
        for z in range(DEPTH):
            part = slice(8 * z, 8 * z + 8)
            both = jnp.maximum(jnp.abs(flow_ref[c, part, :]), jnp.abs(halo_ref[c, part, :]))
            top = both if top is None else jnp.maximum(top, both)
    top = jnp.maximum(largest(top), TINY)
    scale = 2.0**15 / top
    for c in range(3):
        per_x = []
        for x in range(4):
            tiles = [
                halo_ref[c, pl.ds(4 + x, DEPTH, stride=8), :],
                flow_ref[c, pl.ds(x, DEPTH, stride=8), :],
                flow_ref[c, pl.ds(4 + x, DEPTH, stride=8), :],
                halo_ref[c, pl.ds(x, DEPTH, stride=8), :],
            ]
            per_x.append(tiles)
        by_basis = [basis_fields([per_x[x][t] for x in range(4)]) for t in range(4)]
        for xf in range(3):
            tiles = [by_basis[t][xf] for t in range(4)]
            four = [shifted(tiles, s) for s in (-1, 0, 1, 2)]
            for half in range(2):
                fields = basis_fields([four[s][half] for s in range(4)])
                columns = slice(half * 128, half * 128 + 128)
                for yf in range(3):
                    row = ((c * 3 + yf) * 3 + xf) * DEPTH
                    value = fields[yf] * scale
                    high = value.astype(jnp.bfloat16)
                    matrix_ref[row : row + DEPTH, columns] = high
                    rest_ref[row : row + DEPTH, columns] = value - high.astype(jnp.float32)
    return top


def couple(slots, table_ref, matrix_ref, rest_ref, total_ref, speed_ref, top):
    group = min(GROUP, slots)
    unscale = top * 2.0**-15
    bound = jnp.maximum(table_ref[0, 12:13, 0:1] + feedback_gain * top, TINY)
    scale = 2.0**17 / bound
    total_ref[...] = jnp.zeros_like(total_ref)
    column = lax.broadcasted_iota(jnp.int32, (256, BLOCK), 0).astype(jnp.float32).astype(jnp.bfloat16)
    one, none = jnp.bfloat16(1), jnp.bfloat16(0)
    z_cell = lax.broadcasted_iota(jnp.int32, (DEPTH, BLOCK), 0).astype(jnp.float32)
    rest = rest_ref[...].astype(FINE)

    def body(step):
        first = step * group
        hot, weight_z, coef = [], [], []
        for g in range(group):
            slot = first + g
            q = lambda k: table_ref[slot, k : k + 1, :]
            hot.append(jnp.where(column == q(0).astype(jnp.bfloat16), one, none))
            gap = z_cell - q(5)
            sine, cosine = q(6), q(7)
            weight_z.append(
                jnp.where(
                    gap == -1.0,
                    0.25 - 0.25 * sine,
                    jnp.where(
                        gap == 0.0,
                        0.25 + 0.25 * cosine,
                        jnp.where(gap == 1.0, 0.25 + 0.25 * sine, jnp.where(gap == 2.0, 0.25 - 0.25 * cosine, 0.0)),
                    ),
                )
            )
            by, bx = (None, q(1), q(2)), (None, q(3), q(4))
            coef.append(
                [
                    [by[i] if bx[k] is None else bx[k] if by[i] is None else by[i] * bx[k] for k in range(3)]
                    for i in range(3)
                ]
            )
        coarse = jnp.concatenate(hot, axis=1)
        fine = coarse.astype(FINE)
        across = jnp.dot(matrix_ref[...], coarse, preferred_element_type=jnp.float32)
        across += jnp.dot(rest, fine, preferred_element_type=jnp.float32)
        spread_high, spread_low = [], []
        for g in range(group):
            slot = first + g
            columns = slice(g * BLOCK, (g + 1) * BLOCK)
            pieces = []
            for c in range(3):
                sums = None
                for yf in range(3):
                    for xf in range(3):
                        row = ((c * 3 + yf) * 3 + xf) * DEPTH
                        term = across[row : row + DEPTH, columns]
                        factor = coef[g][yf][xf]
                        term = term if factor is None else term * factor
                        sums = term if sums is None else sums + term
                speed = jnp.sum(sums * weight_z[g], axis=0, keepdims=True) * unscale
                speed_ref[slot, c : c + 1, :] = speed
                push = (table_ref[slot, 8 + c : 9 + c, :] - feedback_gain * speed) * table_ref[slot, 11:12, :] * scale
                for yf in range(3):
                    for xf in range(3):
                        factor = coef[g][yf][xf]
                        pieces.append(weight_z[g] * (push if factor is None else push * factor))
            piece = jnp.concatenate(pieces, axis=0)
            high = piece.astype(jnp.bfloat16)
            spread_high.append(high)
            spread_low.append((piece - high.astype(jnp.float32)).astype(FINE))
        across_rows = (((1,), (1,)), ((), ()))
        total_ref[...] += lax.dot_general(
            jnp.concatenate(spread_high, axis=1), coarse, across_rows, preferred_element_type=jnp.float32
        ) + lax.dot_general(
            jnp.concatenate(spread_low, axis=1), fine, across_rows, preferred_element_type=jnp.float32
        )

    for step in range(slots // group):
        body(step)
    return bound * 2.0**-21


def finish_force(unscale, total_ref, halo_ref, force_ref, force_edge_ref, start=0):
    lane = lax.broadcasted_iota(jnp.int32, (DEPTH, 128), 1)
    zero = jnp.zeros((DEPTH, 128), jnp.float32)
    for c in range(3):
        by_basis = []
        for xf in range(3):
            field = []
            for yf in range(3):
                row = ((c * 3 + yf) * 3 + xf) * DEPTH
                field.append([total_ref[row : row + DEPTH, 0:128], total_ref[row : row + DEPTH, 128:256]])
            cells = [basis_cells([field[yf][half] for yf in range(3)]) for half in range(2)]
            sums = None
            for k, shift in enumerate((1, 0, -1, -2)):
                tiles = shifted([zero, zero, cells[0][k], cells[1][k], zero, zero], shift)
                sums = tiles if sums is None else [a + b for a, b in zip(sums, tiles)]
            by_basis.append(sums)
        by_x = [basis_cells([by_basis[xf][t] * unscale for xf in range(3)]) for t in range(4)]
        for x in range(4):
            left, low, high, right = (by_x[t][x] for t in range(4))
            force_ref[c, pl.ds(x, DEPTH, stride=8), :] = low
            force_ref[c, pl.ds(4 + x, DEPTH, stride=8), :] = high
            halo_ref[c, pl.ds(4 + x, DEPTH, stride=8), :] = jnp.where(lane >= 64, left, low)
            halo_ref[c, pl.ds(x, DEPTH, stride=8), :] = jnp.where(lane >= 64, high, right)
        row = start + 8 * c
        force_edge_ref[row : row + 8, :] = pack_edges(lambda z: halo_ref[c, 8 * z : 8 * z + 8, :])


def flow_slices(load, flow_ref):
    for z in range(DEPTH):
        total, momentum, dens = moments(load(z))
        inverse = 1.0 / dens
        for c in range(3):
            flow_ref[c, 8 * z : 8 * z + 8, :] = momentum[c] * inverse


def edge_flow(edges):
    total, momentum, dens = moments(edges)
    inverse = 1.0 / dens
    return [momentum[c] * inverse for c in range(3)]


def flow_edges(flows, halo_ref):
    for c in range(3):
        flow = flows[c]
        for z in range(DEPTH):
            halo_ref[c, 8 * z : 8 * z + 8, :] = turn(flow, -(5 * z + 2), 1)


def gather_markers(span_y, slots, filaments, share, spans_ref, where_ref, chosen_ref, stiff_ref, part_refs, places_ref, picked_ref, table_ref):
    columns = len(part_refs)
    blocks = share * columns
    block, lane = iotas((blocks, BLOCK))
    anchor = (where_ref[0] * 4).astype(jnp.float32)
    mine = where_ref[1]
    tile_start = (mine * 256).astype(jnp.float32)
    for s in range(columns):
        source = lax.rem(mine + (columns - s), columns)
        for f in range(filaments):
            for k in range(share):
                index = f * blocks + source * share + k
                span = (spans_ref[f, 0, source * share + k] * 256).astype(jnp.float32)
                row = lambda c: part_refs[s][(c * share + k) * filaments + f][None, :]
                start = pl.multiple_of(index * 8, 8)
                three = [anchor + 1.0 + row(0) * (4 - 3.01), span + row(1) * 256.0, 1.0 + row(2) * (DEPTH - 3.01)]
                places_ref[pl.ds(start, 8), :] = jnp.concatenate(three + [jnp.zeros((5, BLOCK), jnp.float32)], axis=0)
    for f in range(filaments):
        factor = stiff_ref[f].astype(jnp.float32) * (1.0 / 256.0)
        start = f * blocks * 8
        places = [places_ref[pl.ds(start + c, blocks, stride=8), :] for c in range(3)]
        for c in range(3):
            ahead = turn(places[c], -1, 1)
            ahead = jnp.where(lane == BLOCK - 1, turn(ahead, -1, 0), ahead) - places[c]
            if c == 1:
                half = 0.5 * span_y
                ahead = jnp.where(ahead > half, ahead - span_y, jnp.where(ahead < -half, ahead + span_y, ahead))
            ahead = jnp.where((lane == BLOCK - 1) & (block == blocks - 1), 0.0, ahead)
            behind = turn(ahead, 1, 1)
            behind = jnp.where(lane == 0, turn(behind, 1, 0), behind)
            places_ref[pl.ds(start + 3 + c, blocks, stride=8), :] = (ahead - behind) * factor
        places_ref[pl.ds(start, blocks, stride=8), :] = places[0] - anchor
        places_ref[pl.ds(start + 1, blocks, stride=8), :] = places[1] - tile_start
    total = filaments * blocks
    places_ref[pl.ds(total * 8, 8), :] = jnp.zeros((8, BLOCK), jnp.float32)
    for n in range(slots):
        picked_ref[8 * n : 8 * n + 8, :] = places_ref[pl.ds(pl.multiple_of(chosen_ref[n] * 8, 8), 8), :]
    count = chosen_ref[slots]
    got = lambda k: picked_ref[pl.ds(k, slots, stride=8), :]
    slot, _ = iotas((slots, BLOCK))

    def put(k, value):
        table_ref[:, k, :] = value

    def basis(t):
        square = t * t
        sine = cosine = None
        for k in range(6, -1, -1):
            a, b = ((-1) ** k * (0.5 * math.pi) ** n / math.factorial(n) for n in (2 * k + 1, 2 * k))
            sine = a if sine is None else sine * square + a
            cosine = b if cosine is None else cosine * square + b
        return sine * t, cosine

    y = got(1)
    base = jnp.minimum(jnp.floor(y), 255.0)
    put(0, base)
    sine, cosine = basis(y - base)
    put(1, sine)
    put(2, cosine)
    sine, cosine = basis(got(0) - 1.0)
    put(3, sine)
    put(4, cosine)
    z = got(2)
    base = jnp.floor(z)
    put(5, base)
    sine, cosine = basis(z - base)
    put(6, sine)
    put(7, cosine)
    bends = [got(3 + c) for c in range(3)]
    for c in range(3):
        put(8 + c, bends[c])
    put(11, jnp.where(slot < count, 1.0, 0.0))
    top = largest(jnp.maximum(jnp.maximum(jnp.abs(bends[0]), jnp.abs(bends[1])), jnp.abs(bends[2])))
    table_ref[0, 12:13, :] = jnp.broadcast_to(top, (1, BLOCK))


def first_kernel(span_y, slots, filaments, columns, spans_ref, where_ref, chosen_ref, stiff_ref, flow_ref, right_edge_ref, left_edge_ref, *refs):
    part_refs, refs = refs[:columns], refs[columns:]
    force_ref, to_right_ref, to_left_ref, table_ref = refs[:4]
    halo_ref, matrix_ref, rest_ref, total_ref, speed_ref, places_ref, picked_ref = refs[4:]
    share = spans_ref.shape[2] // columns
    to_right_ref[0:EDGE_ROWS, :] = right_edge_ref[...]
    to_left_ref[0:EDGE_ROWS, :] = left_edge_ref[...]
    gather_markers(
        span_y, slots, filaments, share, spans_ref, where_ref, chosen_ref, stiff_ref, part_refs, places_ref, picked_ref, table_ref
    )
    flows = []
    for c in range(3):
        start = 3 * share * filaments + 8 * c
        flows.append(merge_edges(*(part_refs[s][start : start + 8, :] for s in (0, 1, -1))))
    flow_edges(flows, halo_ref)
    top = prepare_matrix(flow_ref, halo_ref, matrix_ref, rest_ref)
    unscale = couple(slots, table_ref, matrix_ref, rest_ref, total_ref, speed_ref, top)
    finish_force(unscale, total_ref, halo_ref, force_ref, to_right_ref, EDGE_ROWS)
    to_left_ref[EDGE_ROWS:, :] = to_right_ref[EDGE_ROWS:, :]


def collide_kernel(first, *refs):
    dev_refs, (force_ref, post_ref, east_ref, west_ref) = refs[:-4], refs[-4:]

    def dev(e, part):
        if first:
            return dev_refs[0][e, part, :]
        for ref, entries in zip(dev_refs, (STILL, EAST, WEST)):
            if e in entries:
                return ref[entries.index(e), part, :]

    for z in range(DEPTH):
        part = slice(8 * z, 8 * z + 8)
        post = collide([dev(e, part) for e in range(19)], [force_ref[c, part, :] for c in range(3)])
        for e in range(19):
            post_ref[e, part, :] = post[e]
    for k in range(5):
        east_ref[32 * k : 32 * k + 32, :] = post_ref[EAST[k], pl.ds(3, 32, stride=4), :]
        west_ref[32 * k : 32 * k + 32, :] = post_ref[WEST[k], pl.ds(0, 32, stride=4), :]


def collide_edge_kernel(first, edge_ref, own_ref, left_ref, right_ref, to_east_ref, to_west_ref, post_edge_ref, east_ref, west_ref):
    row, _ = iotas()
    start = EDGE_ROWS if first else 0
    edges = []
    for e in range(19):
        value = edge_ref[e]
        if first:
            part, shift = slice(8 * (e // 2), 8 * (e // 2) + 8), 4 * (e % 2)
            value = merge_edges(value, turn(left_ref[part, :], shift, 0), turn(right_ref[part, :], shift, 0))
        edges.append(value)
    force = []
    for c in range(3):
        part = slice(start + 8 * c, start + 8 * c + 8)
        force.append(own_ref[part, :] + jnp.where(row >= 4, turn(left_ref[part, :], 4, 0), turn(right_ref[part, :], 4, 0)))
    post = collide(edges, force)
    for e in range(19):
        post_edge_ref[e] = post[e]
    east_ref[0:PLANE, :] = to_east_ref[...]
    west_ref[0:PLANE, :] = to_west_ref[...]
    for k in range(5):
        line = PLANE + 2 * k
        for half in range(2):
            at = 4 * half
            east_ref[line + half : line + half + 1, :] = post[EAST[k]][at + 3 : at + 4, :]
            west_ref[line + half : line + half + 1, :] = post[WEST[k]][at : at + 1, :]
    zero = jnp.zeros((PLANE_ROWS - PLANE - 10, 128), jnp.float32)
    east_ref[PLANE + 10 :, :] = zero
    west_ref[PLANE + 10 :, :] = zero


def stream(entries, post_ref, post_edge_ref, plane_ref, moved_ref, store, store_edge):
    row, lane = iotas()
    low, high = row < 4, row >= 4
    same = (low & (lane < 2)) | (high & (lane == 127))
    patches = {0: same, 1: low & (lane < 3), -1: (low & (lane == 0)) | (high & (lane >= 126))}
    low_wall, high_wall = lane < 5, lane >= 75
    for e in entries:
        cx, cy, cz = velocity_set[e]
        edge = post_edge_ref[e]
        if cx != 0:
            k = (EAST if cx == 1 else WEST).index(e)
            line = PLANE + 2 * k
            beside = jnp.where(low, plane_ref[line : line + 1, :], plane_ref[line + 1 : line + 2, :])
            edge = jnp.where(row % 4 == (0 if cx == 1 else 3), beside, turn(edge, cx, 0))
        edge = turn(edge, cy + 5 * cz, 1)
        if cz == 1:
            edge = jnp.where(low_wall, post_edge_ref[opposite(e)], edge)
        elif cz == -1:
            edge = jnp.where(high_wall, post_edge_ref[opposite(e)], edge)
        store_edge(e, edge)
        if cx != 0:
            for z in range(DEPTH):
                moved_ref[k, 8 * z : 8 * z + 8, :] = turn(post_ref[e, 8 * z : 8 * z + 8, :], cx, 0)
            moved_ref[k, pl.ds(0 if cx == 1 else 3, 32, stride=4), :] = plane_ref[32 * k : 32 * k + 32, :]
        swapped = turn(edge, 4, 0)
        for z in range(DEPTH):
            source, patch = z - cz, patches[cy]
            if 0 <= source < DEPTH:
                part = slice(8 * source, 8 * source + 8)
                value = post_ref[e, part, :] if cx == 0 else moved_ref[k, part, :]
                if cy != 0:
                    value = turn(value, cy, 1)
                    value = jnp.where(lane == (0 if cy == 1 else 127), turn(value, 4, 0), value)
            else:
                value, patch = post_ref[opposite(e), 8 * z : 8 * z + 8, :], same
            store(e, z, jnp.where(patch, turn(swapped, -(5 * z + 2), 1), value))


def stream_kernel(entries, post_ref, post_edge_ref, *refs):
    plane_ref, refs = (None, refs) if entries is STILL else (refs[0], refs[1:])
    dev_ref, edges_ref = refs[:2]
    moved_ref = None if entries is STILL else refs[2]

    def store(e, z, value):
        dev_ref[entries.index(e), 8 * z : 8 * z + 8, :] = value

    def store_edge(e, value):
        edges_ref[entries.index(e)] = value

    stream(entries, post_ref, post_edge_ref, plane_ref, moved_ref, store, store_edge)


def second_kernel(
    slots, blocks, columns, where_ref, chosen_ref,
    post_ref, post_edge_ref, still_ref, still_edge_ref, east_dev_ref, east_edge_ref, west_ref, table_ref, *refs
):
    dev_ref, edges_ref, force_ref, to_right_ref, to_left_ref = refs[:5]
    share_refs, refs = refs[5 : 3 + columns], refs[3 + columns :]
    moved_ref, flow_ref, halo_ref, matrix_ref, rest_ref, total_ref, speed_ref, spot_ref = refs

    def store(e, z, value):
        dev_ref[WEST.index(e), 8 * z : 8 * z + 8, :] = value

    def store_edge(e, value):
        edges_ref[e] = value

    def dev(e, z):
        part = slice(8 * z, 8 * z + 8)
        for ref, entries in ((still_ref, STILL), (east_dev_ref, EAST), (dev_ref, WEST)):
            if e in entries:
                return ref[entries.index(e), part, :]

    stream(WEST, post_ref, post_edge_ref, west_ref, moved_ref, store, store_edge)
    for k, e in enumerate(EAST):
        edges_ref[e] = east_edge_ref[k]
    for k, e in enumerate(STILL):
        edges_ref[e] = still_edge_ref[k]
    flow_slices(lambda z: [dev(e, z) for e in range(19)], flow_ref)
    flow_edges(edge_flow([edges_ref[e] for e in range(19)]), halo_ref)
    top = prepare_matrix(flow_ref, halo_ref, matrix_ref, rest_ref)
    unscale = couple(slots, table_ref, matrix_ref, rest_ref, total_ref, speed_ref, top)
    finish_force(unscale, total_ref, halo_ref, force_ref, to_right_ref)
    to_left_ref[0:24, :] = to_right_ref[0:24, :]
    mine = where_ref[1]

    total = spot_ref.shape[0] - 1
    spot_ref[...] = jnp.zeros_like(spot_ref)
    for n in range(slots):
        spot_ref[chosen_ref[n]] = speed_ref[n]
    filaments = total // blocks
    share = blocks // columns
    others = iter(share_refs)
    for s in range(columns):
        target, start = (to_right_ref, 24) if s == 1 else (to_left_ref, 24) if s == columns - 1 else (next(others), 0)
        owner = lax.rem(mine + s, columns)
        for f in range(filaments):
            for k in range(share):
                for c in range(3):
                    row = start + (c * share + k) * filaments + f
                    target[row : row + 1, :] = spot_ref[f * blocks + owner * share + k, c : c + 1, :]


def last_kernel(entries, post_ref, post_edge_ref, *refs):
    planes = refs[:2]
    refs = refs if entries is STILL else refs[3:]
    dev_ref, kept_ref, sems = refs[:3]
    moved_ref = None if entries is STILL else refs[3]

    def store(e, z, value):
        kept_ref[entries.index(e), 8 * z : 8 * z + 8, :] = value

    copies = []
    for k, e in enumerate(entries):
        plane_ref = planes[0 if e in EAST else 1]
        stream((e,), post_ref, post_edge_ref, plane_ref, moved_ref, store, lambda e, value: None)
        copies.append(pltpu.make_async_copy(kept_ref.at[k], dev_ref.at[e], sems.at[k]))
        copies[-1].start()
    for copy in copies:
        copy.wait()


def call(body, outs, scratch, n_smem, args, flops=0, **extra):
    spec = [pl.BlockSpec(memory_space=pltpu.SMEM)] * n_smem
    spec += [pl.BlockSpec(memory_space=pltpu.VMEM)] * (len(args) - n_smem)
    outs = [out if isinstance(out[-1], type) else (out, jnp.float32) for out in outs]
    moved = 4 * sum(math.prod(shape) for shape, _ in outs)
    options = dict(
        in_specs=spec,
        out_specs=[pl.BlockSpec(memory_space=pltpu.VMEM)] * len(outs),
        cost_estimate=pl.CostEstimate(flops=flops, bytes_accessed=2 * moved, transcendentals=0),
    )
    options.update(extra)
    return pl.pallas_call(
        body,
        out_shape=[jax.ShapeDtypeStruct(*out) for out in outs],
        scratch_shapes=scratch,
        compiler_params=pltpu.CompilerParams(vmem_limit_bytes=VMEM_LIMIT),
        **options,
    )(*args)


def ring(value, axis, step):
    count = lax.axis_size(axis)
    return lax.ppermute(value, axis, [(i, (i + step) % count) for i in range(count)])


def per_device(populations, fraction, spans, stiffness):
    depth, tile_x, tile_y = populations.shape[1:]
    columns = lax.axis_size("gy")
    span_y = float(tile_y * columns)
    filaments, _, share = fraction.shape
    blocks = spans.shape[1]
    share_blocks = share // BLOCK
    slots = max(8, 2 * filaments * blocks // columns)
    f32 = jnp.float32

    own_part = fraction.reshape(filaments, 3, share_blocks, BLOCK).transpose(1, 2, 0, 3)
    own_part = own_part.reshape(3 * share_blocks * filaments, BLOCK)

    field = (19, ROWS, 128)
    edge = (19, 8, 128)
    halves = tile_y // 128
    pop = populations.reshape(19, depth, tile_x, halves, 128).transpose(0, 1, 3, 2, 4).reshape(field)
    flat_spans = spans.transpose(0, 2, 1)
    where = jnp.stack([lax.axis_index("gx"), lax.axis_index("gy")]).astype(jnp.int32)

    force_shape = (3, ROWS, 128)
    share_rows = 3 * share_blocks * filaments
    inside, anywhere = pl.BlockSpec(memory_space=pltpu.VMEM), pl.BlockSpec(memory_space=pl.ANY)
    flow, payload = call(
        flow_kernel, [force_shape, (share_rows + 24, BLOCK)], [pltpu.SemaphoreType.DMA], 0, (pop, own_part),
        in_specs=[inside, anywhere],
    )
    parts = [payload] + [ring(payload, "gy", s) for s in range(1, columns)]
    edge_shapes = [edge, (EDGE_ROWS, 128), (EDGE_ROWS, 128)]
    own_edge, right_edge, left_edge, chosen = call(
        edge_kernel, edge_shapes + [((slots + 8,), jnp.int32)], [], 2, (flat_spans, where, pop),
        out_specs=[inside] * 3 + [pl.BlockSpec(memory_space=pltpu.SMEM)],
    )

    table_shape = (slots, 16, BLOCK)
    coupling = [
        pltpu.VMEM(force_shape, f32),
        pltpu.VMEM((3 * FIELDS * DEPTH, 256), jnp.bfloat16),
        pltpu.VMEM((3 * FIELDS * DEPTH, 256), f32),
        pltpu.VMEM((3 * FIELDS * DEPTH, 256), f32),
        pltpu.VMEM((slots, 8, BLOCK), f32),
    ]
    force, to_right, to_left, table = call(
        functools.partial(first_kernel, span_y, slots, filaments, columns),
        [force_shape, (EDGE_ROWS + 24, 128), (EDGE_ROWS + 24, 128), table_shape],
        coupling + [pltpu.VMEM((filaments * blocks * 8 + 8, BLOCK), f32), pltpu.VMEM((slots * 8, BLOCK), f32)],
        4,
        (flat_spans, where, chosen, stiffness, flow, right_edge, left_edge, *parts),
    )

    moved = pltpu.VMEM((5, ROWS, 128), f32)
    side = (5, ROWS, 128)

    def collision(first, dev, edges, force, to_right, to_left):
        left, right = ring(to_right, "gy", 1), ring(to_left, "gy", -1)
        post, east, west = call(
            functools.partial(collide_kernel, first), [field, (PLANE, 128), (PLANE, 128)], [], 0, (*dev, force)
        )
        post_edge, east, west = call(
            functools.partial(collide_edge_kernel, first), [edge, (PLANE_ROWS, 128), (PLANE_ROWS, 128)], [], 0,
            (edges, to_right, left, right, east, west),
        )
        return post, post_edge, ring(east, "gx", 1), ring(west, "gx", -1), left, right

    post, post_edge, east, west, _, _ = collision(True, (pop,), own_edge, force, to_right, to_left)
    still, still_edge = call(
        functools.partial(stream_kernel, STILL), [(9, ROWS, 128), (9, 8, 128)], [], 0, (post, post_edge)
    )
    east_dev, east_edge = call(
        functools.partial(stream_kernel, EAST), [side, (5, 8, 128)], [moved], 0, (post, post_edge, east)
    )
    dev, edges, force, to_right, to_left, *chunks = call(
        functools.partial(second_kernel, slots, blocks, columns),
        [side, edge, force_shape] + [(24 + share_rows, BLOCK)] * 2 + [(share_rows, BLOCK)] * (columns - 2),
        [moved, pltpu.VMEM(force_shape, f32)] + coupling + [pltpu.VMEM((filaments * blocks + 1, 8, BLOCK), f32)],
        2,
        (where, chosen, post, post_edge, still, still_edge, east_dev, east_edge, west, table),
    )
    post, post_edge, east, west, left, right = collision(
        False, (still, east_dev, dev), edges, force, to_right, to_left
    )
    speed = chunks[0] + left[24:] + right[24:]
    for s in range(2, columns - 1):
        speed = speed + ring(chunks[s - 1], "gy", s)
    speed = speed.reshape(3, share_blocks, filaments, BLOCK).transpose(2, 0, 1, 3).reshape(fraction.shape)

    dev = None
    for entries in (STILL, EAST + WEST):
        count = len(entries)
        scratch = [pltpu.VMEM((count, ROWS, 128), f32), pltpu.SemaphoreType.DMA((count,))]
        extra, args = {}, (post, post_edge)
        if entries is not STILL:
            scratch, args = scratch + [moved], args + (east, west, dev)
            extra = dict(in_specs=[inside] * 4 + [anywhere], input_output_aliases={4: 0})
        (dev,) = call(functools.partial(last_kernel, entries), [field], scratch, 0, args, out_specs=[anywhere], **extra)
    dev = dev.reshape(19, depth, halves, tile_x, 128).transpose(0, 1, 3, 2, 4).reshape(populations.shape)
    return dev, speed


def solution(mesh):
    placed = (P(None, None, "gx", "gy"), P("gx", None, "gy"), P("gx", None, None), P("gx"))
    return jax.shard_map(
        per_device,
        mesh=mesh,
        in_specs=placed,
        out_specs=(P(None, None, "gx", "gy"), P("gx", None, "gy")),
        check_vma=False,
    )
```

```python
import functools
import math

import jax
import jax.numpy as jnp
from jax import lax
from jax.experimental import pallas as pl
from jax.experimental.pallas import tpu as pltpu
from jax.sharding import PartitionSpec as P

STEPS = 2

velocity_set = (
    (0, 0, 0),
    (1, 0, 0),
    (-1, 0, 0),
    (0, 1, 0),
    (0, -1, 0),
    (0, 0, 1),
    (0, 0, -1),
    (1, 1, 0),
    (-1, -1, 0),
    (1, -1, 0),
    (-1, 1, 0),
    (1, 0, 1),
    (-1, 0, -1),
    (1, 0, -1),
    (-1, 0, 1),
    (0, 1, 1),
    (0, -1, -1),
    (0, 1, -1),
    (0, -1, 1),
)
lattice_weight = (1.0 / 3.0,) + (1.0 / 18.0,) * 6 + (1.0 / 36.0,) * 12
unit = 0.002
feedback_gain = 2.0
EAST = tuple(i for i in range(19) if velocity_set[i][0] == 1)
WEST = tuple(i for i in range(19) if velocity_set[i][0] == -1)
STILL = tuple(i for i in range(19) if velocity_set[i][0] == 0)
MOVING = EAST + WEST

DEPTH = 16
ROWS = DEPTH * 8
BLOCK = 128
GROUP = 32
PLANE = 160
PLANE_ROWS = 176
FIELDS = 9
EDGE_ROWS = 80
TINY = 1e-30
FINE = jnp.float8_e4m3fn
VMEM_LIMIT = 40 * 1024 * 1024


def opposite(entry):
    return entry + 1 if entry % 2 == 1 else entry - 1


def iotas(shape=(8, 128)):
    return lax.broadcasted_iota(jnp.int32, shape, 0), lax.broadcasted_iota(jnp.int32, shape, 1)


def turn(value, shift, axis):
    shift = shift % value.shape[axis]
    return pltpu.roll(value, shift, axis) if shift else value


def pack_edges(slices):
    _, lane = iotas()
    total = jnp.zeros((8, 128), jnp.float32)
    for z in range(DEPTH):
        at = 5 * (DEPTH - 1 - z)
        total = jnp.where((lane >= at) & (lane < at + 5), turn(slices(z), at + 2, 1), total)
    return total


def signed_sum(terms):
    total = None
    for sign, value in terms:
        if total is None:
            total = value if sign > 0 else -value
        else:
            total = total + value if sign > 0 else total - value
    return total


def dot_c(vector, parts):
    return signed_sum([(vector[a], parts[a]) for a in range(3) if vector[a] != 0])


def moments(dev):
    total = dev[0]
    for entry in range(1, 19):
        total = total + dev[entry]
    momentum = [
        signed_sum([(velocity_set[e][a], dev[e]) for e in range(19) if velocity_set[e][a] != 0]) for a in range(3)
    ]
    return total, momentum, 1.0 + unit * total


def collide(dev, force):
    total, momentum, dens = moments(dev)
    inverse = 1.0 / dens
    vel = [(momentum[a] + 0.5 * force[a]) * inverse for a in range(3)]
    odd_base = [3.75 * momentum[a] + 3.0 * force[a] for a in range(3)]
    even_base = [5.625 * momentum[a] + 6.1875 * force[a] for a in range(3)]
    along = vel[0] * even_base[0] + vel[1] * even_base[1] + vel[2] * even_base[2]
    base = 1.25 * total - (unit / 3.0) * along
    post = [lattice_weight[0] * base - 0.25 * dev[0]]
    scaled = [unit * vel[a] for a in range(3)]
    for entry in range(1, 19, 2):
        vector, weight = velocity_set[entry], lattice_weight[entry]
        odd = weight * dot_c(vector, odd_base)
        even = weight * (base + dot_c(vector, scaled) * dot_c(vector, even_base))
        post.append((even + odd) - 0.25 * dev[entry])
        post.append((even - odd) - 0.25 * dev[entry + 1])
    return post


def merge_edges(own, left, right):
    row, lane = iotas()
    j = lane % 5
    from_left = (row >= 4) & (j < 2)
    from_right = (row < 4) & (j >= 2)
    return jnp.where(from_left, left, jnp.where(from_right, right, turn(own, 4, 0)))


def flow_kernel(pop_ref, part_ref, flow_ref, payload_ref, sem):
    rows = part_ref.shape[0]
    copy = pltpu.make_async_copy(part_ref, payload_ref.at[pl.ds(0, rows)], sem)
    copy.start()
    flow_slices(lambda z: [pop_ref[e, 8 * z : 8 * z + 8, :] for e in range(19)], flow_ref)
    for c in range(3):
        payload_ref[rows + 8 * c : rows + 8 * c + 8, :] = pack_edges(lambda z: flow_ref[c, 8 * z : 8 * z + 8, :])
    copy.wait()


def edge_kernel(spans_ref, where_ref, pop_ref, edge_ref, to_right_ref, to_left_ref, chosen_ref):
    row, _ = iotas()
    filaments, _, blocks = spans_ref.shape
    slots, mine = chosen_ref.shape[0] - 8, where_ref[1]
    count = jnp.int32(0)
    for f in range(filaments):
        for k in range(blocks):
            chosen_ref[count] = f * blocks + k
            count = count + (spans_ref[f, 0, k] == mine).astype(jnp.int32)
    for n in range(slots):
        chosen_ref[n] = jnp.where(n < count, chosen_ref[n], filaments * blocks)
    chosen_ref[slots] = count
    edges = []
    for e in range(19):
        edges.append(pack_edges(lambda z: pop_ref[e, 8 * z : 8 * z + 8, :]))
        edge_ref[e] = edges[e]
    for k in range(10):
        other = turn(edges[2 * k + 1], 4, 0) if k < 9 else edges[2 * k]
        to_right_ref[8 * k : 8 * k + 8, :] = jnp.where(row >= 4, edges[2 * k], other)
        to_left_ref[8 * k : 8 * k + 8, :] = jnp.where(row < 4, edges[2 * k], other)


def shifted(tiles, shift):
    lane = lax.broadcasted_iota(jnp.int32, tiles[0].shape, 1)
    if shift == 0:
        return tiles[1:-1]
    rolled = [turn(tile, -shift, 1) for tile in tiles]
    if shift > 0:
        return [jnp.where(lane >= 128 - shift, rolled[i + 1], rolled[i]) for i in range(1, len(tiles) - 1)]
    return [jnp.where(lane < -shift, rolled[i - 1], rolled[i]) for i in range(1, len(tiles) - 1)]


def basis_fields(four):
    return (
        0.25 * ((four[0] + four[2]) + (four[1] + four[3])),
        0.25 * (four[2] - four[0]),
        0.25 * (four[1] - four[3]),
    )


def basis_cells(three):
    one, sine, cosine = three
    return one - sine, one + cosine, one + sine, one - cosine


def largest(value):
    return jnp.max(jnp.max(jnp.abs(value), axis=1, keepdims=True), axis=0, keepdims=True)


def prepare_matrix(flow_ref, halo_ref, matrix_ref, rest_ref):
    top = None
    for c in range(3):
        for z in range(DEPTH):
            part = slice(8 * z, 8 * z + 8)
            both = jnp.maximum(jnp.abs(flow_ref[c, part, :]), jnp.abs(halo_ref[c, part, :]))
            top = both if top is None else jnp.maximum(top, both)
    top = jnp.maximum(largest(top), TINY)
    scale = 2.0**15 / top
    for c in range(3):
        per_x = []
        for x in range(4):
            tiles = [
                halo_ref[c, pl.ds(4 + x, DEPTH, stride=8), :],
                flow_ref[c, pl.ds(x, DEPTH, stride=8), :],
                flow_ref[c, pl.ds(4 + x, DEPTH, stride=8), :],
                halo_ref[c, pl.ds(x, DEPTH, stride=8), :],
            ]
            per_x.append(tiles)
        by_basis = [basis_fields([per_x[x][t] for x in range(4)]) for t in range(4)]
        for xf in range(3):
            tiles = [by_basis[t][xf] for t in range(4)]
            four = [shifted(tiles, s) for s in (-1, 0, 1, 2)]
            for half in range(2):
                fields = basis_fields([four[s][half] for s in range(4)])
                columns = slice(half * 128, half * 128 + 128)
                for yf in range(3):
                    row = ((c * 3 + yf) * 3 + xf) * DEPTH
                    value = fields[yf] * scale
                    high = value.astype(jnp.bfloat16)
                    matrix_ref[row : row + DEPTH, columns] = high
                    rest_ref[row : row + DEPTH, columns] = value - high.astype(jnp.float32)
    return top


def couple(slots, table_ref, matrix_ref, rest_ref, total_ref, speed_ref, top):
    group = min(GROUP, slots)
    unscale = top * 2.0**-15
    bound = jnp.maximum(table_ref[0, 12:13, 0:1] + feedback_gain * top, TINY)
    scale = 2.0**17 / bound
    column = lax.broadcasted_iota(jnp.int32, (256, BLOCK), 0).astype(jnp.float32).astype(jnp.bfloat16)
    one, none = jnp.bfloat16(1), jnp.bfloat16(0)
    z_cell = lax.broadcasted_iota(jnp.int32, (DEPTH, BLOCK), 0).astype(jnp.float32)
    rest = rest_ref[...].astype(FINE)

    def body(step):
        first = step * group
        hot, weight_z, coef = [], [], []
        for g in range(group):
            slot = first + g
            q = lambda k: table_ref[slot, k : k + 1, :]
            hot.append(jnp.where(column == q(0).astype(jnp.bfloat16), one, none))
            gap = z_cell - q(5)
            sine, cosine = q(6), q(7)
            weight_z.append(
                jnp.where(
                    gap == -1.0,
                    0.25 - 0.25 * sine,
                    jnp.where(
                        gap == 0.0,
                        0.25 + 0.25 * cosine,
                        jnp.where(gap == 1.0, 0.25 + 0.25 * sine, jnp.where(gap == 2.0, 0.25 - 0.25 * cosine, 0.0)),
                    ),
                )
            )
            by, bx = (None, q(1), q(2)), (None, q(3), q(4))
            coef.append(
                [
                    [by[i] if bx[k] is None else bx[k] if by[i] is None else by[i] * bx[k] for k in range(3)]
                    for i in range(3)
                ]
            )
        coarse = jnp.concatenate(hot, axis=1)
        fine = coarse.astype(FINE)
        across = jnp.dot(matrix_ref[...], coarse, preferred_element_type=jnp.float32)
        across += jnp.dot(rest, fine, preferred_element_type=jnp.float32)
        spread_high, spread_low = [], []
        for g in range(group):
            slot = first + g
            columns = slice(g * BLOCK, (g + 1) * BLOCK)
            pieces = []
            for c in range(3):
                sums = None
                for yf in range(3):
                    for xf in range(3):
                        row = ((c * 3 + yf) * 3 + xf) * DEPTH
                        term = across[row : row + DEPTH, columns]
                        factor = coef[g][yf][xf]
                        term = term if factor is None else term * factor
                        sums = term if sums is None else sums + term
                speed = jnp.sum(sums * weight_z[g], axis=0, keepdims=True) * unscale
                speed_ref[slot, c : c + 1, :] = speed
                push = (table_ref[slot, 8 + c : 9 + c, :] - feedback_gain * speed) * table_ref[slot, 11:12, :] * scale
                for yf in range(3):
                    for xf in range(3):
                        factor = coef[g][yf][xf]
                        pieces.append(weight_z[g] * (push if factor is None else push * factor))
            piece = jnp.concatenate(pieces, axis=0)
            high = piece.astype(jnp.bfloat16)
            spread_high.append(high)
            spread_low.append((piece - high.astype(jnp.float32)).astype(FINE))
        across_rows = (((1,), (1,)), ((), ()))
        total = lax.dot_general(
            jnp.concatenate(spread_high, axis=1), coarse, across_rows, preferred_element_type=jnp.float32
        ) + lax.dot_general(
            jnp.concatenate(spread_low, axis=1), fine, across_rows, preferred_element_type=jnp.float32
        )
        total_ref[...] = total if step == 0 else total_ref[...] + total

    for step in range(slots // group):
        body(step)
    return bound * 2.0**-21


def finish_force(unscale, total_ref, halo_ref, force_ref, force_edge_ref, start=0):
    lane = lax.broadcasted_iota(jnp.int32, (DEPTH, 128), 1)
    zero = jnp.zeros((DEPTH, 128), jnp.float32)
    for c in range(3):
        by_basis = []
        for xf in range(3):
            field = []
            for yf in range(3):
                row = ((c * 3 + yf) * 3 + xf) * DEPTH
                field.append([total_ref[row : row + DEPTH, 0:128], total_ref[row : row + DEPTH, 128:256]])
            cells = [basis_cells([field[yf][half] for yf in range(3)]) for half in range(2)]
            sums = None
            for k, shift in enumerate((1, 0, -1, -2)):
                tiles = shifted([zero, zero, cells[0][k], cells[1][k], zero, zero], shift)
                sums = tiles if sums is None else [a + b for a, b in zip(sums, tiles)]
            by_basis.append(sums)
        by_x = [basis_cells([by_basis[xf][t] * unscale for xf in range(3)]) for t in range(4)]
        for x in range(4):
            left, low, high, right = (by_x[t][x] for t in range(4))
            force_ref[c, pl.ds(x, DEPTH, stride=8), :] = low
            force_ref[c, pl.ds(4 + x, DEPTH, stride=8), :] = high
            halo_ref[c, pl.ds(4 + x, DEPTH, stride=8), :] = jnp.where(lane >= 64, left, low)
            halo_ref[c, pl.ds(x, DEPTH, stride=8), :] = jnp.where(lane >= 64, high, right)
        row = start + 8 * c
        force_edge_ref[row : row + 8, :] = pack_edges(lambda z: halo_ref[c, 8 * z : 8 * z + 8, :])


def flow_slices(load, flow_ref):
    for z in range(DEPTH):
        total, momentum, dens = moments(load(z))
        inverse = 1.0 / dens
        for c in range(3):
            flow_ref[c, 8 * z : 8 * z + 8, :] = momentum[c] * inverse


def edge_flow(edges):
    total, momentum, dens = moments(edges)
    inverse = 1.0 / dens
    return [momentum[c] * inverse for c in range(3)]


def flow_edges(flows, halo_ref):
    for c in range(3):
        flow = flows[c]
        for z in range(DEPTH):
            halo_ref[c, 8 * z : 8 * z + 8, :] = turn(flow, -(5 * (DEPTH - 1 - z) + 2), 1)


def gather_markers(span_y, slots, filaments, share, spans_ref, where_ref, chosen_ref, stiff_ref, part_refs, places_ref, picked_ref, table_ref):
    columns = len(part_refs)
    blocks = share * columns
    block, lane = iotas((blocks, BLOCK))
    anchor = (where_ref[0] * 4).astype(jnp.float32)
    mine = where_ref[1]
    tile_start = (mine * 256).astype(jnp.float32)
    for s in range(columns):
        source = lax.rem(mine + (columns - s), columns)
        for f in range(filaments):
            for k in range(share):
                index = f * blocks + source * share + k
                span = (spans_ref[f, 0, source * share + k] * 256).astype(jnp.float32)
                row = lambda c: part_refs[s][(c * share + k) * filaments + f][None, :]
                start = pl.multiple_of(index * 8, 8)
                three = [anchor + 1.0 + row(0) * (4 - 3.01), span + row(1) * 256.0, 1.0 + row(2) * (DEPTH - 3.01)]
                places_ref[pl.ds(start, 8), :] = jnp.concatenate(three + [jnp.zeros((5, BLOCK), jnp.float32)], axis=0)
    for f in range(filaments):
        factor = stiff_ref[f].astype(jnp.float32) * (1.0 / 256.0)
        start = f * blocks * 8
        places = [places_ref[pl.ds(start + c, blocks, stride=8), :] for c in range(3)]
        for c in range(3):
            ahead = turn(places[c], -1, 1)
            ahead = jnp.where(lane == BLOCK - 1, turn(ahead, -1, 0), ahead) - places[c]
            if c == 1:
                half = 0.5 * span_y
                ahead = jnp.where(ahead > half, ahead - span_y, jnp.where(ahead < -half, ahead + span_y, ahead))
            ahead = jnp.where((lane == BLOCK - 1) & (block == blocks - 1), 0.0, ahead)
            behind = turn(ahead, 1, 1)
            behind = jnp.where(lane == 0, turn(behind, 1, 0), behind)
            places_ref[pl.ds(start + 3 + c, blocks, stride=8), :] = (ahead - behind) * factor
        places_ref[pl.ds(start, blocks, stride=8), :] = places[0] - anchor
        places_ref[pl.ds(start + 1, blocks, stride=8), :] = places[1] - tile_start
    total = filaments * blocks
    places_ref[pl.ds(total * 8, 8), :] = jnp.zeros((8, BLOCK), jnp.float32)
    for n in range(slots):
        picked_ref[8 * n : 8 * n + 8, :] = places_ref[pl.ds(pl.multiple_of(chosen_ref[n] * 8, 8), 8), :]
    count = chosen_ref[slots]
    got = lambda k: picked_ref[pl.ds(k, slots, stride=8), :]
    slot, _ = iotas((slots, BLOCK))

    def put(k, value):
        table_ref[:, k, :] = value

    def basis(t):
        square = t * t
        sine = cosine = None
        for k in range(6, -1, -1):
            a, b = ((-1) ** k * (0.5 * math.pi) ** n / math.factorial(n) for n in (2 * k + 1, 2 * k))
            sine = a if sine is None else sine * square + a
            cosine = b if cosine is None else cosine * square + b
        return sine * t, cosine

    y = got(1)
    base = jnp.minimum(jnp.floor(y), 255.0)
    put(0, base)
    sine, cosine = basis(y - base)
    put(1, sine)
    put(2, cosine)
    sine, cosine = basis(got(0) - 1.0)
    put(3, sine)
    put(4, cosine)
    z = got(2)
    base = jnp.floor(z)
    put(5, base)
    sine, cosine = basis(z - base)
    put(6, sine)
    put(7, cosine)
    bends = [got(3 + c) for c in range(3)]
    for c in range(3):
        put(8 + c, bends[c])
    put(11, jnp.where(slot < count, 1.0, 0.0))
    top = largest(jnp.maximum(jnp.maximum(jnp.abs(bends[0]), jnp.abs(bends[1])), jnp.abs(bends[2])))
    table_ref[0, 12:13, :] = jnp.broadcast_to(top, (1, BLOCK))


def first_kernel(span_y, slots, filaments, columns, spans_ref, where_ref, chosen_ref, stiff_ref, flow_ref, right_edge_ref, left_edge_ref, *refs):
    part_refs, refs = refs[:columns], refs[columns:]
    force_ref, to_right_ref, to_left_ref, table_ref = refs[:4]
    halo_ref, matrix_ref, rest_ref, total_ref, speed_ref, places_ref, picked_ref = refs[4:]
    share = spans_ref.shape[2] // columns
    to_right_ref[0:EDGE_ROWS, :] = right_edge_ref[...]
    to_left_ref[0:EDGE_ROWS, :] = left_edge_ref[...]
    gather_markers(
        span_y, slots, filaments, share, spans_ref, where_ref, chosen_ref, stiff_ref, part_refs, places_ref, picked_ref, table_ref
    )
    flows = []
    for c in range(3):
        start = 3 * share * filaments + 8 * c
        flows.append(merge_edges(*(part_refs[s][start : start + 8, :] for s in (0, 1, -1))))
    flow_edges(flows, halo_ref)
    top = prepare_matrix(flow_ref, halo_ref, matrix_ref, rest_ref)
    unscale = couple(slots, table_ref, matrix_ref, rest_ref, total_ref, speed_ref, top)
    finish_force(unscale, total_ref, halo_ref, force_ref, to_right_ref, EDGE_ROWS)
    to_left_ref[EDGE_ROWS:, :] = to_right_ref[EDGE_ROWS:, :]


def collide_kernel(first, *refs):
    dev_refs, (force_ref, post_ref, east_ref, west_ref) = refs[:-4], refs[-4:]

    def dev(e, part):
        if first:
            return dev_refs[0][e, part, :]
        return dev_refs[0][e, part, :] if e in STILL else dev_refs[1][MOVING.index(e), part, :]

    for z in range(DEPTH):
        part = slice(8 * z, 8 * z + 8)
        post = collide([dev(e, part) for e in range(19)], [force_ref[c, part, :] for c in range(3)])
        for e in range(19):
            post_ref[e, part, :] = post[e]
    for k in range(5):
        east_ref[32 * k : 32 * k + 32, :] = post_ref[EAST[k], pl.ds(3, 32, stride=4), :]
        west_ref[32 * k : 32 * k + 32, :] = post_ref[WEST[k], pl.ds(0, 32, stride=4), :]


def collide_edge_kernel(first, edge_ref, own_ref, left_ref, right_ref, to_east_ref, to_west_ref, post_edge_ref, east_ref, west_ref):
    row, _ = iotas()
    start = EDGE_ROWS if first else 0
    edges = []
    for e in range(19):
        value = edge_ref[e]
        if first:
            part, shift = slice(8 * (e // 2), 8 * (e // 2) + 8), 4 * (e % 2)
            value = merge_edges(value, turn(left_ref[part, :], shift, 0), turn(right_ref[part, :], shift, 0))
        edges.append(value)
    force = []
    for c in range(3):
        part = slice(start + 8 * c, start + 8 * c + 8)
        force.append(own_ref[part, :] + jnp.where(row >= 4, turn(left_ref[part, :], 4, 0), turn(right_ref[part, :], 4, 0)))
    post = collide(edges, force)
    for e in range(19):
        post_edge_ref[e] = post[e]
    east_ref[0:PLANE, :] = to_east_ref[...]
    west_ref[0:PLANE, :] = to_west_ref[...]
    for k in range(5):
        line = PLANE + 2 * k
        for half in range(2):
            at = 4 * half
            east_ref[line + half : line + half + 1, :] = post[EAST[k]][at + 3 : at + 4, :]
            west_ref[line + half : line + half + 1, :] = post[WEST[k]][at : at + 1, :]
    zero = jnp.zeros((PLANE_ROWS - PLANE - 10, 128), jnp.float32)
    east_ref[PLANE + 10 :, :] = zero
    west_ref[PLANE + 10 :, :] = zero


def stream(entries, post_ref, post_edge_ref, moved_ref, store, store_edge):
    row, lane = iotas()
    low, high = row < 4, row >= 4
    same = (low & (lane < 2)) | (high & (lane == 127))
    patches = {0: same, 1: low & (lane < 3), -1: (low & (lane == 0)) | (high & (lane >= 126))}
    low_wall, high_wall = lane >= 75, lane < 5
    for e in entries:
        cx, cy, cz = velocity_set[e]
        edge = turn(turn(post_edge_ref[e], cx, 0), cy - 5 * cz, 1)
        if cz == 1:
            edge = jnp.where(low_wall, post_edge_ref[opposite(e)], edge)
        elif cz == -1:
            edge = jnp.where(high_wall, post_edge_ref[opposite(e)], edge)
        store_edge(e, edge)
        swapped = turn(edge, 4, 0)
        for z in range(DEPTH):
            source, patch = z - cz, patches[cy]
            if 0 <= source < DEPTH:
                value = turn(post_ref[e, 8 * source : 8 * source + 8, :], cx, 0)
                if cy != 0:
                    value = turn(value, cy, 1)
                    value = jnp.where(lane == (0 if cy == 1 else 127), turn(value, 4, 0), value)
            else:
                value, patch = post_ref[opposite(e), 8 * z : 8 * z + 8, :], same
            store(e, z, jnp.where(patch, turn(swapped, -(5 * (DEPTH - 1 - z) + 2), 1), value))


def join(e, plane_ref, post_ref, post_edge_ref, before, before_edge, moved_ref, store, store_edge):
    cx, cy, cz = velocity_set[e]
    k, x = (EAST if cx == 1 else WEST).index(e), 0 if cx == 1 else 3
    row, lane = iotas((DEPTH, 128))
    _, single = iotas((1, 128))
    edges = []
    for half in range(2):
        line, at = PLANE + 2 * k + half, 4 * half + x
        edge = turn(plane_ref[line : line + 1, :], cy - 5 * cz, 1)
        if cz != 0:
            edge = jnp.where(single >= 75 if cz == 1 else single < 5, post_edge_ref[opposite(e), at : at + 1, :], edge)
        edges.append(edge)
    tiles = [plane_ref[pl.ds(32 * k + half, DEPTH, stride=2), :] for half in range(2)]
    if cy != 0:
        turned = [turn(tile, cy, 1) for tile in tiles]
        tiles = [turned[0], jnp.where(lane == 0, turned[0], turned[1])]
        if cy == -1:
            tiles = [jnp.where(lane == 127, turned[1], turned[0]), turned[1]]
    wall = row == (0 if cz == 1 else DEPTH - 1)
    place = MOVING.index(e)
    for half in range(2):
        tile = tiles[half]
        same = lane < 2 if half == 0 else lane == 127
        patch = {
            0: same, 1: lane < 3 if half == 0 else lane < 0, -1: lane == 0 if half == 0 else lane >= 126
        }[cy]
        if cz != 0:
            at = (0 if cz == 1 else 8 * DEPTH - 8) + 4 * half + x
            tile = jnp.where(wall, post_ref[opposite(e), at : at + 1, :], turn(tile, cz, 0))
            patch = (wall & same) | (jnp.logical_not(wall) & patch)
        shown = pltpu.roll(jnp.broadcast_to(edges[1 - half], (DEPTH, 128)), 51, 1, stride=5, stride_axis=0)
        moved_ref[place, pl.ds(4 * half + x, DEPTH, stride=8), :] = jnp.where(patch, shown, tile)
    row, _ = iotas()
    for z in range(DEPTH):
        part = slice(8 * z, 8 * z + 8)
        store(e, z, jnp.where(row % 4 == x, moved_ref[place, part, :], before[part, :]))
    if store_edge is not None:
        store_edge(e, jnp.where(row == x, edges[0], jnp.where(row == 4 + x, edges[1], before_edge[...])))


def stream_kernel(post_ref, post_edge_ref, dev_ref, edges_ref):
    def store(e, z, value):
        dev_ref[e, 8 * z : 8 * z + 8, :] = value

    def store_edge(e, value):
        edges_ref[e] = value

    stream(range(19), post_ref, post_edge_ref, None, store, store_edge)


def second_kernel(
    slots, blocks, columns, where_ref, chosen_ref,
    post_ref, post_edge_ref, streamed_ref, streamed_edge_ref, east_ref, west_ref, table_ref, *refs
):
    dev_ref, edges_ref, force_ref, to_right_ref, to_left_ref = refs[:5]
    share_refs, refs = refs[5 : 3 + columns], refs[3 + columns :]
    moved_ref, flow_ref, halo_ref, matrix_ref, rest_ref, total_ref, speed_ref, spot_ref = refs

    def store(e, z, value):
        dev_ref[MOVING.index(e), 8 * z : 8 * z + 8, :] = value

    def store_edge(e, value):
        edges_ref[e] = value

    def dev(e, z):
        part = slice(8 * z, 8 * z + 8)
        return streamed_ref[e, part, :] if e in STILL else dev_ref[MOVING.index(e), part, :]

    for e in MOVING:
        join(
            e, east_ref if e in EAST else west_ref, post_ref, post_edge_ref,
            streamed_ref.at[e], streamed_edge_ref.at[e], moved_ref, store, store_edge,
        )
    for e in STILL:
        edges_ref[e] = streamed_edge_ref[e]
    flow_slices(lambda z: [dev(e, z) for e in range(19)], flow_ref)
    flow_edges(edge_flow([edges_ref[e] for e in range(19)]), halo_ref)
    top = prepare_matrix(flow_ref, halo_ref, matrix_ref, rest_ref)
    unscale = couple(slots, table_ref, matrix_ref, rest_ref, total_ref, speed_ref, top)
    finish_force(unscale, total_ref, halo_ref, force_ref, to_right_ref)
    to_left_ref[0:24, :] = to_right_ref[0:24, :]
    mine = where_ref[1]

    total = spot_ref.shape[0] - 1
    spot_ref[...] = jnp.zeros_like(spot_ref)
    for n in range(slots):
        spot_ref[chosen_ref[n]] = speed_ref[n]
    filaments = total // blocks
    share = blocks // columns
    others = iter(share_refs)
    for s in range(columns):
        target, start = (to_right_ref, 24) if s == 1 else (to_left_ref, 24) if s == columns - 1 else (next(others), 0)
        owner = lax.rem(mine + s, columns)
        for f in range(filaments):
            for k in range(share):
                for c in range(3):
                    row = start + (c * share + k) * filaments + f
                    target[row : row + 1, :] = spot_ref[f * blocks + owner * share + k, c : c + 1, :]


def last_still_kernel(post_ref, post_edge_ref, dev_ref, before_ref, kept_ref, sems):
    def store(e, z, value):
        if e in STILL:
            kept_ref[STILL.index(e), 8 * z : 8 * z + 8, :] = value
        else:
            before_ref[MOVING.index(e), 8 * z : 8 * z + 8, :] = value

    copies = []
    for k, e in enumerate(STILL):
        stream((e,), post_ref, post_edge_ref, None, store, lambda e, value: None)
        copies.append(pltpu.make_async_copy(kept_ref.at[k], dev_ref.at[e], sems.at[k]))
        copies[-1].start()
    stream(MOVING, post_ref, post_edge_ref, None, store, lambda e, value: None)
    for copy in copies:
        copy.wait()


def last_kernel(
    post_ref, post_edge_ref, before_ref, east_ref, west_ref, home_ref, old_ref, dev_ref, speed_ref, moved_ref, kept_ref, sems
):
    def store(e, z, value):
        kept_ref[MOVING.index(e), 8 * z : 8 * z + 8, :] = value

    copies = [pltpu.make_async_copy(home_ref, speed_ref, sems.at[10])]
    copies[0].start()
    for k, e in enumerate(MOVING):
        plane_ref = east_ref if e in EAST else west_ref
        join(e, plane_ref, post_ref, post_edge_ref, before_ref.at[k], None, moved_ref, store, None)
        copies.append(pltpu.make_async_copy(kept_ref.at[k], dev_ref.at[e], sems.at[k]))
        copies[-1].start()
    for copy in copies:
        copy.wait()


def call(body, outs, scratch, n_smem, args, flops=0, **extra):
    spec = [pl.BlockSpec(memory_space=pltpu.SMEM)] * n_smem
    spec += [pl.BlockSpec(memory_space=pltpu.VMEM)] * (len(args) - n_smem)
    outs = [out if isinstance(out[-1], type) else (out, jnp.float32) for out in outs]
    moved = 4 * sum(math.prod(shape) for shape, _ in outs)
    options = dict(
        in_specs=spec,
        out_specs=[pl.BlockSpec(memory_space=pltpu.VMEM)] * len(outs),
        cost_estimate=pl.CostEstimate(flops=flops, bytes_accessed=2 * moved, transcendentals=0),
    )
    options.update(extra)
    return pl.pallas_call(
        body,
        out_shape=[jax.ShapeDtypeStruct(*out) for out in outs],
        scratch_shapes=scratch,
        compiler_params=pltpu.CompilerParams(vmem_limit_bytes=VMEM_LIMIT),
        **options,
    )(*args)


def ring(value, axis, step):
    count = lax.axis_size(axis)
    return lax.ppermute(value, axis, [(i, (i + step) % count) for i in range(count)])


def per_device(populations, fraction, spans, stiffness):
    depth, tile_x, tile_y = populations.shape[1:]
    columns = lax.axis_size("gy")
    span_y = float(tile_y * columns)
    filaments, _, share = fraction.shape
    blocks = spans.shape[1]
    share_blocks = share // BLOCK
    slots = max(8, 2 * filaments * blocks // columns)
    f32 = jnp.float32

    own_part = fraction.reshape(filaments, 3, share_blocks, BLOCK).transpose(1, 2, 0, 3)
    own_part = own_part.reshape(3 * share_blocks * filaments, BLOCK)

    field = (19, ROWS, 128)
    edge = (19, 8, 128)
    halves = tile_y // 128
    pop = populations.reshape(19, depth, tile_x, halves, 128).transpose(0, 1, 3, 2, 4).reshape(field)
    flat_spans = spans.transpose(0, 2, 1)
    where = jnp.stack([lax.axis_index("gx"), lax.axis_index("gy")]).astype(jnp.int32)

    force_shape = (3, ROWS, 128)
    share_rows = 3 * share_blocks * filaments
    inside, anywhere = pl.BlockSpec(memory_space=pltpu.VMEM), pl.BlockSpec(memory_space=pl.ANY)
    flow, payload = call(
        flow_kernel, [force_shape, (share_rows + 24, BLOCK)], [pltpu.SemaphoreType.DMA], 0, (pop, own_part),
        in_specs=[inside, anywhere],
    )
    parts = [payload] + [ring(payload, "gy", s) for s in range(1, columns)]
    edge_shapes = [edge, (EDGE_ROWS, 128), (EDGE_ROWS, 128)]
    own_edge, right_edge, left_edge, chosen = call(
        edge_kernel, edge_shapes + [((slots + 8,), jnp.int32)], [], 2, (flat_spans, where, pop),
        out_specs=[inside] * 3 + [pl.BlockSpec(memory_space=pltpu.SMEM)],
    )

    table_shape = (slots, 16, BLOCK)
    coupling = [
        pltpu.VMEM(force_shape, f32),
        pltpu.VMEM((3 * FIELDS * DEPTH, 256), jnp.bfloat16),
        pltpu.VMEM((3 * FIELDS * DEPTH, 256), f32),
        pltpu.VMEM((3 * FIELDS * DEPTH, 256), f32),
        pltpu.VMEM((slots, 8, BLOCK), f32),
    ]
    force, to_right, to_left, table = call(
        functools.partial(first_kernel, span_y, slots, filaments, columns),
        [force_shape, (EDGE_ROWS + 24, 128), (EDGE_ROWS + 24, 128), table_shape],
        coupling + [pltpu.VMEM((filaments * blocks * 8 + 8, BLOCK), f32), pltpu.VMEM((slots * 8, BLOCK), f32)],
        4,
        (flat_spans, where, chosen, stiffness, flow, right_edge, left_edge, *parts),
    )

    moving = (len(MOVING), ROWS, 128)
    moved = pltpu.VMEM(moving, f32)

    def collision(first, dev, edges, force, to_right, to_left):
        left, right = ring(to_right, "gy", 1), ring(to_left, "gy", -1)
        post, east, west = call(
            functools.partial(collide_kernel, first), [field, (PLANE, 128), (PLANE, 128)], [], 0, (*dev, force)
        )
        post_edge, east, west = call(
            functools.partial(collide_edge_kernel, first), [edge, (PLANE_ROWS, 128), (PLANE_ROWS, 128)], [], 0,
            (edges, to_right, left, right, east, west),
        )
        return post, post_edge, ring(east, "gx", 1), ring(west, "gx", -1), left, right

    post, post_edge, east, west, _, _ = collision(True, (pop,), own_edge, force, to_right, to_left)
    streamed, streamed_edge = call(stream_kernel, [field, edge], [], 0, (post, post_edge))
    dev, edges, force, to_right, to_left, *chunks = call(
        functools.partial(second_kernel, slots, blocks, columns),
        [moving, edge, force_shape] + [(24 + share_rows, BLOCK)] * 2 + [(share_rows, BLOCK)] * (columns - 2),
        [moved, pltpu.VMEM(force_shape, f32)] + coupling + [pltpu.VMEM((filaments * blocks + 1, 8, BLOCK), f32)],
        2,
        (where, chosen, post, post_edge, streamed, streamed_edge, east, west, table),
    )
    post, post_edge, east, west, left, right = collision(
        False, (streamed, dev), edges, force, to_right, to_left
    )
    speed = chunks[0] + left[24:] + right[24:]
    for s in range(2, columns - 1):
        speed = speed + ring(chunks[s - 1], "gy", s)

    dev, before = call(
        last_still_kernel, [field, moving],
        [pltpu.VMEM((9, ROWS, 128), f32), pltpu.SemaphoreType.DMA((9,))],
        0, (post, post_edge), out_specs=[anywhere, inside],
    )
    dev, speed = call(
        last_kernel, [field, (share_rows, BLOCK)],
        [moved, pltpu.VMEM(moving, f32), pltpu.SemaphoreType.DMA((11,))],
        0, (post, post_edge, before, east, west, speed, dev),
        in_specs=[inside] * 6 + [anywhere], out_specs=[anywhere] * 2, input_output_aliases={6: 0},
    )
    speed = speed.reshape(3, share_blocks, filaments, BLOCK).transpose(2, 0, 1, 3).reshape(fraction.shape)
    dev = dev.reshape(19, depth, halves, tile_x, 128).transpose(0, 1, 3, 2, 4).reshape(populations.shape)
    return dev, speed


def solution(mesh):
    placed = (P(None, None, "gx", "gy"), P("gx", None, "gy"), P("gx", None, None), P("gx"))
    return jax.shard_map(
        per_device,
        mesh=mesh,
        in_specs=placed,
        out_specs=(P(None, None, "gx", "gy"), P("gx", None, "gy")),
        check_vma=False,
    )
```

```python
import functools
import math

import jax
import jax.numpy as jnp
from jax import lax
from jax.experimental import pallas as pl
from jax.experimental.pallas import tpu as pltpu
from jax.sharding import PartitionSpec as P

STEPS = 2

velocity_set = (
    (0, 0, 0),
    (1, 0, 0),
    (-1, 0, 0),
    (0, 1, 0),
    (0, -1, 0),
    (0, 0, 1),
    (0, 0, -1),
    (1, 1, 0),
    (-1, -1, 0),
    (1, -1, 0),
    (-1, 1, 0),
    (1, 0, 1),
    (-1, 0, -1),
    (1, 0, -1),
    (-1, 0, 1),
    (0, 1, 1),
    (0, -1, -1),
    (0, 1, -1),
    (0, -1, 1),
)
lattice_weight = (1.0 / 3.0,) + (1.0 / 18.0,) * 6 + (1.0 / 36.0,) * 12
unit = 0.002
feedback_gain = 2.0
EAST = tuple(i for i in range(19) if velocity_set[i][0] == 1)
WEST = tuple(i for i in range(19) if velocity_set[i][0] == -1)
STILL = tuple(i for i in range(19) if velocity_set[i][0] == 0)
MOVING = EAST + WEST

DEPTH = 16
ROWS = DEPTH * 8
BLOCK = 128
GROUP = 32
PLANE = 160
PLANE_ROWS = 176
FIELDS = 9
EDGE_ROWS = 80
TINY = 1e-30
FINE = jnp.float8_e4m3fn
VMEM_LIMIT = 40 * 1024 * 1024


def opposite(entry):
    return entry + 1 if entry % 2 == 1 else entry - 1


def iotas(shape=(8, 128)):
    return lax.broadcasted_iota(jnp.int32, shape, 0), lax.broadcasted_iota(jnp.int32, shape, 1)


def turn(value, shift, axis):
    shift = shift % value.shape[axis]
    return pltpu.roll(value, shift, axis) if shift else value


def pack_edges(slices):
    _, lane = iotas()
    total = jnp.zeros((8, 128), jnp.float32)
    for z in range(DEPTH):
        at = 5 * (DEPTH - 1 - z)
        total = jnp.where((lane >= at) & (lane < at + 5), turn(slices(z), at + 2, 1), total)
    return total


def signed_sum(terms):
    total = None
    for sign, value in terms:
        if total is None:
            total = value if sign > 0 else -value
        else:
            total = total + value if sign > 0 else total - value
    return total


def dot_c(vector, parts):
    return signed_sum([(vector[a], parts[a]) for a in range(3) if vector[a] != 0])


def moments(dev):
    total = dev[0]
    for entry in range(1, 19):
        total = total + dev[entry]
    momentum = [
        signed_sum([(velocity_set[e][a], dev[e]) for e in range(19) if velocity_set[e][a] != 0]) for a in range(3)
    ]
    return total, momentum, 1.0 + unit * total


def collide(dev, force):
    total, momentum, dens = moments(dev)
    inverse = 1.0 / dens
    vel = [(momentum[a] + 0.5 * force[a]) * inverse for a in range(3)]
    odd_base = [3.75 * momentum[a] + 3.0 * force[a] for a in range(3)]
    even_base = [5.625 * momentum[a] + 6.1875 * force[a] for a in range(3)]
    along = vel[0] * even_base[0] + vel[1] * even_base[1] + vel[2] * even_base[2]
    base = 1.25 * total - (unit / 3.0) * along
    post = [lattice_weight[0] * base - 0.25 * dev[0]]
    scaled = [unit * vel[a] for a in range(3)]
    for entry in range(1, 19, 2):
        vector, weight = velocity_set[entry], lattice_weight[entry]
        odd = weight * dot_c(vector, odd_base)
        even = weight * (base + dot_c(vector, scaled) * dot_c(vector, even_base))
        post.append((even + odd) - 0.25 * dev[entry])
        post.append((even - odd) - 0.25 * dev[entry + 1])
    return post


def merge_edges(own, left, right):
    row, lane = iotas()
    j = lane % 5
    from_left = (row >= 4) & (j < 2)
    from_right = (row < 4) & (j >= 2)
    return jnp.where(from_left, left, jnp.where(from_right, right, turn(own, 4, 0)))


def flow_kernel(pop_ref, part_ref, flow_ref, payload_ref, sem):
    rows = part_ref.shape[0]
    copy = pltpu.make_async_copy(part_ref, payload_ref.at[pl.ds(0, rows)], sem)
    copy.start()
    flow_slices(lambda z: [pop_ref[e, 8 * z : 8 * z + 8, :] for e in range(19)], flow_ref)
    for c in range(3):
        payload_ref[rows + 8 * c : rows + 8 * c + 8, :] = pack_edges(lambda z: flow_ref[c, 8 * z : 8 * z + 8, :])
    copy.wait()


def edge_kernel(spans_ref, where_ref, pop_ref, edge_ref, to_right_ref, to_left_ref, chosen_ref):
    row, _ = iotas()
    filaments, _, blocks = spans_ref.shape
    slots, mine = chosen_ref.shape[0] - 8, where_ref[1]
    count = jnp.int32(0)
    for f in range(filaments):
        for k in range(blocks):
            chosen_ref[count] = f * blocks + k
            count = count + (spans_ref[f, 0, k] == mine).astype(jnp.int32)
    for n in range(slots):
        chosen_ref[n] = jnp.where(n < count, chosen_ref[n], filaments * blocks)
    chosen_ref[slots] = count
    edges = []
    for e in range(19):
        edges.append(pack_edges(lambda z: pop_ref[e, 8 * z : 8 * z + 8, :]))
        edge_ref[e] = edges[e]
    for k in range(10):
        other = turn(edges[2 * k + 1], 4, 0) if k < 9 else edges[2 * k]
        to_right_ref[8 * k : 8 * k + 8, :] = jnp.where(row >= 4, edges[2 * k], other)
        to_left_ref[8 * k : 8 * k + 8, :] = jnp.where(row < 4, edges[2 * k], other)


def shifted(tiles, shift):
    lane = lax.broadcasted_iota(jnp.int32, tiles[0].shape, 1)
    if shift == 0:
        return tiles[1:-1]
    rolled = [turn(tile, -shift, 1) for tile in tiles]
    if shift > 0:
        return [jnp.where(lane >= 128 - shift, rolled[i + 1], rolled[i]) for i in range(1, len(tiles) - 1)]
    return [jnp.where(lane < -shift, rolled[i - 1], rolled[i]) for i in range(1, len(tiles) - 1)]


def basis_fields(four):
    return (
        0.25 * ((four[0] + four[2]) + (four[1] + four[3])),
        0.25 * (four[2] - four[0]),
        0.25 * (four[1] - four[3]),
    )


def basis_cells(three):
    one, sine, cosine = three
    return one - sine, one + cosine, one + sine, one - cosine


def largest(value):
    return jnp.max(jnp.max(jnp.abs(value), axis=1, keepdims=True), axis=0, keepdims=True)


def prepare_matrix(flow_ref, halo_ref, matrix_ref, rest_ref):
    top = None
    for c in range(3):
        for z in range(DEPTH):
            part = slice(8 * z, 8 * z + 8)
            both = jnp.maximum(jnp.abs(flow_ref[c, part, :]), jnp.abs(halo_ref[c, part, :]))
            top = both if top is None else jnp.maximum(top, both)
    top = jnp.maximum(largest(top), TINY)
    scale = 2.0**15 / top
    for c in range(3):
        per_x = []
        for x in range(4):
            tiles = [
                halo_ref[c, pl.ds(4 + x, DEPTH, stride=8), :],
                flow_ref[c, pl.ds(x, DEPTH, stride=8), :],
                flow_ref[c, pl.ds(4 + x, DEPTH, stride=8), :],
                halo_ref[c, pl.ds(x, DEPTH, stride=8), :],
            ]
            per_x.append(tiles)
        by_basis = [basis_fields([per_x[x][t] for x in range(4)]) for t in range(4)]
        for xf in range(3):
            tiles = [by_basis[t][xf] for t in range(4)]
            four = [shifted(tiles, s) for s in (-1, 0, 1, 2)]
            for half in range(2):
                fields = basis_fields([four[s][half] for s in range(4)])
                columns = slice(half * 128, half * 128 + 128)
                for yf in range(3):
                    row = ((c * 3 + yf) * 3 + xf) * DEPTH
                    value = fields[yf] * scale
                    high = value.astype(jnp.bfloat16)
                    matrix_ref[row : row + DEPTH, columns] = high
                    rest_ref[row : row + DEPTH, columns] = value - high.astype(jnp.float32)
    return top


def couple(slots, table_ref, matrix_ref, rest_ref, total_ref, speed_ref, top):
    group = min(GROUP, slots)
    unscale = top * 2.0**-15
    bound = jnp.maximum(table_ref[0, 12:13, 0:1] + feedback_gain * top, TINY)
    scale = 2.0**17 / bound
    column = lax.broadcasted_iota(jnp.int32, (256, BLOCK), 0).astype(jnp.float32).astype(jnp.bfloat16)
    one, none = jnp.bfloat16(1), jnp.bfloat16(0)
    z_cell = lax.broadcasted_iota(jnp.int32, (DEPTH, BLOCK), 0).astype(jnp.float32)
    rest = rest_ref[...].astype(FINE)

    def body(step):
        first = step * group
        hot, weight_z, coef = [], [], []
        for g in range(group):
            slot = first + g
            q = lambda k: table_ref[slot, k : k + 1, :]
            hot.append(jnp.where(column == q(0).astype(jnp.bfloat16), one, none))
            gap = z_cell - q(5)
            sine, cosine = q(6), q(7)
            weight_z.append(
                jnp.where(
                    gap == -1.0,
                    0.25 - 0.25 * sine,
                    jnp.where(
                        gap == 0.0,
                        0.25 + 0.25 * cosine,
                        jnp.where(gap == 1.0, 0.25 + 0.25 * sine, jnp.where(gap == 2.0, 0.25 - 0.25 * cosine, 0.0)),
                    ),
                )
            )
            by, bx = (None, q(1), q(2)), (None, q(3), q(4))
            coef.append(
                [
                    [by[i] if bx[k] is None else bx[k] if by[i] is None else by[i] * bx[k] for k in range(3)]
                    for i in range(3)
                ]
            )
        coarse = jnp.concatenate(hot, axis=1)
        fine = coarse.astype(FINE)
        across = jnp.dot(matrix_ref[...], coarse, preferred_element_type=jnp.float32)
        across += jnp.dot(rest, fine, preferred_element_type=jnp.float32)
        spread_high, spread_low = [], []
        for g in range(group):
            slot = first + g
            columns = slice(g * BLOCK, (g + 1) * BLOCK)
            pieces = []
            for c in range(3):
                sums = None
                for yf in range(3):
                    for xf in range(3):
                        row = ((c * 3 + yf) * 3 + xf) * DEPTH
                        term = across[row : row + DEPTH, columns]
                        factor = coef[g][yf][xf]
                        term = term if factor is None else term * factor
                        sums = term if sums is None else sums + term
                speed = jnp.sum(sums * weight_z[g], axis=0, keepdims=True) * unscale
                speed_ref[slot, c : c + 1, :] = speed
                push = (table_ref[slot, 8 + c : 9 + c, :] - feedback_gain * speed) * table_ref[slot, 11:12, :] * scale
                for yf in range(3):
                    for xf in range(3):
                        factor = coef[g][yf][xf]
                        pieces.append(weight_z[g] * (push if factor is None else push * factor))
            piece = jnp.concatenate(pieces, axis=0)
            high = piece.astype(jnp.bfloat16)
            spread_high.append(high)
            spread_low.append((piece - high.astype(jnp.float32)).astype(FINE))
        across_rows = (((1,), (1,)), ((), ()))
        total = lax.dot_general(
            jnp.concatenate(spread_high, axis=1), coarse, across_rows, preferred_element_type=jnp.float32
        ) + lax.dot_general(
            jnp.concatenate(spread_low, axis=1), fine, across_rows, preferred_element_type=jnp.float32
        )
        total_ref[...] = total if step == 0 else total_ref[...] + total

    for step in range(slots // group):
        body(step)
    return bound * 2.0**-21


def finish_force(unscale, total_ref, halo_ref, force_ref, force_edge_ref, start=0):
    lane = lax.broadcasted_iota(jnp.int32, (DEPTH, 128), 1)
    zero = jnp.zeros((DEPTH, 128), jnp.float32)
    for c in range(3):
        by_basis = []
        for xf in range(3):
            field = []
            for yf in range(3):
                row = ((c * 3 + yf) * 3 + xf) * DEPTH
                field.append([total_ref[row : row + DEPTH, 0:128], total_ref[row : row + DEPTH, 128:256]])
            cells = [basis_cells([field[yf][half] for yf in range(3)]) for half in range(2)]
            sums = None
            for k, shift in enumerate((1, 0, -1, -2)):
                low, high = (turn(cells[half][k], -shift, 1) for half in range(2))
                if shift == 1:
                    last = lane == 127
                    tiles = [jnp.where(last, low, zero), jnp.where(last, high, low), jnp.where(last, zero, high), zero]
                elif shift == 0:
                    tiles = [zero, low, high, zero]
                else:
                    begin = lane < -shift
                    tiles = [zero, jnp.where(begin, zero, low), jnp.where(begin, low, high), jnp.where(begin, high, zero)]
                sums = tiles if sums is None else [a + b for a, b in zip(sums, tiles)]
            by_basis.append(sums)
        by_x = [basis_cells([by_basis[xf][t] * unscale for xf in range(3)]) for t in range(4)]
        for x in range(4):
            left, low, high, right = (by_x[t][x] for t in range(4))
            force_ref[c, pl.ds(x, DEPTH, stride=8), :] = low
            force_ref[c, pl.ds(4 + x, DEPTH, stride=8), :] = high
            halo_ref[c, pl.ds(4 + x, DEPTH, stride=8), :] = jnp.where(lane >= 64, left, low)
            halo_ref[c, pl.ds(x, DEPTH, stride=8), :] = jnp.where(lane >= 64, high, right)
        row = start + 8 * c
        force_edge_ref[row : row + 8, :] = pack_edges(lambda z: halo_ref[c, 8 * z : 8 * z + 8, :])


def flow_slices(load, flow_ref):
    for z in range(DEPTH):
        total, momentum, dens = moments(load(z))
        inverse = 1.0 / dens
        for c in range(3):
            flow_ref[c, 8 * z : 8 * z + 8, :] = momentum[c] * inverse


def edge_flow(edges):
    total, momentum, dens = moments(edges)
    inverse = 1.0 / dens
    return [momentum[c] * inverse for c in range(3)]


def flow_edges(flows, halo_ref):
    for c in range(3):
        flow = flows[c]
        for z in range(DEPTH):
            halo_ref[c, 8 * z : 8 * z + 8, :] = turn(flow, -(5 * (DEPTH - 1 - z) + 2), 1)


def gather_markers(span_y, slots, filaments, share, spans_ref, where_ref, chosen_ref, stiff_ref, part_refs, places_ref, picked_ref, table_ref):
    columns = len(part_refs)
    blocks = share * columns
    block, lane = iotas((blocks, BLOCK))
    anchor = (where_ref[0] * 4).astype(jnp.float32)
    mine = where_ref[1]
    tile_start = (mine * 256).astype(jnp.float32)
    for s in range(columns):
        source = lax.rem(mine + (columns - s), columns)
        for f in range(filaments):
            for k in range(share):
                index = f * blocks + source * share + k
                span = (spans_ref[f, 0, source * share + k] * 256).astype(jnp.float32)
                row = lambda c: part_refs[s][(c * share + k) * filaments + f][None, :]
                start = pl.multiple_of(index * 8, 8)
                three = [anchor + 1.0 + row(0) * (4 - 3.01), span + row(1) * 256.0, 1.0 + row(2) * (DEPTH - 3.01)]
                places_ref[pl.ds(start, 8), :] = jnp.concatenate(three + [jnp.zeros((5, BLOCK), jnp.float32)], axis=0)
    for f in range(filaments):
        factor = stiff_ref[f].astype(jnp.float32) * (1.0 / 256.0)
        start = f * blocks * 8
        places = [places_ref[pl.ds(start + c, blocks, stride=8), :] for c in range(3)]
        for c in range(3):
            ahead = turn(places[c], -1, 1)
            ahead = jnp.where(lane == BLOCK - 1, turn(ahead, -1, 0), ahead) - places[c]
            if c == 1:
                half = 0.5 * span_y
                ahead = jnp.where(ahead > half, ahead - span_y, jnp.where(ahead < -half, ahead + span_y, ahead))
            ahead = jnp.where((lane == BLOCK - 1) & (block == blocks - 1), 0.0, ahead)
            behind = turn(ahead, 1, 1)
            behind = jnp.where(lane == 0, turn(behind, 1, 0), behind)
            places_ref[pl.ds(start + 3 + c, blocks, stride=8), :] = (ahead - behind) * factor
        places_ref[pl.ds(start, blocks, stride=8), :] = places[0] - anchor
        places_ref[pl.ds(start + 1, blocks, stride=8), :] = places[1] - tile_start
    total = filaments * blocks
    places_ref[pl.ds(total * 8, 8), :] = jnp.zeros((8, BLOCK), jnp.float32)
    for n in range(slots):
        picked_ref[8 * n : 8 * n + 8, :] = places_ref[pl.ds(pl.multiple_of(chosen_ref[n] * 8, 8), 8), :]
    count = chosen_ref[slots]
    got = lambda k: picked_ref[pl.ds(k, slots, stride=8), :]
    slot, _ = iotas((slots, BLOCK))

    def put(k, value):
        table_ref[:, k, :] = value

    def basis(t):
        square = t * t
        sine = cosine = None
        for k in range(6, -1, -1):
            a, b = ((-1) ** k * (0.5 * math.pi) ** n / math.factorial(n) for n in (2 * k + 1, 2 * k))
            sine = a if sine is None else sine * square + a
            cosine = b if cosine is None else cosine * square + b
        return sine * t, cosine

    y = got(1)
    base = jnp.minimum(jnp.floor(y), 255.0)
    put(0, base)
    sine, cosine = basis(y - base)
    put(1, sine)
    put(2, cosine)
    sine, cosine = basis(got(0) - 1.0)
    put(3, sine)
    put(4, cosine)
    z = got(2)
    base = jnp.floor(z)
    put(5, base)
    sine, cosine = basis(z - base)
    put(6, sine)
    put(7, cosine)
    bends = [got(3 + c) for c in range(3)]
    for c in range(3):
        put(8 + c, bends[c])
    put(11, jnp.where(slot < count, 1.0, 0.0))
    top = largest(jnp.maximum(jnp.maximum(jnp.abs(bends[0]), jnp.abs(bends[1])), jnp.abs(bends[2])))
    table_ref[0, 12:13, :] = jnp.broadcast_to(top, (1, BLOCK))


def first_kernel(span_y, slots, filaments, columns, spans_ref, where_ref, chosen_ref, stiff_ref, flow_ref, right_edge_ref, left_edge_ref, *refs):
    part_refs, refs = refs[:columns], refs[columns:]
    force_ref, to_right_ref, to_left_ref, table_ref = refs[:4]
    halo_ref, matrix_ref, rest_ref, total_ref, speed_ref, places_ref, picked_ref = refs[4:]
    share = spans_ref.shape[2] // columns
    to_right_ref[0:EDGE_ROWS, :] = right_edge_ref[...]
    to_left_ref[0:EDGE_ROWS, :] = left_edge_ref[...]
    gather_markers(
        span_y, slots, filaments, share, spans_ref, where_ref, chosen_ref, stiff_ref, part_refs, places_ref, picked_ref, table_ref
    )
    flows = []
    for c in range(3):
        start = 3 * share * filaments + 8 * c
        flows.append(merge_edges(*(part_refs[s][start : start + 8, :] for s in (0, 1, -1))))
    flow_edges(flows, halo_ref)
    top = prepare_matrix(flow_ref, halo_ref, matrix_ref, rest_ref)
    unscale = couple(slots, table_ref, matrix_ref, rest_ref, total_ref, speed_ref, top)
    finish_force(unscale, total_ref, halo_ref, force_ref, to_right_ref, EDGE_ROWS)
    to_left_ref[EDGE_ROWS:, :] = to_right_ref[EDGE_ROWS:, :]


def collide_kernel(first, *refs):
    dev_refs, (force_ref, post_ref, east_ref, west_ref) = refs[:-4], refs[-4:]

    def dev(e, part):
        if first:
            return dev_refs[0][e, part, :]
        return dev_refs[0][e, part, :] if e in STILL else dev_refs[1][MOVING.index(e), part, :]

    for z in range(DEPTH):
        part = slice(8 * z, 8 * z + 8)
        post = collide([dev(e, part) for e in range(19)], [force_ref[c, part, :] for c in range(3)])
        for e in range(19):
            post_ref[e, part, :] = post[e]
    for k in range(5):
        east_ref[32 * k : 32 * k + 32, :] = post_ref[EAST[k], pl.ds(3, 32, stride=4), :]
        west_ref[32 * k : 32 * k + 32, :] = post_ref[WEST[k], pl.ds(0, 32, stride=4), :]


def collide_edge_kernel(first, edge_ref, own_ref, left_ref, right_ref, to_east_ref, to_west_ref, post_edge_ref, east_ref, west_ref):
    row, _ = iotas()
    start = EDGE_ROWS if first else 0
    edges = []
    for e in range(19):
        value = edge_ref[e]
        if first:
            part, shift = slice(8 * (e // 2), 8 * (e // 2) + 8), 4 * (e % 2)
            value = merge_edges(value, turn(left_ref[part, :], shift, 0), turn(right_ref[part, :], shift, 0))
        edges.append(value)
    force = []
    for c in range(3):
        part = slice(start + 8 * c, start + 8 * c + 8)
        force.append(own_ref[part, :] + jnp.where(row >= 4, turn(left_ref[part, :], 4, 0), turn(right_ref[part, :], 4, 0)))
    post = collide(edges, force)
    for e in range(19):
        post_edge_ref[e] = post[e]
    east_ref[0:PLANE, :] = to_east_ref[...]
    west_ref[0:PLANE, :] = to_west_ref[...]
    for k in range(5):
        line = PLANE + 2 * k
        for half in range(2):
            at = 4 * half
            east_ref[line + half : line + half + 1, :] = post[EAST[k]][at + 3 : at + 4, :]
            west_ref[line + half : line + half + 1, :] = post[WEST[k]][at : at + 1, :]
    zero = jnp.zeros((PLANE_ROWS - PLANE - 10, 128), jnp.float32)
    east_ref[PLANE + 10 :, :] = zero
    west_ref[PLANE + 10 :, :] = zero


def stream(entries, post_ref, post_edge_ref, moved_ref, store, store_edge):
    row, lane = iotas()
    low, high = row < 4, row >= 4
    same = (low & (lane < 2)) | (high & (lane == 127))
    patches = {0: same, 1: low & (lane < 3), -1: (low & (lane == 0)) | (high & (lane >= 126))}
    low_wall, high_wall = lane >= 75, lane < 5
    for e in entries:
        cx, cy, cz = velocity_set[e]
        edge = turn(turn(post_edge_ref[e], cx, 0), cy - 5 * cz, 1)
        if cz == 1:
            edge = jnp.where(low_wall, post_edge_ref[opposite(e)], edge)
        elif cz == -1:
            edge = jnp.where(high_wall, post_edge_ref[opposite(e)], edge)
        store_edge(e, edge)
        swapped = turn(edge, 4, 0)
        for z in range(DEPTH):
            source, patch = z - cz, patches[cy]
            if 0 <= source < DEPTH:
                value = turn(post_ref[e, 8 * source : 8 * source + 8, :], cx, 0)
                if cy != 0:
                    value = turn(value, cy, 1)
                    value = jnp.where(lane == (0 if cy == 1 else 127), turn(value, 4, 0), value)
            else:
                value, patch = post_ref[opposite(e), 8 * z : 8 * z + 8, :], same
            store(e, z, jnp.where(patch, turn(swapped, -(5 * (DEPTH - 1 - z) + 2), 1), value))


def join(e, plane_ref, post_ref, post_edge_ref, before, before_edge, moved_ref, store, store_edge):
    cx, cy, cz = velocity_set[e]
    k, x = (EAST if cx == 1 else WEST).index(e), 0 if cx == 1 else 3
    row, lane = iotas((DEPTH, 128))
    _, single = iotas((1, 128))
    edges = []
    for half in range(2):
        line, at = PLANE + 2 * k + half, 4 * half + x
        edge = turn(plane_ref[line : line + 1, :], cy - 5 * cz, 1)
        if cz != 0:
            edge = jnp.where(single >= 75 if cz == 1 else single < 5, post_edge_ref[opposite(e), at : at + 1, :], edge)
        edges.append(edge)
    tiles = [plane_ref[pl.ds(32 * k + half, DEPTH, stride=2), :] for half in range(2)]
    if cy != 0:
        turned = [turn(tile, cy, 1) for tile in tiles]
        tiles = [turned[0], jnp.where(lane == 0, turned[0], turned[1])]
        if cy == -1:
            tiles = [jnp.where(lane == 127, turned[1], turned[0]), turned[1]]
    wall = row == (0 if cz == 1 else DEPTH - 1)
    place = MOVING.index(e)
    for half in range(2):
        tile = tiles[half]
        same = lane < 2 if half == 0 else lane == 127
        patch = {
            0: same, 1: lane < 3 if half == 0 else lane < 0, -1: lane == 0 if half == 0 else lane >= 126
        }[cy]
        if cz != 0:
            at = (0 if cz == 1 else 8 * DEPTH - 8) + 4 * half + x
            tile = jnp.where(wall, post_ref[opposite(e), at : at + 1, :], turn(tile, cz, 0))
            patch = (wall & same) | (jnp.logical_not(wall) & patch)
        shown = pltpu.roll(jnp.broadcast_to(edges[1 - half], (DEPTH, 128)), 51, 1, stride=5, stride_axis=0)
        moved_ref[place, pl.ds(4 * half + x, DEPTH, stride=8), :] = jnp.where(patch, shown, tile)
    row, _ = iotas()
    for z in range(DEPTH):
        part = slice(8 * z, 8 * z + 8)
        store(e, z, jnp.where(row % 4 == x, moved_ref[place, part, :], before[part, :]))
    if store_edge is not None:
        store_edge(e, jnp.where(row == x, edges[0], jnp.where(row == 4 + x, edges[1], before_edge[...])))


def stream_kernel(post_ref, post_edge_ref, dev_ref, edges_ref):
    def store(e, z, value):
        dev_ref[e, 8 * z : 8 * z + 8, :] = value

    def store_edge(e, value):
        edges_ref[e] = value

    stream(range(19), post_ref, post_edge_ref, None, store, store_edge)


def second_kernel(
    slots, blocks, columns, where_ref, chosen_ref,
    post_ref, post_edge_ref, streamed_ref, streamed_edge_ref, east_ref, west_ref, table_ref, *refs
):
    dev_ref, edges_ref, force_ref, to_right_ref, to_left_ref = refs[:5]
    share_refs, refs = refs[5 : 3 + columns], refs[3 + columns :]
    moved_ref, flow_ref, halo_ref, matrix_ref, rest_ref, total_ref, speed_ref, spot_ref = refs

    def store(e, z, value):
        dev_ref[MOVING.index(e), 8 * z : 8 * z + 8, :] = value

    def store_edge(e, value):
        edges_ref[e] = value

    def dev(e, z):
        part = slice(8 * z, 8 * z + 8)
        return streamed_ref[e, part, :] if e in STILL else dev_ref[MOVING.index(e), part, :]

    for e in MOVING:
        join(
            e, east_ref if e in EAST else west_ref, post_ref, post_edge_ref,
            streamed_ref.at[e], streamed_edge_ref.at[e], moved_ref, store, store_edge,
        )
    for e in STILL:
        edges_ref[e] = streamed_edge_ref[e]
    flow_slices(lambda z: [dev(e, z) for e in range(19)], flow_ref)
    flow_edges(edge_flow([edges_ref[e] for e in range(19)]), halo_ref)
    top = prepare_matrix(flow_ref, halo_ref, matrix_ref, rest_ref)
    unscale = couple(slots, table_ref, matrix_ref, rest_ref, total_ref, speed_ref, top)
    finish_force(unscale, total_ref, halo_ref, force_ref, to_right_ref)
    to_left_ref[0:24, :] = to_right_ref[0:24, :]
    mine = where_ref[1]

    total = spot_ref.shape[0] - 1
    spot_ref[...] = jnp.zeros_like(spot_ref)
    for n in range(slots):
        spot_ref[chosen_ref[n]] = speed_ref[n]
    filaments = total // blocks
    share = blocks // columns
    others = iter(share_refs)
    for s in range(columns):
        target, start = (to_right_ref, 24) if s == 1 else (to_left_ref, 24) if s == columns - 1 else (next(others), 0)
        owner = lax.rem(mine + s, columns)
        for f in range(filaments):
            for k in range(share):
                for c in range(3):
                    row = start + (c * share + k) * filaments + f
                    target[row : row + 1, :] = spot_ref[f * blocks + owner * share + k, c : c + 1, :]


def last_still_kernel(post_ref, post_edge_ref, dev_ref, before_ref, kept_ref, sems):
    def store(e, z, value):
        if e in STILL:
            kept_ref[STILL.index(e), 8 * z : 8 * z + 8, :] = value
        else:
            before_ref[MOVING.index(e), 8 * z : 8 * z + 8, :] = value

    copies = []
    for k, e in enumerate(STILL):
        stream((e,), post_ref, post_edge_ref, None, store, lambda e, value: None)
        copies.append(pltpu.make_async_copy(kept_ref.at[k], dev_ref.at[e], sems.at[k]))
        copies[-1].start()
    stream(MOVING, post_ref, post_edge_ref, None, store, lambda e, value: None)
    for copy in copies:
        copy.wait()


def last_kernel(
    post_ref, post_edge_ref, before_ref, east_ref, west_ref, home_ref, old_ref, dev_ref, speed_ref, moved_ref, kept_ref, sems
):
    def store(e, z, value):
        kept_ref[MOVING.index(e), 8 * z : 8 * z + 8, :] = value

    copies = [pltpu.make_async_copy(home_ref, speed_ref, sems.at[10])]
    copies[0].start()
    for k, e in enumerate(MOVING):
        plane_ref = east_ref if e in EAST else west_ref
        join(e, plane_ref, post_ref, post_edge_ref, before_ref.at[k], None, moved_ref, store, None)
        copies.append(pltpu.make_async_copy(kept_ref.at[k], dev_ref.at[e], sems.at[k]))
        copies[-1].start()
    for copy in copies:
        copy.wait()


def call(body, outs, scratch, n_smem, args, flops=0, **extra):
    spec = [pl.BlockSpec(memory_space=pltpu.SMEM)] * n_smem
    spec += [pl.BlockSpec(memory_space=pltpu.VMEM)] * (len(args) - n_smem)
    outs = [out if isinstance(out[-1], type) else (out, jnp.float32) for out in outs]
    moved = 4 * sum(math.prod(shape) for shape, _ in outs)
    options = dict(
        in_specs=spec,
        out_specs=[pl.BlockSpec(memory_space=pltpu.VMEM)] * len(outs),
        cost_estimate=pl.CostEstimate(flops=flops, bytes_accessed=2 * moved, transcendentals=0),
    )
    options.update(extra)
    return pl.pallas_call(
        body,
        out_shape=[jax.ShapeDtypeStruct(*out) for out in outs],
        scratch_shapes=scratch,
        compiler_params=pltpu.CompilerParams(vmem_limit_bytes=VMEM_LIMIT),
        **options,
    )(*args)


def ring(value, axis, step):
    count = lax.axis_size(axis)
    return lax.ppermute(value, axis, [(i, (i + step) % count) for i in range(count)])


def per_device(populations, fraction, spans, stiffness):
    depth, tile_x, tile_y = populations.shape[1:]
    columns = lax.axis_size("gy")
    span_y = float(tile_y * columns)
    filaments, _, share = fraction.shape
    blocks = spans.shape[1]
    share_blocks = share // BLOCK
    slots = max(8, 2 * filaments * blocks // columns)
    f32 = jnp.float32

    own_part = fraction.reshape(filaments, 3, share_blocks, BLOCK).transpose(1, 2, 0, 3)
    own_part = own_part.reshape(3 * share_blocks * filaments, BLOCK)

    field = (19, ROWS, 128)
    edge = (19, 8, 128)
    halves = tile_y // 128
    pop = populations.reshape(19, depth, tile_x, halves, 128).transpose(0, 1, 3, 2, 4).reshape(field)
    flat_spans = spans.transpose(0, 2, 1)
    where = jnp.stack([lax.axis_index("gx"), lax.axis_index("gy")]).astype(jnp.int32)

    force_shape = (3, ROWS, 128)
    share_rows = 3 * share_blocks * filaments
    inside, anywhere = pl.BlockSpec(memory_space=pltpu.VMEM), pl.BlockSpec(memory_space=pl.ANY)
    flow, payload = call(
        flow_kernel, [force_shape, (share_rows + 24, BLOCK)], [pltpu.SemaphoreType.DMA], 0, (pop, own_part),
        in_specs=[inside, anywhere],
    )
    parts = [payload] + [ring(payload, "gy", s) for s in range(1, columns)]
    edge_shapes = [edge, (EDGE_ROWS, 128), (EDGE_ROWS, 128)]
    own_edge, right_edge, left_edge, chosen = call(
        edge_kernel, edge_shapes + [((slots + 8,), jnp.int32)], [], 2, (flat_spans, where, pop),
        out_specs=[inside] * 3 + [pl.BlockSpec(memory_space=pltpu.SMEM)],
    )

    table_shape = (slots, 16, BLOCK)
    coupling = [
        pltpu.VMEM(force_shape, f32),
        pltpu.VMEM((3 * FIELDS * DEPTH, 256), jnp.bfloat16),
        pltpu.VMEM((3 * FIELDS * DEPTH, 256), f32),
        pltpu.VMEM((3 * FIELDS * DEPTH, 256), f32),
        pltpu.VMEM((slots, 8, BLOCK), f32),
    ]
    force, to_right, to_left, table = call(
        functools.partial(first_kernel, span_y, slots, filaments, columns),
        [force_shape, (EDGE_ROWS + 24, 128), (EDGE_ROWS + 24, 128), table_shape],
        coupling + [pltpu.VMEM((filaments * blocks * 8 + 8, BLOCK), f32), pltpu.VMEM((slots * 8, BLOCK), f32)],
        4,
        (flat_spans, where, chosen, stiffness, flow, right_edge, left_edge, *parts),
    )

    moving = (len(MOVING), ROWS, 128)
    moved = pltpu.VMEM(moving, f32)

    def collision(first, dev, edges, force, to_right, to_left):
        left, right = ring(to_right, "gy", 1), ring(to_left, "gy", -1)
        post, east, west = call(
            functools.partial(collide_kernel, first), [field, (PLANE, 128), (PLANE, 128)], [], 0, (*dev, force)
        )
        post_edge, east, west = call(
            functools.partial(collide_edge_kernel, first), [edge, (PLANE_ROWS, 128), (PLANE_ROWS, 128)], [], 0,
            (edges, to_right, left, right, east, west),
        )
        return post, post_edge, ring(east, "gx", 1), ring(west, "gx", -1), left, right

    post, post_edge, east, west, _, _ = collision(True, (pop,), own_edge, force, to_right, to_left)
    streamed, streamed_edge = call(stream_kernel, [field, edge], [], 0, (post, post_edge))
    dev, edges, force, to_right, to_left, *chunks = call(
        functools.partial(second_kernel, slots, blocks, columns),
        [moving, edge, force_shape] + [(24 + share_rows, BLOCK)] * 2 + [(share_rows, BLOCK)] * (columns - 2),
        [moved, pltpu.VMEM(force_shape, f32)] + coupling + [pltpu.VMEM((filaments * blocks + 1, 8, BLOCK), f32)],
        2,
        (where, chosen, post, post_edge, streamed, streamed_edge, east, west, table),
    )
    post, post_edge, east, west, left, right = collision(
        False, (streamed, dev), edges, force, to_right, to_left
    )
    speed = chunks[0] + left[24:] + right[24:]
    for s in range(2, columns - 1):
        speed = speed + ring(chunks[s - 1], "gy", s)

    dev, before = call(
        last_still_kernel, [field, moving],
        [pltpu.VMEM((9, ROWS, 128), f32), pltpu.SemaphoreType.DMA((9,))],
        0, (post, post_edge), out_specs=[anywhere, inside],
    )
    dev, speed = call(
        last_kernel, [field, (share_rows, BLOCK)],
        [moved, pltpu.VMEM(moving, f32), pltpu.SemaphoreType.DMA((11,))],
        0, (post, post_edge, before, east, west, speed, dev),
        in_specs=[inside] * 6 + [anywhere], out_specs=[anywhere] * 2, input_output_aliases={6: 0},
    )
    speed = speed.reshape(3, share_blocks, filaments, BLOCK).transpose(2, 0, 1, 3).reshape(fraction.shape)
    dev = dev.reshape(19, depth, halves, tile_x, 128).transpose(0, 1, 3, 2, 4).reshape(populations.shape)
    return dev, speed


def solution(mesh):
    placed = (P(None, None, "gx", "gy"), P("gx", None, "gy"), P("gx", None, None), P("gx"))
    return jax.shard_map(
        per_device,
        mesh=mesh,
        in_specs=placed,
        out_specs=(P(None, None, "gx", "gy"), P("gx", None, "gy")),
        check_vma=False,
    )
```

```python
import functools
import math

import jax
import jax.numpy as jnp
from jax import lax
from jax.experimental import pallas as pl
from jax.experimental.pallas import tpu as pltpu
from jax.sharding import PartitionSpec as P

STEPS = 2

velocity_set = (
    (0, 0, 0),
    (1, 0, 0),
    (-1, 0, 0),
    (0, 1, 0),
    (0, -1, 0),
    (0, 0, 1),
    (0, 0, -1),
    (1, 1, 0),
    (-1, -1, 0),
    (1, -1, 0),
    (-1, 1, 0),
    (1, 0, 1),
    (-1, 0, -1),
    (1, 0, -1),
    (-1, 0, 1),
    (0, 1, 1),
    (0, -1, -1),
    (0, 1, -1),
    (0, -1, 1),
)
lattice_weight = (1.0 / 3.0,) + (1.0 / 18.0,) * 6 + (1.0 / 36.0,) * 12
unit = 0.002
feedback_gain = 2.0
EAST = tuple(i for i in range(19) if velocity_set[i][0] == 1)
WEST = tuple(i for i in range(19) if velocity_set[i][0] == -1)
STILL = tuple(i for i in range(19) if velocity_set[i][0] == 0)
MOVING = EAST + WEST

DEPTH = 16
ROWS = DEPTH * 8
BLOCK = 128
GROUP = 32
PLANE = 160
PLANE_ROWS = 176
FIELDS = 9
EDGE_ROWS = 80
TINY = 1e-30
FINE = jnp.float8_e4m3fn
VMEM_LIMIT = 40 * 1024 * 1024


def opposite(entry):
    return entry + 1 if entry % 2 == 1 else entry - 1


def iotas(shape=(8, 128)):
    return lax.broadcasted_iota(jnp.int32, shape, 0), lax.broadcasted_iota(jnp.int32, shape, 1)


def turn(value, shift, axis):
    shift = shift % value.shape[axis]
    return pltpu.roll(value, shift, axis) if shift else value


def pack_edges(slices):
    _, lane = iotas()
    total = jnp.zeros((8, 128), jnp.float32)
    for z in range(DEPTH):
        at = 5 * (DEPTH - 1 - z)
        total = jnp.where((lane >= at) & (lane < at + 5), turn(slices(z), at + 2, 1), total)
    return total


def signed_sum(terms):
    total = None
    for sign, value in terms:
        if total is None:
            total = value if sign > 0 else -value
        else:
            total = total + value if sign > 0 else total - value
    return total


def dot_c(vector, parts):
    return signed_sum([(vector[a], parts[a]) for a in range(3) if vector[a] != 0])


def moments(dev):
    total = dev[0]
    for entry in range(1, 19):
        total = total + dev[entry]
    momentum = [
        signed_sum([(velocity_set[e][a], dev[e]) for e in range(19) if velocity_set[e][a] != 0]) for a in range(3)
    ]
    return total, momentum, 1.0 + unit * total


def collide(dev, force):
    total, momentum, dens = moments(dev)
    inverse = 1.0 / dens
    vel = [(momentum[a] + 0.5 * force[a]) * inverse for a in range(3)]
    odd_base = [3.75 * momentum[a] + 3.0 * force[a] for a in range(3)]
    even_base = [5.625 * momentum[a] + 6.1875 * force[a] for a in range(3)]
    along = vel[0] * even_base[0] + vel[1] * even_base[1] + vel[2] * even_base[2]
    base = 1.25 * total - (unit / 3.0) * along
    post = [lattice_weight[0] * base - 0.25 * dev[0]]
    scaled = [unit * vel[a] for a in range(3)]
    for entry in range(1, 19, 2):
        vector, weight = velocity_set[entry], lattice_weight[entry]
        odd = weight * dot_c(vector, odd_base)
        even = weight * (base + dot_c(vector, scaled) * dot_c(vector, even_base))
        post.append((even + odd) - 0.25 * dev[entry])
        post.append((even - odd) - 0.25 * dev[entry + 1])
    return post


def merge_edges(own, left, right):
    row, lane = iotas()
    j = lane % 5
    from_left = (row >= 4) & (j < 2)
    from_right = (row < 4) & (j >= 2)
    return jnp.where(from_left, left, jnp.where(from_right, right, turn(own, 4, 0)))


def flow_kernel(pop_ref, part_ref, flow_ref, payload_ref, sem):
    rows = part_ref.shape[0]
    copy = pltpu.make_async_copy(part_ref, payload_ref.at[pl.ds(0, rows)], sem)
    copy.start()
    flow_slices(lambda z: [pop_ref[e, 8 * z : 8 * z + 8, :] for e in range(19)], flow_ref)
    for c in range(3):
        payload_ref[rows + 8 * c : rows + 8 * c + 8, :] = pack_edges(lambda z: flow_ref[c, 8 * z : 8 * z + 8, :])
    copy.wait()


def edge_kernel(spans_ref, where_ref, pop_ref, edge_ref, to_right_ref, to_left_ref, chosen_ref):
    row, _ = iotas()
    filaments, _, blocks = spans_ref.shape
    slots, mine = chosen_ref.shape[0] - 8, where_ref[1]
    for n in range(slots):
        chosen_ref[n] = filaments * blocks
    count = jnp.int32(0)
    for f in range(filaments):
        for k in range(blocks):
            chosen_ref[count] = f * blocks + k
            count = count + (spans_ref[f, 0, k] == mine).astype(jnp.int32)
    chosen_ref[count] = filaments * blocks
    chosen_ref[slots] = count
    edges = []
    for e in range(19):
        edges.append(pack_edges(lambda z: pop_ref[e, 8 * z : 8 * z + 8, :]))
        edge_ref[e] = edges[e]
    for k in range(10):
        other = turn(edges[2 * k + 1], 4, 0) if k < 9 else edges[2 * k]
        to_right_ref[8 * k : 8 * k + 8, :] = jnp.where(row >= 4, edges[2 * k], other)
        to_left_ref[8 * k : 8 * k + 8, :] = jnp.where(row < 4, edges[2 * k], other)


def shifted(tiles, shift):
    lane = lax.broadcasted_iota(jnp.int32, tiles[0].shape, 1)
    if shift == 0:
        return tiles[1:-1]
    rolled = [turn(tile, -shift, 1) for tile in tiles]
    if shift > 0:
        return [jnp.where(lane >= 128 - shift, rolled[i + 1], rolled[i]) for i in range(1, len(tiles) - 1)]
    return [jnp.where(lane < -shift, rolled[i - 1], rolled[i]) for i in range(1, len(tiles) - 1)]


def basis_fields(four):
    return (
        0.25 * ((four[0] + four[2]) + (four[1] + four[3])),
        0.25 * (four[2] - four[0]),
        0.25 * (four[1] - four[3]),
    )


def basis_cells(three):
    one, sine, cosine = three
    return one - sine, one + cosine, one + sine, one - cosine


def largest(value):
    return jnp.max(jnp.max(jnp.abs(value), axis=1, keepdims=True), axis=0, keepdims=True)


def prepare_matrix(flow_ref, halo_ref, matrix_ref, rest_ref):
    top = None
    for c in range(3):
        for z in range(DEPTH):
            part = slice(8 * z, 8 * z + 8)
            both = jnp.maximum(jnp.abs(flow_ref[c, part, :]), jnp.abs(halo_ref[c, part, :]))
            top = both if top is None else jnp.maximum(top, both)
    top = jnp.maximum(largest(top), TINY)
    scale = 2.0**15 / top
    for c in range(3):
        per_x = []
        for x in range(4):
            tiles = [
                halo_ref[c, pl.ds(4 + x, DEPTH, stride=8), :],
                flow_ref[c, pl.ds(x, DEPTH, stride=8), :],
                flow_ref[c, pl.ds(4 + x, DEPTH, stride=8), :],
                halo_ref[c, pl.ds(x, DEPTH, stride=8), :],
            ]
            per_x.append(tiles)
        by_basis = [basis_fields([per_x[x][t] for x in range(4)]) for t in range(4)]
        for xf in range(3):
            tiles = [by_basis[t][xf] for t in range(4)]
            four = [shifted(tiles, s) for s in (-1, 0, 1, 2)]
            for half in range(2):
                fields = basis_fields([four[s][half] for s in range(4)])
                columns = slice(half * 128, half * 128 + 128)
                for yf in range(3):
                    row = ((c * 3 + yf) * 3 + xf) * DEPTH
                    value = fields[yf] * scale
                    high = value.astype(jnp.bfloat16)
                    matrix_ref[row : row + DEPTH, columns] = high
                    rest_ref[row : row + DEPTH, columns] = value - high.astype(jnp.float32)
    return top


def couple(slots, table_ref, matrix_ref, rest_ref, total_ref, speed_ref, top):
    group = min(GROUP, slots)
    unscale = top * 2.0**-15
    bound = jnp.maximum(table_ref[0, 12:13, 0:1] + feedback_gain * top, TINY)
    scale = 2.0**17 / bound
    column = lax.broadcasted_iota(jnp.int32, (256, BLOCK), 0).astype(jnp.float32).astype(jnp.bfloat16)
    one, none = jnp.bfloat16(1), jnp.bfloat16(0)
    z_cell = lax.broadcasted_iota(jnp.int32, (DEPTH, BLOCK), 0).astype(jnp.float32)
    rest = rest_ref[...].astype(FINE)

    def body(step):
        first = step * group
        hot, weight_z, coef = [], [], []
        for g in range(group):
            slot = first + g
            q = lambda k: table_ref[slot, k : k + 1, :]
            hot.append(jnp.where(column == q(0).astype(jnp.bfloat16), one, none))
            gap = z_cell - q(5)
            sine, cosine = q(6), q(7)
            weight_z.append(
                jnp.where(
                    gap == -1.0,
                    0.25 - 0.25 * sine,
                    jnp.where(
                        gap == 0.0,
                        0.25 + 0.25 * cosine,
                        jnp.where(gap == 1.0, 0.25 + 0.25 * sine, jnp.where(gap == 2.0, 0.25 - 0.25 * cosine, 0.0)),
                    ),
                )
            )
            by, bx = (None, q(1), q(2)), (None, q(3), q(4))
            coef.append(
                [
                    [by[i] if bx[k] is None else bx[k] if by[i] is None else by[i] * bx[k] for k in range(3)]
                    for i in range(3)
                ]
            )
        coarse = jnp.concatenate(hot, axis=1)
        fine = coarse.astype(FINE)
        across = jnp.dot(matrix_ref[...], coarse, preferred_element_type=jnp.float32)
        across += jnp.dot(rest, fine, preferred_element_type=jnp.float32)
        spread_high, spread_low = [], []
        for g in range(group):
            slot = first + g
            columns = slice(g * BLOCK, (g + 1) * BLOCK)
            pieces = []
            for c in range(3):
                sums = None
                for yf in range(3):
                    for xf in range(3):
                        row = ((c * 3 + yf) * 3 + xf) * DEPTH
                        term = across[row : row + DEPTH, columns]
                        factor = coef[g][yf][xf]
                        term = term if factor is None else term * factor
                        sums = term if sums is None else sums + term
                speed = jnp.sum(sums * weight_z[g], axis=0, keepdims=True) * unscale
                speed_ref[slot, c : c + 1, :] = speed
                push = (table_ref[slot, 8 + c : 9 + c, :] - feedback_gain * speed) * table_ref[slot, 11:12, :] * scale
                for yf in range(3):
                    for xf in range(3):
                        factor = coef[g][yf][xf]
                        pieces.append(weight_z[g] * (push if factor is None else push * factor))
            piece = jnp.concatenate(pieces, axis=0)
            high = piece.astype(jnp.bfloat16)
            spread_high.append(high)
            spread_low.append((piece - high.astype(jnp.float32)).astype(FINE))
        across_rows = (((1,), (1,)), ((), ()))
        total = lax.dot_general(
            jnp.concatenate(spread_high, axis=1), coarse, across_rows, preferred_element_type=jnp.float32
        ) + lax.dot_general(
            jnp.concatenate(spread_low, axis=1), fine, across_rows, preferred_element_type=jnp.float32
        )
        total_ref[...] = total if step == 0 else total_ref[...] + total

    for step in range(slots // group):
        body(step)
    return bound * 2.0**-21


def finish_force(unscale, total_ref, halo_ref, force_ref, force_edge_ref, start=0):
    lane = lax.broadcasted_iota(jnp.int32, (DEPTH, 128), 1)
    zero = jnp.zeros((DEPTH, 128), jnp.float32)
    for c in range(3):
        by_basis = []
        for xf in range(3):
            field = []
            for yf in range(3):
                row = ((c * 3 + yf) * 3 + xf) * DEPTH
                field.append([total_ref[row : row + DEPTH, 0:128], total_ref[row : row + DEPTH, 128:256]])
            cells = [basis_cells([field[yf][half] for yf in range(3)]) for half in range(2)]
            sums = None
            for k, shift in enumerate((1, 0, -1, -2)):
                low, high = (turn(cells[half][k], -shift, 1) for half in range(2))
                if shift == 1:
                    last = lane == 127
                    tiles = [jnp.where(last, low, zero), jnp.where(last, high, low), jnp.where(last, zero, high), zero]
                elif shift == 0:
                    tiles = [zero, low, high, zero]
                else:
                    begin = lane < -shift
                    tiles = [zero, jnp.where(begin, zero, low), jnp.where(begin, low, high), jnp.where(begin, high, zero)]
                sums = tiles if sums is None else [a + b for a, b in zip(sums, tiles)]
            by_basis.append(sums)
        by_x = [basis_cells([by_basis[xf][t] * unscale for xf in range(3)]) for t in range(4)]
        for x in range(4):
            left, low, high, right = (by_x[t][x] for t in range(4))
            force_ref[c, pl.ds(x, DEPTH, stride=8), :] = low
            force_ref[c, pl.ds(4 + x, DEPTH, stride=8), :] = high
            halo_ref[c, pl.ds(4 + x, DEPTH, stride=8), :] = jnp.where(lane >= 64, left, low)
            halo_ref[c, pl.ds(x, DEPTH, stride=8), :] = jnp.where(lane >= 64, high, right)
        row = start + 8 * c
        force_edge_ref[row : row + 8, :] = pack_edges(lambda z: halo_ref[c, 8 * z : 8 * z + 8, :])


def flow_slices(load, flow_ref):
    for z in range(DEPTH):
        total, momentum, dens = moments(load(z))
        inverse = 1.0 / dens
        for c in range(3):
            flow_ref[c, 8 * z : 8 * z + 8, :] = momentum[c] * inverse


def edge_flow(edges):
    total, momentum, dens = moments(edges)
    inverse = 1.0 / dens
    return [momentum[c] * inverse for c in range(3)]


def flow_edges(flows, halo_ref):
    for c in range(3):
        flow = flows[c]
        for z in range(DEPTH):
            halo_ref[c, 8 * z : 8 * z + 8, :] = turn(flow, -(5 * (DEPTH - 1 - z) + 2), 1)


def gather_markers(span_y, slots, filaments, share, spans_ref, where_ref, chosen_ref, stiff_ref, part_refs, places_ref, picked_ref, table_ref):
    columns = len(part_refs)
    blocks = share * columns
    block, lane = iotas((blocks, BLOCK))
    anchor = (where_ref[0] * 4).astype(jnp.float32)
    mine = where_ref[1]
    tile_start = (mine * 256).astype(jnp.float32)
    for s in range(columns):
        source = lax.rem(mine + (columns - s), columns)
        for f in range(filaments):
            for k in range(share):
                index = f * blocks + source * share + k
                span = (spans_ref[f, 0, source * share + k] * 256).astype(jnp.float32)
                row = lambda c: part_refs[s][(c * share + k) * filaments + f][None, :]
                start = pl.multiple_of(index * 8, 8)
                three = [anchor + 1.0 + row(0) * (4 - 3.01), span + row(1) * 256.0, 1.0 + row(2) * (DEPTH - 3.01)]
                places_ref[pl.ds(start, 8), :] = jnp.concatenate(three + [jnp.zeros((5, BLOCK), jnp.float32)], axis=0)
    for f in range(filaments):
        factor = stiff_ref[f].astype(jnp.float32) * (1.0 / 256.0)
        start = f * blocks * 8
        places = [places_ref[pl.ds(start + c, blocks, stride=8), :] for c in range(3)]
        for c in range(3):
            ahead = turn(places[c], -1, 1)
            ahead = jnp.where(lane == BLOCK - 1, turn(ahead, -1, 0), ahead) - places[c]
            if c == 1:
                half = 0.5 * span_y
                ahead = jnp.where(ahead > half, ahead - span_y, jnp.where(ahead < -half, ahead + span_y, ahead))
            ahead = jnp.where((lane == BLOCK - 1) & (block == blocks - 1), 0.0, ahead)
            behind = turn(ahead, 1, 1)
            behind = jnp.where(lane == 0, turn(behind, 1, 0), behind)
            places_ref[pl.ds(start + 3 + c, blocks, stride=8), :] = (ahead - behind) * factor
        places_ref[pl.ds(start, blocks, stride=8), :] = places[0] - anchor
        places_ref[pl.ds(start + 1, blocks, stride=8), :] = places[1] - tile_start
    total = filaments * blocks
    places_ref[pl.ds(total * 8, 8), :] = jnp.zeros((8, BLOCK), jnp.float32)
    for n in range(slots):
        picked_ref[8 * n : 8 * n + 8, :] = places_ref[pl.ds(pl.multiple_of(chosen_ref[n] * 8, 8), 8), :]
    count = chosen_ref[slots]
    got = lambda k: picked_ref[pl.ds(k, slots, stride=8), :]
    slot, _ = iotas((slots, BLOCK))

    def put(k, value):
        table_ref[:, k, :] = value

    def basis(t):
        square = t * t
        sine = cosine = None
        for k in range(6, -1, -1):
            a, b = ((-1) ** k * (0.5 * math.pi) ** n / math.factorial(n) for n in (2 * k + 1, 2 * k))
            sine = a if sine is None else sine * square + a
            cosine = b if cosine is None else cosine * square + b
        return sine * t, cosine

    y = got(1)
    base = jnp.minimum(jnp.floor(y), 255.0)
    put(0, base)
    sine, cosine = basis(y - base)
    put(1, sine)
    put(2, cosine)
    sine, cosine = basis(got(0) - 1.0)
    put(3, sine)
    put(4, cosine)
    z = got(2)
    base = jnp.floor(z)
    put(5, base)
    sine, cosine = basis(z - base)
    put(6, sine)
    put(7, cosine)
    bends = [got(3 + c) for c in range(3)]
    for c in range(3):
        put(8 + c, bends[c])
    put(11, jnp.where(slot < count, 1.0, 0.0))
    top = largest(jnp.maximum(jnp.maximum(jnp.abs(bends[0]), jnp.abs(bends[1])), jnp.abs(bends[2])))
    table_ref[0, 12:13, :] = jnp.broadcast_to(top, (1, BLOCK))


def first_kernel(span_y, slots, filaments, columns, spans_ref, where_ref, chosen_ref, stiff_ref, flow_ref, right_edge_ref, left_edge_ref, *refs):
    part_refs, refs = refs[:columns], refs[columns:]
    force_ref, to_right_ref, to_left_ref, table_ref = refs[:4]
    halo_ref, matrix_ref, rest_ref, total_ref, speed_ref, places_ref, picked_ref = refs[4:]
    share = spans_ref.shape[2] // columns
    to_right_ref[0:EDGE_ROWS, :] = right_edge_ref[...]
    to_left_ref[0:EDGE_ROWS, :] = left_edge_ref[...]
    gather_markers(
        span_y, slots, filaments, share, spans_ref, where_ref, chosen_ref, stiff_ref, part_refs, places_ref, picked_ref, table_ref
    )
    flows = []
    for c in range(3):
        start = 3 * share * filaments + 8 * c
        flows.append(merge_edges(*(part_refs[s][start : start + 8, :] for s in (0, 1, -1))))
    flow_edges(flows, halo_ref)
    top = prepare_matrix(flow_ref, halo_ref, matrix_ref, rest_ref)
    unscale = couple(slots, table_ref, matrix_ref, rest_ref, total_ref, speed_ref, top)
    finish_force(unscale, total_ref, halo_ref, force_ref, to_right_ref, EDGE_ROWS)
    to_left_ref[EDGE_ROWS:, :] = to_right_ref[EDGE_ROWS:, :]


def collide_kernel(first, *refs):
    dev_refs, (force_ref, post_ref, east_ref, west_ref) = refs[:-4], refs[-4:]

    def dev(e, part):
        if first:
            return dev_refs[0][e, part, :]
        return dev_refs[0][e, part, :] if e in STILL else dev_refs[1][MOVING.index(e), part, :]

    for z in range(DEPTH):
        part = slice(8 * z, 8 * z + 8)
        post = collide([dev(e, part) for e in range(19)], [force_ref[c, part, :] for c in range(3)])
        for e in range(19):
            post_ref[e, part, :] = post[e]
    for k in range(5):
        east_ref[32 * k : 32 * k + 32, :] = post_ref[EAST[k], pl.ds(3, 32, stride=4), :]
        west_ref[32 * k : 32 * k + 32, :] = post_ref[WEST[k], pl.ds(0, 32, stride=4), :]


def collide_edge_kernel(first, edge_ref, own_ref, left_ref, right_ref, to_east_ref, to_west_ref, post_edge_ref, east_ref, west_ref):
    row, _ = iotas()
    start = EDGE_ROWS if first else 0
    edges = []
    for e in range(19):
        value = edge_ref[e]
        if first:
            part, shift = slice(8 * (e // 2), 8 * (e // 2) + 8), 4 * (e % 2)
            value = merge_edges(value, turn(left_ref[part, :], shift, 0), turn(right_ref[part, :], shift, 0))
        edges.append(value)
    force = []
    for c in range(3):
        part = slice(start + 8 * c, start + 8 * c + 8)
        force.append(own_ref[part, :] + jnp.where(row >= 4, turn(left_ref[part, :], 4, 0), turn(right_ref[part, :], 4, 0)))
    post = collide(edges, force)
    for e in range(19):
        post_edge_ref[e] = post[e]
    east_ref[0:PLANE, :] = to_east_ref[...]
    west_ref[0:PLANE, :] = to_west_ref[...]
    for k in range(5):
        line = PLANE + 2 * k
        for half in range(2):
            at = 4 * half
            east_ref[line + half : line + half + 1, :] = post[EAST[k]][at + 3 : at + 4, :]
            west_ref[line + half : line + half + 1, :] = post[WEST[k]][at : at + 1, :]
    zero = jnp.zeros((PLANE_ROWS - PLANE - 10, 128), jnp.float32)
    east_ref[PLANE + 10 :, :] = zero
    west_ref[PLANE + 10 :, :] = zero


def stream(entries, post_ref, post_edge_ref, moved_ref, store, store_edge):
    row, lane = iotas()
    low, high = row < 4, row >= 4
    same = (low & (lane < 2)) | (high & (lane == 127))
    patches = {0: same, 1: low & (lane < 3), -1: (low & (lane == 0)) | (high & (lane >= 126))}
    low_wall, high_wall = lane >= 75, lane < 5
    for e in entries:
        cx, cy, cz = velocity_set[e]
        edge = turn(turn(post_edge_ref[e], cx, 0), cy - 5 * cz, 1)
        if cz == 1:
            edge = jnp.where(low_wall, post_edge_ref[opposite(e)], edge)
        elif cz == -1:
            edge = jnp.where(high_wall, post_edge_ref[opposite(e)], edge)
        store_edge(e, edge)
        swapped = turn(edge, 4, 0)
        for z in range(DEPTH):
            source, patch = z - cz, patches[cy]
            if 0 <= source < DEPTH:
                value = turn(post_ref[e, 8 * source : 8 * source + 8, :], cx, 0)
                if cy != 0:
                    value = turn(value, cy, 1)
                    value = jnp.where(lane == (0 if cy == 1 else 127), turn(value, 4, 0), value)
            else:
                value, patch = post_ref[opposite(e), 8 * z : 8 * z + 8, :], same
            store(e, z, jnp.where(patch, turn(swapped, -(5 * (DEPTH - 1 - z) + 2), 1), value))


def join(e, plane_ref, post_ref, post_edge_ref, before, before_edge, moved_ref, store, store_edge):
    cx, cy, cz = velocity_set[e]
    k, x = (EAST if cx == 1 else WEST).index(e), 0 if cx == 1 else 3
    row, lane = iotas((DEPTH, 128))
    _, single = iotas((1, 128))
    edges = []
    for half in range(2):
        line, at = PLANE + 2 * k + half, 4 * half + x
        edge = turn(plane_ref[line : line + 1, :], cy - 5 * cz, 1)
        if cz != 0:
            edge = jnp.where(single >= 75 if cz == 1 else single < 5, post_edge_ref[opposite(e), at : at + 1, :], edge)
        edges.append(edge)
    tiles = [plane_ref[pl.ds(32 * k + half, DEPTH, stride=2), :] for half in range(2)]
    if cy != 0:
        turned = [turn(tile, cy, 1) for tile in tiles]
        tiles = [turned[0], jnp.where(lane == 0, turned[0], turned[1])]
        if cy == -1:
            tiles = [jnp.where(lane == 127, turned[1], turned[0]), turned[1]]
    wall = row == (0 if cz == 1 else DEPTH - 1)
    place = MOVING.index(e)
    for half in range(2):
        tile = tiles[half]
        same = lane < 2 if half == 0 else lane == 127
        patch = {
            0: same, 1: lane < 3 if half == 0 else lane < 0, -1: lane == 0 if half == 0 else lane >= 126
        }[cy]
        if cz != 0:
            at = (0 if cz == 1 else 8 * DEPTH - 8) + 4 * half + x
            tile = jnp.where(wall, post_ref[opposite(e), at : at + 1, :], turn(tile, cz, 0))
            patch = (wall & same) | (jnp.logical_not(wall) & patch)
        shown = pltpu.roll(jnp.broadcast_to(edges[1 - half], (DEPTH, 128)), 51, 1, stride=5, stride_axis=0)
        moved_ref[place, pl.ds(4 * half + x, DEPTH, stride=8), :] = jnp.where(patch, shown, tile)
    row, _ = iotas()
    for z in range(DEPTH):
        part = slice(8 * z, 8 * z + 8)
        store(e, z, jnp.where(row % 4 == x, moved_ref[place, part, :], before[part, :]))
    if store_edge is not None:
        store_edge(e, jnp.where(row == x, edges[0], jnp.where(row == 4 + x, edges[1], before_edge[...])))


def stream_kernel(post_ref, post_edge_ref, dev_ref, edges_ref):
    def store(e, z, value):
        dev_ref[e, 8 * z : 8 * z + 8, :] = value

    def store_edge(e, value):
        edges_ref[e] = value

    stream(range(19), post_ref, post_edge_ref, None, store, store_edge)


def second_kernel(
    slots, blocks, columns, where_ref, chosen_ref,
    post_ref, post_edge_ref, streamed_ref, streamed_edge_ref, east_ref, west_ref, table_ref, *refs
):
    dev_ref, edges_ref, force_ref, to_right_ref, to_left_ref = refs[:5]
    share_refs, refs = refs[5 : 3 + columns], refs[3 + columns :]
    moved_ref, flow_ref, halo_ref, matrix_ref, rest_ref, total_ref, speed_ref, spot_ref = refs

    def store(e, z, value):
        dev_ref[MOVING.index(e), 8 * z : 8 * z + 8, :] = value

    def store_edge(e, value):
        edges_ref[e] = value

    def dev(e, z):
        part = slice(8 * z, 8 * z + 8)
        return streamed_ref[e, part, :] if e in STILL else dev_ref[MOVING.index(e), part, :]

    for e in MOVING:
        join(
            e, east_ref if e in EAST else west_ref, post_ref, post_edge_ref,
            streamed_ref.at[e], streamed_edge_ref.at[e], moved_ref, store, store_edge,
        )
    for e in STILL:
        edges_ref[e] = streamed_edge_ref[e]
    flow_slices(lambda z: [dev(e, z) for e in range(19)], flow_ref)
    flow_edges(edge_flow([edges_ref[e] for e in range(19)]), halo_ref)
    top = prepare_matrix(flow_ref, halo_ref, matrix_ref, rest_ref)
    unscale = couple(slots, table_ref, matrix_ref, rest_ref, total_ref, speed_ref, top)
    finish_force(unscale, total_ref, halo_ref, force_ref, to_right_ref)
    to_left_ref[0:24, :] = to_right_ref[0:24, :]
    mine = where_ref[1]

    total = spot_ref.shape[0] - 1
    spot_ref[...] = jnp.zeros_like(spot_ref)
    for n in range(slots):
        spot_ref[chosen_ref[n]] = speed_ref[n]
    filaments = total // blocks
    share = blocks // columns
    others = iter(share_refs)
    for s in range(columns):
        target, start = (to_right_ref, 24) if s == 1 else (to_left_ref, 24) if s == columns - 1 else (next(others), 0)
        owner = lax.rem(mine + s, columns)
        for f in range(filaments):
            for k in range(share):
                for c in range(3):
                    row = start + (c * share + k) * filaments + f
                    target[row : row + 1, :] = spot_ref[f * blocks + owner * share + k, c : c + 1, :]


def last_still_kernel(post_ref, post_edge_ref, dev_ref, before_ref, kept_ref, sems):
    def store(e, z, value):
        if e in STILL:
            kept_ref[STILL.index(e), 8 * z : 8 * z + 8, :] = value
        else:
            before_ref[MOVING.index(e), 8 * z : 8 * z + 8, :] = value

    copies = []
    for k, e in enumerate(STILL):
        stream((e,), post_ref, post_edge_ref, None, store, lambda e, value: None)
        copies.append(pltpu.make_async_copy(kept_ref.at[k], dev_ref.at[e], sems.at[k]))
        copies[-1].start()
    stream(MOVING, post_ref, post_edge_ref, None, store, lambda e, value: None)
    for copy in copies:
        copy.wait()


def last_kernel(
    post_ref, post_edge_ref, before_ref, east_ref, west_ref, home_ref, old_ref, dev_ref, speed_ref, moved_ref, kept_ref, sems
):
    def store(e, z, value):
        kept_ref[MOVING.index(e), 8 * z : 8 * z + 8, :] = value

    copies = [pltpu.make_async_copy(home_ref, speed_ref, sems.at[10])]
    copies[0].start()
    for k, e in enumerate(MOVING):
        plane_ref = east_ref if e in EAST else west_ref
        join(e, plane_ref, post_ref, post_edge_ref, before_ref.at[k], None, moved_ref, store, None)
        copies.append(pltpu.make_async_copy(kept_ref.at[k], dev_ref.at[e], sems.at[k]))
        copies[-1].start()
    for copy in copies:
        copy.wait()


def call(body, outs, scratch, n_smem, args, flops=0, **extra):
    spec = [pl.BlockSpec(memory_space=pltpu.SMEM)] * n_smem
    spec += [pl.BlockSpec(memory_space=pltpu.VMEM)] * (len(args) - n_smem)
    outs = [out if isinstance(out[-1], type) else (out, jnp.float32) for out in outs]
    moved = 4 * sum(math.prod(shape) for shape, _ in outs)
    options = dict(
        in_specs=spec,
        out_specs=[pl.BlockSpec(memory_space=pltpu.VMEM)] * len(outs),
        cost_estimate=pl.CostEstimate(flops=flops, bytes_accessed=2 * moved, transcendentals=0),
    )
    options.update(extra)
    return pl.pallas_call(
        body,
        out_shape=[jax.ShapeDtypeStruct(*out) for out in outs],
        scratch_shapes=scratch,
        compiler_params=pltpu.CompilerParams(vmem_limit_bytes=VMEM_LIMIT),
        **options,
    )(*args)


def ring(value, axis, step):
    count = lax.axis_size(axis)
    return lax.ppermute(value, axis, [(i, (i + step) % count) for i in range(count)])


def per_device(populations, fraction, spans, stiffness):
    depth, tile_x, tile_y = populations.shape[1:]
    columns = lax.axis_size("gy")
    span_y = float(tile_y * columns)
    filaments, _, share = fraction.shape
    blocks = spans.shape[1]
    share_blocks = share // BLOCK
    slots = max(8, 2 * filaments * blocks // columns)
    f32 = jnp.float32

    own_part = fraction.reshape(filaments, 3, share_blocks, BLOCK).transpose(1, 2, 0, 3)
    own_part = own_part.reshape(3 * share_blocks * filaments, BLOCK)

    field = (19, ROWS, 128)
    edge = (19, 8, 128)
    halves = tile_y // 128
    pop = populations.reshape(19, depth, tile_x, halves, 128).transpose(0, 1, 3, 2, 4).reshape(field)
    flat_spans = spans.transpose(0, 2, 1)
    where = jnp.stack([lax.axis_index("gx"), lax.axis_index("gy")]).astype(jnp.int32)

    force_shape = (3, ROWS, 128)
    share_rows = 3 * share_blocks * filaments
    inside, anywhere = pl.BlockSpec(memory_space=pltpu.VMEM), pl.BlockSpec(memory_space=pl.ANY)
    flow, payload = call(
        flow_kernel, [force_shape, (share_rows + 24, BLOCK)], [pltpu.SemaphoreType.DMA], 0, (pop, own_part),
        in_specs=[inside, anywhere],
    )
    parts = [payload] + [ring(payload, "gy", s) for s in range(1, columns)]
    edge_shapes = [edge, (EDGE_ROWS, 128), (EDGE_ROWS, 128)]
    own_edge, right_edge, left_edge, chosen = call(
        edge_kernel, edge_shapes + [((slots + 8,), jnp.int32)], [], 2, (flat_spans, where, pop),
        out_specs=[inside] * 3 + [pl.BlockSpec(memory_space=pltpu.SMEM)],
    )

    table_shape = (slots, 16, BLOCK)
    coupling = [
        pltpu.VMEM(force_shape, f32),
        pltpu.VMEM((3 * FIELDS * DEPTH, 256), jnp.bfloat16),
        pltpu.VMEM((3 * FIELDS * DEPTH, 256), f32),
        pltpu.VMEM((3 * FIELDS * DEPTH, 256), f32),
        pltpu.VMEM((slots, 8, BLOCK), f32),
    ]
    force, to_right, to_left, table = call(
        functools.partial(first_kernel, span_y, slots, filaments, columns),
        [force_shape, (EDGE_ROWS + 24, 128), (EDGE_ROWS + 24, 128), table_shape],
        coupling + [pltpu.VMEM((filaments * blocks * 8 + 8, BLOCK), f32), pltpu.VMEM((slots * 8, BLOCK), f32)],
        4,
        (flat_spans, where, chosen, stiffness, flow, right_edge, left_edge, *parts),
    )

    moving = (len(MOVING), ROWS, 128)
    moved = pltpu.VMEM(moving, f32)

    def collision(first, dev, edges, force, to_right, to_left):
        left, right = ring(to_right, "gy", 1), ring(to_left, "gy", -1)
        post, east, west = call(
            functools.partial(collide_kernel, first), [field, (PLANE, 128), (PLANE, 128)], [], 0, (*dev, force)
        )
        post_edge, east, west = call(
            functools.partial(collide_edge_kernel, first), [edge, (PLANE_ROWS, 128), (PLANE_ROWS, 128)], [], 0,
            (edges, to_right, left, right, east, west),
        )
        return post, post_edge, ring(east, "gx", 1), ring(west, "gx", -1), left, right

    post, post_edge, east, west, _, _ = collision(True, (pop,), own_edge, force, to_right, to_left)
    streamed, streamed_edge = call(stream_kernel, [field, edge], [], 0, (post, post_edge))
    dev, edges, force, to_right, to_left, *chunks = call(
        functools.partial(second_kernel, slots, blocks, columns),
        [moving, edge, force_shape] + [(24 + share_rows, BLOCK)] * 2 + [(share_rows, BLOCK)] * (columns - 2),
        [moved, pltpu.VMEM(force_shape, f32)] + coupling + [pltpu.VMEM((filaments * blocks + 1, 8, BLOCK), f32)],
        2,
        (where, chosen, post, post_edge, streamed, streamed_edge, east, west, table),
    )
    post, post_edge, east, west, left, right = collision(
        False, (streamed, dev), edges, force, to_right, to_left
    )
    speed = chunks[0] + left[24:] + right[24:]
    for s in range(2, columns - 1):
        speed = speed + ring(chunks[s - 1], "gy", s)

    dev, before = call(
        last_still_kernel, [field, moving],
        [pltpu.VMEM((9, ROWS, 128), f32), pltpu.SemaphoreType.DMA((9,))],
        0, (post, post_edge), out_specs=[anywhere, inside],
    )
    dev, speed = call(
        last_kernel, [field, (share_rows, BLOCK)],
        [moved, pltpu.VMEM(moving, f32), pltpu.SemaphoreType.DMA((11,))],
        0, (post, post_edge, before, east, west, speed, dev),
        in_specs=[inside] * 6 + [anywhere], out_specs=[anywhere] * 2, input_output_aliases={6: 0},
    )
    speed = speed.reshape(3, share_blocks, filaments, BLOCK).transpose(2, 0, 1, 3).reshape(fraction.shape)
    dev = dev.reshape(19, depth, halves, tile_x, 128).transpose(0, 1, 3, 2, 4).reshape(populations.shape)
    return dev, speed


def solution(mesh):
    placed = (P(None, None, "gx", "gy"), P("gx", None, "gy"), P("gx", None, None), P("gx"))
    return jax.shard_map(
        per_device,
        mesh=mesh,
        in_specs=placed,
        out_specs=(P(None, None, "gx", "gy"), P("gx", None, "gy")),
        check_vma=False,
    )
```
